32 devices in a mesh: dev: 32 (over z, y, x, core).
Axes of the slice: x: 2, y: 2, z: 4, core: 2. Of those that a mesh axis runs over, the one named last changes fastest.
Arguments:
- inputs: bfloat16 [8192, 1536], P('dev'), may hold values from -6 to 6
- positions: int32 [8192], P('dev'), may hold values from 0 to 2047, as said below
- norm_first: bfloat16 [1536], P('dev'), may hold values from 0.25 to 1.75
- query_weight: bfloat16 [1536, 1536], P('dev'), may hold values from -0.15625 to 0.15625
- key_weight: bfloat16 [1536, 768], P('dev'), may hold values from -0.15625 to 0.15625
- value_weight: bfloat16 [1536, 768], P('dev'), may hold values from -0.15625 to 0.15625
- out_weight: bfloat16 [1536, 1536], P('dev'), may hold values from -2.5 to 2.5
- norm_second: bfloat16 [1536], P('dev'), may hold values from 0.25 to 1.75
- gate_weight: bfloat16 [1536, 4096], P('dev'), may hold values from -0.15625 to 0.15625
- up_weight: bfloat16 [1536, 4096], P('dev'), may hold values from -0.15625 to 0.15625
- down_weight: bfloat16 [4096, 1536], P('dev'), may hold values from -0.09375 to 0.09375
- cotangent: bfloat16 [8192, 1536], P('dev'), may hold values from -6 to 6
Outputs:
- outputs: bfloat16 [8192, 1536], P('dev')
- input_grad: float32 [8192, 1536], P('dev')
- first_grad: float32 [1536], P('dev')
- query_grad: float32 [1536, 1536], P('dev')
- key_grad: float32 [1536, 768], P('dev')
- value_grad: float32 [1536, 768], P('dev')
- out_grad: float32 [1536, 1536], P('dev')
- second_grad: float32 [1536], P('dev')
- gate_grad: float32 [1536, 4096], P('dev')
- up_grad: float32 [1536, 4096], P('dev')
- down_grad: float32 [4096, 1536], P('dev')
The draws below stay inside these ranges and needn't reach their ends.
Inputs may be any that keep to these rules, and one draw needn't show every extreme that they name: positions count 0, 1, 2, ... along each sequence and start at 0 at the first token; every sequence but the last has 1024 to 2048 tokens, one has exactly 2048.
All inputs are finite; a program needn't handle non-finite values.
Results may differ from the reference program's by a relative error of at most 0.02.
Values may be sent and summed in bfloat16 or wider, within the bound.
No kernel may reach another device: no remote copies, remote signals or barrier semaphores. Data moves between devices by JAX's collectives and lax.ppermute only.
A program may use at most 448 MiB of HBM per device.

```python
import math
import jax
import jax.numpy as jnp
from jax import lax

D = 1536
HEADS = 16
KV_HEADS = 8
HEAD_DIM = 96
FF = 4096
TOKENS = 8192
SEQ_MAX = 2048


def draw_positions(key, part):
    key = jax.random.fold_in(key, 7)
    seq_count = TOKENS // (SEQ_MAX // 2) + 2
    lengths = jax.random.randint(jax.random.fold_in(key, 1), (seq_count,), SEQ_MAX // 2, SEQ_MAX + 1)
    longest = jax.random.randint(jax.random.fold_in(key, 2), (), 1, 3)
    lengths = jnp.where(jnp.arange(seq_count) == longest, SEQ_MAX, lengths)
    starts = jnp.cumsum(lengths) - lengths
    token_index = jnp.arange(TOKENS)
    segment = jnp.sum((starts[None, :] <= token_index[:, None]).astype(jnp.int32), axis=1) - 1
    chosen = jnp.sum(jnp.where(jnp.arange(seq_count)[None, :] == segment[:, None], starts[None, :], 0), axis=1)
    return (token_index - chosen).astype(jnp.int32)


def strengthened(values, rng, source, target, shards_of, factor):
    def block_of(position):
        return (jnp.arange(values.shape[position]) // (values.shape[position] // shards_of)).reshape((-1,) + (1,) * (values.ndim - 1 - position))

    near = jax.random.permutation(rng, shards_of)[block_of(target)]
    second = (block_of(target) + shards_of // 2) % shards_of
    return jnp.where((block_of(source) == near) | (block_of(source) == second), factor * values, values)


def shard_levels(key, shape, split, low, top_value):
    level = 1.0
    for dim, shards_of in split:
        draws = jax.random.uniform(jax.random.fold_in(jax.random.fold_in(key, 6), dim), (shards_of,), jnp.float32, low / len(split), top_value / len(split))
        level = level * jnp.repeat(jnp.exp(draws), shape[dim] // shards_of).reshape((-1,) + (1,) * (len(shape) - 1 - dim))
    return level


def normal_values(rng, shape, scale, most, shards=(), kind=jnp.bfloat16):
    loudness = shard_levels(rng, shape, shards, -0.22, 0.18) if shards else 1.0
    values = jax.random.normal(rng, shape, jnp.float32) * scale * loudness
    return jnp.minimum(jnp.maximum(values, -most), most).astype(kind)


def noise_with(stream_key, dims, scale, most, cuts, heavy, kind=jnp.bfloat16):
    values = scale * jax.random.normal(stream_key, dims, jnp.float32)
    if cuts:
        values = values * shard_levels(stream_key, dims, cuts, -0.22, 0.18)
    return jnp.clip(strengthened(values, jax.random.fold_in(stream_key, 3), *heavy), -most, most).astype(kind)


def setup_inputs(seed: int = 0) -> dict:
    streams_of = jax.random.split(jax.random.key(seed), 13)
    inputs = noise_with(streams_of[0], (TOKENS, D), 1.0, 6.0, ((0, 32),), (0, 1, 32, 2.75))
    positions = draw_positions(jax.random.fold_in(streams_of[12], 71), 0)
    norm_first = jnp.clip(1.0 + 0.15 * jax.random.normal(streams_of[2], (D,), jnp.float32), 0.25, 1.75).astype(jnp.bfloat16)
    query_weight = normal_values(streams_of[3], (D, D), D ** -0.5, 0.15625, ((0, 32),))
    key_weight = normal_values(streams_of[4], (D, KV_HEADS * HEAD_DIM), D ** -0.5, 0.15625, ((0, 32),))
    value_weight = normal_values(streams_of[5], (D, KV_HEADS * HEAD_DIM), D ** -0.5, 0.15625, ((0, 32),))
    out_weight = normal_values(streams_of[6], (D, D), (max(D // 256, 1)) ** -0.5, 2.5, ((0, 32),))
    norm_second = jnp.clip(1.0 + 0.15 * jax.random.normal(streams_of[7], (D,), jnp.float32), 0.25, 1.75).astype(jnp.bfloat16)
    gate_weight = normal_values(streams_of[8], (D, FF), D ** -0.5, 0.15625, ((0, 32),))
    up_weight = normal_values(streams_of[9], (D, FF), D ** -0.5, 0.15625, ((0, 32),))
    down_weight = normal_values(streams_of[10], (FF, D), FF ** -0.5, 0.09375, ((0, 32),))
    cotangent = noise_with(streams_of[11], (TOKENS, D), 1.0, 6.0, ((0, 32),), (0, 1, 32, 2.75))
    return dict(inputs=inputs, positions=positions, norm_first=norm_first, query_weight=query_weight, key_weight=key_weight, value_weight=value_weight, out_weight=out_weight, norm_second=norm_second, gate_weight=gate_weight, up_weight=up_weight, down_weight=down_weight, cotangent=cotangent)


eps_norm = 1e-05
rope_base = 100000.0
masked_score = -1e+30

@jax.custom_vjp
def low(v):
    return lax.optimization_barrier(v.astype(jnp.bfloat16)).astype(jnp.float32)

@jax.custom_vjp
def low_back(v):
    return v

def low_keep(v):
    return (low(v), None)

def low_pass(kept, grad):
    return (grad,)

def back_keep(v):
    return (v, None)

def back_low(kept, grad):
    return (low(grad),)
low.defvjp(low_keep, low_pass)
low_back.defvjp(back_keep, back_low)

def rms_scale(values, gain):
    return values * lax.rsqrt(lax.optimization_barrier(jnp.mean(values * values, axis=-1, keepdims=True)) + eps_norm) * gain

def rope_tables(positions):
    half_dim = HEAD_DIM // 2
    frequency = rope_base ** (-(jnp.arange(half_dim, dtype=jnp.float32) * 2.0 / HEAD_DIM))
    angles = positions.astype(jnp.float32)[:, None] * frequency[None, :]
    angles = jnp.concatenate([angles, angles], axis=1)
    return (jnp.cos(angles), jnp.sin(angles))

def rotate(values, cosine, sine_table):
    half_dim = HEAD_DIM // 2
    turned = jnp.concatenate([-values[..., half_dim:], values[..., :half_dim]], axis=-1)
    return values * cosine[:, None, :] + turned * sine_table[:, None, :]

def product(operand, weights):
    return jnp.dot(operand, weights, precision=lax.Precision.HIGHEST)

def attend(queries, keys, values, positions):
    block_rows = math.gcd(512, TOKENS)
    group_size = HEADS // KV_HEADS
    score_scale = 1.0 / math.sqrt(HEAD_DIM)
    padding = jnp.zeros((SEQ_MAX, KV_HEADS, HEAD_DIM), jnp.float32)
    keys_pad = jnp.concatenate([padding, keys], axis=0)
    values_pad = jnp.concatenate([padding, values], axis=0)
    grouped = queries.reshape(TOKENS // block_rows, block_rows, KV_HEADS, group_size, HEAD_DIM)
    place_blocks = positions.reshape(TOKENS // block_rows, block_rows)

    def one_block(packed):
        block_index, query_rows, place_rows = packed
        block_start = block_index * block_rows
        key_rows = lax.dynamic_slice_in_dim(keys_pad, block_start, block_rows + SEQ_MAX, 0)
        value_rows = lax.dynamic_slice_in_dim(values_pad, block_start, block_rows + SEQ_MAX, 0)
        scores = jnp.einsum('qkgd,tkd->kgqt', query_rows, key_rows, precision=lax.Precision.HIGHEST) * score_scale
        scores = low_back(scores)
        distance = jnp.arange(block_rows, dtype=jnp.int32)[:, None] + SEQ_MAX - jnp.arange(block_rows + SEQ_MAX, dtype=jnp.int32)[None, :]
        visible = (distance >= 0) & (distance <= place_rows[:, None])
        scores = jnp.where(visible, scores, masked_score)
        row_max = lax.optimization_barrier(jnp.max(scores, axis=-1, keepdims=True))
        weights = jnp.exp(scores - row_max)
        probs = weights / lax.optimization_barrier(jnp.sum(weights, axis=-1, keepdims=True))
        return jnp.einsum('kgqt,tkd->qkgd', low(probs), value_rows, precision=lax.Precision.HIGHEST)
    block_ids = jnp.arange(TOKENS // block_rows, dtype=jnp.int32)
    outcome = lax.map(jax.checkpoint(one_block), (block_ids, grouped, place_blocks))
    return outcome.reshape(TOKENS, HEADS * HEAD_DIM)

def forward_layer(inputs, norm_first, query_weight, key_weight, value_weight, out_weight, norm_second, gate_weight, up_weight, down_weight, positions):
    cosine, sine_table = rope_tables(positions)
    normed = low(rms_scale(inputs, norm_first))
    queries = low_back(product(normed, query_weight)).reshape(TOKENS, HEADS, HEAD_DIM)
    keys = low_back(product(normed, key_weight)).reshape(TOKENS, KV_HEADS, HEAD_DIM)
    values = low(low_back(product(normed, value_weight))).reshape(TOKENS, KV_HEADS, HEAD_DIM)
    queries = low(rotate(queries, cosine, sine_table))
    keys = low(rotate(keys, cosine, sine_table))
    attended = low(low_back(attend(queries, keys, values, positions)))
    middle = inputs + low_back(product(attended, out_weight))
    normed_mid = low(rms_scale(middle, norm_second))
    gate = low_back(product(normed_mid, gate_weight))
    up_part = low_back(product(normed_mid, up_weight))
    hidden = low(jax.nn.silu(gate) * up_part)
    return middle + low_back(product(hidden, down_weight))

def reference(inputs, positions, norm_first, query_weight, key_weight, value_weight, out_weight, norm_second, gate_weight, up_weight, down_weight, cotangent):
    floats = tuple((array.astype(jnp.float32) for array in (inputs, norm_first, query_weight, key_weight, value_weight, out_weight, norm_second, gate_weight, up_weight, down_weight)))

    def closed(*arrays):
        return forward_layer(*arrays, positions)
    result, pullback = jax.vjp(closed, *floats)
    gradient = pullback(cotangent.astype(jnp.float32))
    return (result.astype(jnp.bfloat16), gradient[0], gradient[1], gradient[2], gradient[3], gradient[4], gradient[5], gradient[6], gradient[7], gradient[8], gradient[9])
```

```python
import math

import jax
import jax.numpy as jnp
from jax import lax
from jax.experimental import pallas as pl
from jax.experimental.pallas import tpu as pltpu
from jax.sharding import PartitionSpec as P

HEADS = 16
KV_HEADS = 8
HEAD_DIM = 96
TEAM = 8

eps_norm = 1e-05
rope_base = 100000.0
masked_score = -1e30

OWN_HEADS = HEADS // TEAM
OWN_KV = KV_HEADS // TEAM
GROUP = HEADS // KV_HEADS
BLOCK = 256
LANES = 128
score_scale = 1.0 / math.sqrt(HEAD_DIM)
log2_scale = score_scale / math.log(2.0)
kernel_vmem = 56 * 1024 * 1024
small_cost = pl.CostEstimate(flops=1000, bytes_accessed=1000, transcendentals=0)

Q_WIDTH = OWN_HEADS * HEAD_DIM
KV_WIDTH = OWN_KV * HEAD_DIM
LINED = Q_WIDTH + 2 * KV_WIDTH


def relative(position):
    return 2 * (position % 4) + position // 4


def visible_mask(block, starts, ends):
    key = block * BLOCK + lax.broadcasted_iota(jnp.int32, (BLOCK, 1), 0)
    return (key >= starts) & (key <= ends)


def chunk_lanes(ref, chunk):
    spot = pl.ds(chunk * BLOCK, BLOCK)
    return jnp.concatenate([ref[head, :, spot] for head in range(GROUP)], axis=1)


def chunk_range(chunk, starts_ref, last):
    starts = starts_ref[:, pl.ds(chunk * BLOCK, BLOCK)]
    ends = last * BLOCK + lax.broadcasted_iota(jnp.int32, (1, BLOCK), 1)
    return (
        jnp.concatenate([starts] * GROUP, axis=1),
        jnp.concatenate([ends] * GROUP, axis=1),
    )


def attend_kernel(low_ref, starts_ref, query_ref, *refs):
    count = len(refs) - 4
    member = low_ref[TEAM]
    pieces = refs[:count]
    out_ref, norm_ref, keys, values = refs[count:]
    per_piece = pieces[0].shape[-1] // BLOCK
    for back, piece in enumerate(pieces):
        for part in range(per_piece):
            block = (count - 1 - back) * per_piece + (relative(part) ^ member)
            spot = pl.ds(part * BLOCK, BLOCK)
            keys[block] = piece[0, 0, :, spot].T
            values[block] = piece[1, 0, :, spot]
    own_block = (count - 1) * per_piece
    for chunk in range(per_piece):
        queries = chunk_lanes(query_ref, chunk)
        last = own_block + (relative(chunk) ^ member)
        starts, ends = chunk_range(chunk, starts_ref, last)

        def advance(step, running):
            top, total, summed = running
            block = last - step
            scores = (
                jnp.dot(keys[block], queries, preferred_element_type=jnp.float32) * log2_scale
            )
            scores = jnp.where(visible_mask(block, starts, ends), scores, masked_score)
            new_top = jnp.maximum(top, jnp.max(scores, axis=0, keepdims=True))
            factor = jnp.exp2(top - new_top)
            weights = jnp.exp2(scores - new_top)
            total = total * factor + jnp.sum(weights, axis=0, keepdims=True)
            summed = summed * factor + jnp.dot(
                values[block], weights.astype(jnp.bfloat16), preferred_element_type=jnp.float32
            )
            return new_top, total, summed

        lanes = GROUP * BLOCK
        top, total, summed = lax.fori_loop(
            0,
            last - low_ref[chunk] + 1,
            advance,
            (
                jnp.full((1, lanes), masked_score, jnp.float32),
                jnp.zeros((1, lanes), jnp.float32),
                jnp.zeros((HEAD_DIM, lanes), jnp.float32),
            ),
        )
        attended = summed / total
        norm = top + jnp.log2(total)
        spot = pl.ds(chunk * BLOCK, BLOCK)
        for head in range(GROUP):
            out_ref[head, :, spot] = attended[:, head * BLOCK : (head + 1) * BLOCK]
            norm_ref[head, :, spot] = norm[:, head * BLOCK : (head + 1) * BLOCK]


def gradient_kernel(low_ref, starts_ref, query_ref, grad_ref, out_ref, norm_ref, *refs):
    count = len(refs) - 8
    member = low_ref[TEAM]
    pieces = refs[:count]
    query_grad, own_grad, back_grad, keys, keys_t, values, key_sum, value_sum = refs[count:]
    per_piece = pieces[0].shape[-1] // BLOCK
    for back, piece in enumerate(pieces):
        for part in range(per_piece):
            block = (count - 1 - back) * per_piece + (relative(part) ^ member)
            spot = pl.ds(part * BLOCK, BLOCK)
            keys_t[block] = piece[0, 0, :, spot]
            keys[block] = piece[0, 0, :, spot].T
            values[block] = piece[1, 0, :, spot].T
    key_sum[...] = jnp.zeros_like(key_sum)
    value_sum[...] = jnp.zeros_like(value_sum)
    own_block = (count - 1) * per_piece
    rows_rows = (((1,), (1,)), ((), ()))
    for chunk in range(per_piece):
        queries = chunk_lanes(query_ref, chunk)
        grads = chunk_lanes(grad_ref, chunk)
        norm = chunk_lanes(norm_ref, chunk)
        delta = jnp.sum(
            grads.astype(jnp.float32) * chunk_lanes(out_ref, chunk), axis=0, keepdims=True
        )
        last = own_block + (relative(chunk) ^ member)
        starts, ends = chunk_range(chunk, starts_ref, last)

        def advance(block, summed):
            scores = (
                jnp.dot(keys[block], queries, preferred_element_type=jnp.float32) * log2_scale
            )
            scores = jnp.where(visible_mask(block, starts, ends), scores - norm, masked_score)
            probs = jnp.exp2(scores)
            slopes = jnp.dot(values[block], grads, preferred_element_type=jnp.float32)
            grad_scores = (probs * (slopes - delta)).astype(jnp.bfloat16)
            key_sum[block] += lax.dot_general(
                queries, grad_scores, rows_rows, preferred_element_type=jnp.float32
            )
            value_sum[block] += lax.dot_general(
                grads, probs.astype(jnp.bfloat16), rows_rows, preferred_element_type=jnp.float32
            )
            return summed + jnp.dot(
                keys_t[block], grad_scores, preferred_element_type=jnp.float32
            )

        summed = lax.fori_loop(
            low_ref[chunk],
            last + 1,
            advance,
            jnp.zeros((HEAD_DIM, GROUP * BLOCK), jnp.float32),
        )
        spot = pl.ds(chunk * BLOCK, BLOCK)
        for head in range(GROUP):
            query_grad[head, :, spot] = (
                summed[:, head * BLOCK : (head + 1) * BLOCK] * score_scale
            )
    for back in range(count):
        for part in range(per_piece):
            block = (count - 1 - back) * per_piece + (relative(part) ^ member)
            spot = pl.ds(part * BLOCK, BLOCK)
            key_part = key_sum[block] * score_scale
            value_part = value_sum[block]
            if back == 0:
                own_grad[0, 0, :, spot] = key_part
                own_grad[1, 0, :, spot] = value_part
            else:
                back_grad[back - 1, 0, 0, :, spot] = key_part.astype(jnp.bfloat16)
                back_grad[back - 1, 1, 0, :, spot] = value_part.astype(jnp.bfloat16)


def attention_specs(tokens, pieces, first_head):
    whole = pl.BlockSpec((1, tokens), lambda head: (0, 0))
    low = pl.BlockSpec(memory_space=pltpu.SMEM)
    heads = pl.BlockSpec(
        (GROUP, HEAD_DIM, tokens), lambda head: (first_head + head, 0, 0)
    )
    norm = pl.BlockSpec((GROUP, 1, tokens), lambda head: (first_head + head, 0, 0))
    kv = pl.BlockSpec((2, 1, HEAD_DIM, tokens), lambda head: (0, first_head + head, 0, 0))
    return low, whole, heads, norm, [kv] * len(pieces)


def attend(low, starts, queries, pieces, first_head, count):
    tokens = queries.shape[-1]
    blocks = len(pieces) * tokens // BLOCK
    low_spec, whole, heads, norm, kv = attention_specs(tokens, pieces, first_head)
    return pl.pallas_call(
        attend_kernel,
        grid=(count,),
        in_specs=[low_spec, whole, heads] + kv,
        out_specs=[
            pl.BlockSpec((GROUP, HEAD_DIM, tokens), lambda head: (head, 0, 0)),
            pl.BlockSpec((GROUP, 1, tokens), lambda head: (head, 0, 0)),
        ],
        out_shape=[
            jax.ShapeDtypeStruct((count * GROUP, HEAD_DIM, tokens), jnp.float32),
            jax.ShapeDtypeStruct((count * GROUP, 1, tokens), jnp.float32),
        ],
        scratch_shapes=[
            pltpu.VMEM((blocks, BLOCK, HEAD_DIM), jnp.bfloat16),
            pltpu.VMEM((blocks, HEAD_DIM, BLOCK), jnp.bfloat16),
        ],
        compiler_params=pltpu.CompilerParams(vmem_limit_bytes=kernel_vmem),
        cost_estimate=small_cost,
    )(low, starts, queries, *pieces)


def attend_back(low, starts, queries, grads, attended, norm, pieces, first_head, count):
    tokens = queries.shape[-1]
    blocks = len(pieces) * tokens // BLOCK
    low_spec, whole, heads, norm_spec, kv = attention_specs(tokens, pieces, first_head)
    back = len(pieces) - 1
    return pl.pallas_call(
        gradient_kernel,
        grid=(count,),
        in_specs=[low_spec, whole, heads, heads, heads, norm_spec] + kv,
        out_specs=[
            pl.BlockSpec((GROUP, HEAD_DIM, tokens), lambda head: (head, 0, 0)),
            pl.BlockSpec((2, 1, HEAD_DIM, tokens), lambda head: (0, head, 0, 0)),
            pl.BlockSpec((back, 2, 1, HEAD_DIM, tokens), lambda head: (0, 0, head, 0, 0)),
        ],
        out_shape=[
            jax.ShapeDtypeStruct((count * GROUP, HEAD_DIM, tokens), jnp.float32),
            jax.ShapeDtypeStruct((2, count, HEAD_DIM, tokens), jnp.float32),
            jax.ShapeDtypeStruct((back, 2, count, HEAD_DIM, tokens), jnp.bfloat16),
        ],
        scratch_shapes=[
            pltpu.VMEM((blocks, BLOCK, HEAD_DIM), jnp.bfloat16),
            pltpu.VMEM((blocks, HEAD_DIM, BLOCK), jnp.bfloat16),
            pltpu.VMEM((blocks, BLOCK, HEAD_DIM), jnp.bfloat16),
            pltpu.VMEM((blocks, HEAD_DIM, BLOCK), jnp.float32),
            pltpu.VMEM((blocks, HEAD_DIM, BLOCK), jnp.float32),
        ],
        compiler_params=pltpu.CompilerParams(vmem_limit_bytes=kernel_vmem),
        cost_estimate=small_cost,
    )(low, starts, queries, grads, attended, norm, *pieces)

class Order:
    def __init__(self, token):
        self.token = token

    def step(self, *values):
        self.token, tied = lax.optimization_barrier((self.token, values))
        return tied[0] if len(tied) == 1 else tied


class Grid:
    def __init__(self):
        self.count = lax.axis_size("dev")
        self.teams = self.count // TEAM
        index = lax.axis_index("dev")
        self.member = index % TEAM
        self.team = index // TEAM

    def places(self):
        return jnp.stack([self.team, self.member]).astype(jnp.int32)

    def turn(self, value, bits):
        return lax.ppermute(value, "dev", [(d, d ^ bits) for d in range(self.count)])

    def shift(self, value, steps, around=True):
        pairs = []
        for device in range(self.count):
            target = device + steps * TEAM
            if around or 0 <= target < self.count:
                pairs.append((device, target % self.count))
        return lax.ppermute(value, "dev", pairs)

    def spread(self, value):
        return [value] + [self.shift(value, steps) for steps in range(1, self.teams)]

    def both_ways(self, ahead, behind):
        return self.shift(ahead, 1, False), self.shift(behind, -1, False)

    def gather_team(self, blocks):
        return list(blocks) + [self.turn(block, 1) for block in blocks]

    def chips(self, block):
        return [block] + [self.turn(block, 2 * chip) for chip in range(1, 4)]

    def to_members(self, value):
        pairs = [
            (owner, owner % self.teams * TEAM + owner // self.teams)
            for owner in range(self.count)
        ]
        return lax.ppermute(value, "dev", pairs)

    def to_owners(self, value):
        pairs = [
            (owner % self.teams * TEAM + owner // self.teams, owner)
            for owner in range(self.count)
        ]
        return lax.ppermute(value, "dev", pairs)

    def send_chips(self, blocks):
        return [self.turn(block, 2 * chip) for chip, block in enumerate(blocks, 1)]


def call(kernel, grid, in_specs, out_specs, out_shape, scratch=(), prefetch=0):
    return pl.pallas_call(
        kernel,
        out_shape=out_shape,
        grid_spec=pltpu.PrefetchScalarGridSpec(
            num_scalar_prefetch=prefetch,
            grid=grid,
            in_specs=in_specs,
            out_specs=out_specs,
            scratch_shapes=list(scratch),
        ),
        compiler_params=pltpu.CompilerParams(vmem_limit_bytes=kernel_vmem),
        cost_estimate=small_cost,
    )


def fixed(array):
    return pl.BlockSpec(array.shape, lambda *unused: (0,) * array.ndim)


def lanes_at(rows, step_width):
    return pl.BlockSpec((rows, step_width), lambda p, *unused: (0, p))


def rows_at(step_rows, width):
    return pl.BlockSpec((step_rows, width), lambda p, *unused: (p, 0))


def kept_given(rows, width, axis):
    def index(at):
        return (0, at) if axis else (at, 0)

    specs = [
        pl.BlockSpec((rows, width), lambda p, *unused: index(jnp.minimum(p, 3))),
        pl.BlockSpec((rows, width), lambda p, *unused: index(jnp.maximum(p - 4, 0))),
    ]
    shape = (rows, 4 * width) if axis else (4 * rows, width)
    shapes = [
        jax.ShapeDtypeStruct(shape, jnp.float32),
        jax.ShapeDtypeStruct(shape, jnp.bfloat16),
    ]
    return specs, shapes


def keep_or_give(position, keep_ref, give_ref, value):
    @pl.when(position < 4)
    def keep():
        keep_ref[...] = value

    @pl.when(position >= 4)
    def give():
        give_ref[...] = value.astype(give_ref.dtype)


def pick(position, refs, target):
    for number in range(TEAM):

        @pl.when(position == number)
        def move():
            if len(refs) == TEAM:
                target[...] = refs[number][...]
            else:
                target[...] = refs[number // 4][number % 4]


def dot_rows(left, right):
    return lax.dot_general(
        left, right, (((1,), (1,)), ((), ())), preferred_element_type=jnp.float32
    )


def dot(left, right):
    return jnp.dot(left, right, preferred_element_type=jnp.float32)


def place_rows(grid, blocks, start, stop):
    count = len(blocks)
    positions, rows = blocks[0].shape[:2]
    width = stop - start

    def kernel(places_ref, *refs):
        target = refs[-1]
        for number, ref in enumerate(refs[:-1]):

            @pl.when(pl.program_id(0) == number)
            def move():
                for position in range(positions):
                    at = relative(position) ^ places_ref[1] if positions > 1 else 0
                    target[0, pl.ds(at, 1)] = ref[position : position + 1, :, start:stop]

    def target_map(step, places_ref):
        return ((places_ref[0] + count - step) % count, 0, 0, 0)

    return call(
        kernel,
        (count,),
        [fixed(block) for block in blocks],
        pl.BlockSpec((1, positions, rows, width), target_map),
        jax.ShapeDtypeStruct((count, positions, rows, width), blocks[0].dtype),
        prefetch=1,
    )(grid.places(), *blocks)


def place_mixer(grid, own, hops, units, unit_rows):
    count = grid.teams
    positions, rows, wide = own.shape
    third = wide - 2 * units
    sources = [own] + [block for hop in hops for block in hop]

    def kernel(places_ref, *refs):
        mixer_ref, down_ref = refs[-2:]
        team = places_ref[0]

        def move(ref):
            for position in range(positions):
                at = relative(position) ^ places_ref[1]
                mixer_ref[0, pl.ds(at, 1)] = ref[position : position + 1, :, : 2 * units]
                row = position * rows
                while row < (position + 1) * rows:
                    part = row // unit_rows
                    stop = min((part + 1) * unit_rows, (position + 1) * rows)
                    down_ref[
                        0,
                        row - part * unit_rows : stop - part * unit_rows,
                        part * third : (part + 1) * third,
                    ] = ref[position, row - position * rows : stop - position * rows, 2 * units :]
                    row = stop

        for steps in range(count):
            here = pl.program_id(0) == steps
            if steps == 0:
                pl.when(here)(lambda: move(refs[0]))
            else:
                ahead, behind = refs[2 * steps - 1], refs[2 * (count - steps)]
                pl.when(here & (team >= steps))(lambda ahead=ahead: move(ahead))
                pl.when(here & (team < steps))(lambda behind=behind: move(behind))

    def target_map(step, places_ref):
        return (places_ref[0] + count - step) % count

    return call(
        kernel,
        (count,),
        [fixed(source) for source in sources],
        [
            pl.BlockSpec(
                (1, positions, rows, 2 * units), lambda s, p: (target_map(s, p), 0, 0, 0)
            ),
            pl.BlockSpec((1, unit_rows, 3 * third), lambda s, p: (target_map(s, p), 0, 0)),
        ],
        [
            jax.ShapeDtypeStruct((count, positions, rows, 2 * units), own.dtype),
            jax.ShapeDtypeStruct((count, unit_rows, 3 * third), own.dtype),
        ],
        prefetch=1,
    )(grid.places(), *sources)


def project(inputs_t, weights, cosine, sine_table):
    width, own = inputs_t[0].shape
    tokens = TEAM * own
    half = HEAD_DIM // 2

    def kernel(weights_ref, cosine_ref, sine_ref, *refs):
        sources = refs[:TEAM]
        normed_ref, query_ref, kv_ref, chosen, turned = refs[TEAM:]
        position = pl.program_id(0)

        @pl.when(position == 0)
        def prepare():
            turned[...] = weights_ref[:, :LINED].T

        pick(position, sources, chosen)
        values = chosen[...].astype(jnp.float32)
        scale = lax.rsqrt(jnp.mean(values * values, axis=0, keepdims=True) + eps_norm)
        gain = weights_ref[:, LINED : LINED + 1].astype(jnp.float32)
        normed = (values * scale * gain).astype(jnp.bfloat16)
        normed_ref[...] = normed
        lined = dot(turned[...], normed)
        cosines, sines = cosine_ref[...], sine_ref[...]

        def rotated(head):
            block = lined[head * HEAD_DIM : (head + 1) * HEAD_DIM]
            shifted = jnp.concatenate([-block[half:], block[:half]], axis=0)
            return (block * cosines + shifted * sines).astype(jnp.bfloat16)

        for head in range(OWN_HEADS):
            query_ref[head] = rotated(head)
        for head in range(OWN_KV):
            kv_ref[0, head] = rotated(OWN_HEADS + head)
            start = Q_WIDTH + KV_WIDTH + head * HEAD_DIM
            kv_ref[1, head] = lined[start : start + HEAD_DIM].astype(jnp.bfloat16)

    return call(
        kernel,
        (TEAM,),
        [fixed(weights), lanes_at(HEAD_DIM, own), lanes_at(HEAD_DIM, own)]
        + [fixed(block) for block in inputs_t],
        [
            lanes_at(width, own),
            pl.BlockSpec((OWN_HEADS, HEAD_DIM, own), lambda p: (0, 0, p)),
            pl.BlockSpec((2, OWN_KV, HEAD_DIM, own), lambda p: (0, 0, 0, p)),
        ],
        [
            jax.ShapeDtypeStruct((width, tokens), jnp.bfloat16),
            jax.ShapeDtypeStruct((OWN_HEADS, HEAD_DIM, tokens), jnp.bfloat16),
            jax.ShapeDtypeStruct((2, OWN_KV, HEAD_DIM, tokens), jnp.bfloat16),
        ],
        [
            pltpu.VMEM((width, own), jnp.bfloat16),
            pltpu.VMEM((LINED, width), jnp.bfloat16),
        ],
    )(weights, cosine, sine_table, *inputs_t)


def project_out(attended, out_rows):
    tokens = attended.shape[-1]
    own = tokens // TEAM
    width = out_rows.shape[1]
    specs, shapes = kept_given(width, own, 1)

    def kernel(attended_ref, rows_ref, keep_ref, give_ref, turned):
        position = pl.program_id(0)

        @pl.when(position == 0)
        def prepare():
            turned[...] = rows_ref[...].T

        block = attended_ref[...].reshape(Q_WIDTH, own).astype(jnp.bfloat16)
        keep_or_give(position, keep_ref, give_ref, dot(turned[...], block))

    return call(
        kernel,
        (TEAM,),
        [pl.BlockSpec((OWN_HEADS, HEAD_DIM, own), lambda p: (0, 0, p)), fixed(out_rows)],
        specs,
        shapes,
        [pltpu.VMEM((width, Q_WIDTH), jnp.bfloat16)],
    )(attended, out_rows)


def mixer_forward(normed, cotangent, weights, down):
    own, width = cotangent[0].shape[1:]
    units = down.shape[0]
    tokens = TEAM * own

    def kernel(weights_ref, down_ref, *refs):
        normed_refs, cotangent_refs = refs[:TEAM], refs[TEAM : TEAM + 2]
        hidden_ref, grad_ref, chosen, turned, wanted = refs[TEAM + 2 :]
        position = pl.program_id(0)
        pick(position, normed_refs, chosen)
        pick(position, cotangent_refs, wanted)
        turned[...] = chosen[...].T
        gate = dot(turned[...], weights_ref[:, :units])
        up = dot(turned[...], weights_ref[:, units:])
        logistic = 1.0 / (1.0 + jnp.exp(-gate))
        silu = gate * logistic
        hidden_ref[...] = (silu * up).astype(jnp.bfloat16)
        grad_hidden = dot_rows(wanted[...], down_ref[...])
        grad_ref[:, :units] = (
            grad_hidden * up * (logistic * (1.0 + gate * (1.0 - logistic)))
        ).astype(jnp.bfloat16)
        grad_ref[:, units:] = (grad_hidden * silu).astype(jnp.bfloat16)

    return call(
        kernel,
        (TEAM,),
        [fixed(weights), fixed(down)]
        + [fixed(block) for block in normed]
        + [fixed(block) for block in cotangent],
        [rows_at(own, units), rows_at(own, 2 * units)],
        [
            jax.ShapeDtypeStruct((tokens, units), jnp.bfloat16),
            jax.ShapeDtypeStruct((tokens, 2 * units), jnp.bfloat16),
        ],
        [
            pltpu.VMEM((width, own), jnp.bfloat16),
            pltpu.VMEM((own, width), jnp.bfloat16),
            pltpu.VMEM((own, width), jnp.bfloat16),
        ],
    )(weights, down, *normed, *cotangent)


def mixer_backward(grads, weights):
    tokens, columns = grads.shape
    own = tokens // TEAM
    specs, shapes = kept_given(weights.shape[0], own, 1)

    def kernel(grads_ref, weights_ref, keep_ref, give_ref):
        keep_or_give(
            pl.program_id(0), keep_ref, give_ref, dot_rows(weights_ref[...], grads_ref[...])
        )

    return call(
        kernel, (TEAM,), [rows_at(own, columns), fixed(weights)], specs, shapes
    )(grads, weights)


def mixer_output(hidden, down):
    tokens, units = hidden.shape
    own = tokens // TEAM
    specs, shapes = kept_given(own, down.shape[1], 0)

    def kernel(hidden_ref, down_ref, keep_ref, give_ref):
        keep_or_give(pl.program_id(0), keep_ref, give_ref, dot(hidden_ref[...], down_ref[...]))

    return call(kernel, (TEAM,), [rows_at(own, units), fixed(down)], specs, shapes)(hidden, down)


def write_teams(places_ref, total, out_ref, teams):
    rows = total.shape[0] // teams
    for team in range(teams):
        steps = (team + teams - places_ref[0]) % teams
        block = total[team * rows : (team + 1) * rows, :].astype(out_ref.dtype)
        out_ref[pl.ds(steps, 1)] = block[None]


def token_product(grid, lefts, right, by_rows, width):
    own = right.shape[0] // TEAM
    rows = lefts[0].shape[0] if by_rows else lefts.shape[1]
    teams = grid.teams

    def kernel(places_ref, right_ref, *refs):
        sources, (out_ref, total) = refs[:-2], refs[-2:]
        position = pl.program_id(0)

        def add(value):
            @pl.when(position == 0)
            def first():
                total[...] = value

            @pl.when(position > 0)
            def later():
                total[...] += value

        for number, source in enumerate(sources):

            @pl.when(position == number)
            def block():
                add(dot(source[...], right_ref[...]))

        @pl.when(position == TEAM - 1)
        def last():
            write_teams(places_ref, total, out_ref, teams)

    return call(
        kernel,
        (TEAM,),
        [rows_at(own, width)] + [fixed(left) for left in lefts],
        pl.BlockSpec((teams, rows // teams, width), lambda p, *unused: (0, 0, 0)),
        jax.ShapeDtypeStruct((teams, rows // teams, width), jnp.bfloat16),
        [pltpu.VMEM((rows, width), jnp.float32)],
        prefetch=1,
    )(grid.places(), right, *lefts)


def down_product(grid, hidden, cotangent):
    tokens, units = hidden.shape
    own, width = cotangent[0].shape[1:]
    teams = grid.teams

    def kernel(places_ref, hidden_ref, *refs):
        sources, (out_ref, total, wanted) = refs[:2], refs[2:]
        position = pl.program_id(0)
        pick(position, sources, wanted)
        value = dot(hidden_ref[...].T, wanted[...])

        @pl.when(position == 0)
        def first():
            total[...] = value

        @pl.when(position > 0)
        def later():
            total[...] += value

        @pl.when(position == TEAM - 1)
        def last():
            write_teams(places_ref, total, out_ref, teams)

    return call(
        kernel,
        (TEAM,),
        [rows_at(own, units)] + [fixed(block) for block in cotangent],
        pl.BlockSpec((teams, units // teams, width), lambda p, *unused: (0, 0, 0)),
        jax.ShapeDtypeStruct((teams, units // teams, width), jnp.bfloat16),
        [pltpu.VMEM((units, width), jnp.float32), pltpu.VMEM((own, width), jnp.bfloat16)],
        prefetch=1,
    )(grid.places(), hidden, *cotangent)


def project_out_back(grid, grads, out_rows, attended):
    teams = grid.teams
    tokens = attended.shape[-1]
    own = tokens // TEAM
    width = out_rows.shape[1]

    def kernel(places_ref, rows_ref, attended_ref, *refs):
        sources, (grad_ref, out_ref, chosen, total) = refs[:TEAM], refs[TEAM:]
        position = pl.program_id(0)
        pick(position, sources, chosen)
        grad_ref[...] = (
            dot(rows_ref[...], chosen[...])
            .astype(jnp.bfloat16)
            .reshape(OWN_HEADS, HEAD_DIM, own)
        )
        block = attended_ref[...].reshape(Q_WIDTH, own).astype(jnp.bfloat16)
        value = dot_rows(block, chosen[...])

        @pl.when(position == 0)
        def first():
            total[...] = value

        @pl.when(position > 0)
        def later():
            total[...] += value

        @pl.when(position == TEAM - 1)
        def last():
            write_teams(places_ref, total, out_ref, teams)

    heads = pl.BlockSpec((OWN_HEADS, HEAD_DIM, own), lambda p, *unused: (0, 0, p))
    shape = (teams, Q_WIDTH // teams, width)
    return call(
        kernel,
        (TEAM,),
        [fixed(out_rows), heads] + [fixed(block) for block in grads],
        [heads, pl.BlockSpec(shape, lambda p, *unused: (0, 0, 0))],
        [
            jax.ShapeDtypeStruct((OWN_HEADS, HEAD_DIM, tokens), jnp.bfloat16),
            jax.ShapeDtypeStruct(shape, jnp.bfloat16),
        ],
        [pltpu.VMEM((width, own), jnp.bfloat16), pltpu.VMEM((Q_WIDTH, width), jnp.float32)],
        prefetch=1,
    )(grid.places(), out_rows, attended, *grads)


def project_back(grid, normed, query_rot, own_grads, returned, cosine, sine_table, weights):
    width, tokens = normed.shape
    own = tokens // TEAM
    half = HEAD_DIM // 2
    teams = grid.teams
    specs, shapes = kept_given(width, own, 1)

    def kernel(places_ref, normed_ref, query_ref, cosine_ref, sine_ref, weights_ref, *refs):
        kv_refs = refs[: 1 + len(returned)]
        keep_ref, give_ref, out_ref, total, grad_ref = refs[1 + len(returned) :]
        position = pl.program_id(0)
        cosines, sines = cosine_ref[...], sine_ref[...]

        def unrotated(block):
            scaled = block * sines
            shifted = jnp.concatenate([scaled[half:], -scaled[:half]], axis=0)
            return (block * cosines + shifted).astype(jnp.bfloat16)

        for head in range(OWN_HEADS):
            grad_ref[head * HEAD_DIM : (head + 1) * HEAD_DIM] = unrotated(query_ref[head])
        kv = kv_refs[0][...]
        for ref in kv_refs[1:]:
            kv = kv + ref[...].astype(jnp.float32)
        for head in range(OWN_KV):
            start = Q_WIDTH + head * HEAD_DIM
            grad_ref[start : start + HEAD_DIM] = unrotated(kv[0, head])
            start = start + KV_WIDTH
            grad_ref[start : start + HEAD_DIM] = kv[1, head].astype(jnp.bfloat16)
        grad = grad_ref[...]
        keep_or_give(position, keep_ref, give_ref, dot(weights_ref[:, :LINED], grad))
        value = dot_rows(normed_ref[...], grad)

        @pl.when(position == 0)
        def first():
            total[...] = value

        @pl.when(position > 0)
        def later():
            total[...] += value

        @pl.when(position == TEAM - 1)
        def last():
            write_teams(places_ref, total, out_ref, teams)

    heads = pl.BlockSpec((OWN_HEADS, HEAD_DIM, own), lambda p, *unused: (0, 0, p))
    kv_heads = pl.BlockSpec((2, OWN_KV, HEAD_DIM, own), lambda p, *unused: (0, 0, 0, p))
    return call(
        kernel,
        (TEAM,),
        [
            lanes_at(width, own),
            heads,
            lanes_at(HEAD_DIM, own),
            lanes_at(HEAD_DIM, own),
            fixed(weights),
        ]
        + [kv_heads] * (1 + len(returned)),
        specs + [pl.BlockSpec((teams, width // teams, LINED), lambda p, *unused: (0, 0, 0))],
        shapes + [jax.ShapeDtypeStruct((teams, width // teams, LINED), jnp.bfloat16)],
        [pltpu.VMEM((width, LINED), jnp.float32), pltpu.VMEM((LINED, own), jnp.bfloat16)],
        prefetch=1,
    )(grid.places(), normed, query_rot, cosine, sine_table, weights, own_grads, *returned)


def combine(keep, arrived, axis):
    size = keep.shape[axis] // 4
    shape = (keep.shape[0], size) if axis else (size, keep.shape[1])

    def kernel(keep_ref, arrived_ref, own_ref, *block_refs):
        position = pl.program_id(0)
        total = keep_ref[...] + arrived_ref[...].astype(jnp.float32)

        @pl.when(position == 0)
        def own():
            own_ref[...] = total

        for number, ref in enumerate(block_refs, 1):

            @pl.when(position == number)
            def other():
                ref[...] = total.astype(jnp.bfloat16)

    part = pl.BlockSpec(shape, (lambda p: (0, p)) if axis else (lambda p: (p, 0)))
    whole = pl.BlockSpec(shape, lambda p: (0, 0))
    own, *blocks = call(
        kernel,
        (4,),
        [part, part],
        [whole] * 4,
        [jax.ShapeDtypeStruct(shape, jnp.float32)]
        + [jax.ShapeDtypeStruct(shape, jnp.bfloat16)] * 3,
    )(keep, arrived)
    return own, blocks


def summed(refs):
    total = refs[0][...]
    for ref in refs[1:]:
        total = total + ref[...].astype(jnp.float32)
    return total


def finish(kernel, arrays, shapes):
    return call(
        kernel,
        (1,),
        [fixed(array) for array in arrays],
        [pl.BlockSpec(shape.shape, lambda p: (0, 0)) for shape in shapes],
        shapes,
    )(*arrays)


def finish_middle(terms, inputs_t, gain):
    def kernel(*refs):
        inputs_ref, gain_ref, middle_ref, normed_ref = refs[len(terms) :]
        middle = inputs_ref[...].astype(jnp.float32) + summed(refs[: len(terms)])
        middle_ref[...] = middle
        scale = lax.rsqrt(jnp.mean(middle * middle, axis=0, keepdims=True) + eps_norm)
        normed_ref[...] = (middle * scale * gain_ref[...]).astype(jnp.bfloat16)

    shape = inputs_t.shape
    return finish(
        kernel,
        list(terms) + [inputs_t, gain],
        [jax.ShapeDtypeStruct(shape, jnp.float32), jax.ShapeDtypeStruct(shape, jnp.bfloat16)],
    )


def norm_back(values, gain, grad):
    inverse = lax.rsqrt(jnp.mean(values * values, axis=0, keepdims=True) + eps_norm)
    normal = values * inverse
    scaled = grad * gain
    inner = jnp.mean(scaled * normal, axis=0, keepdims=True)
    return inverse * (scaled - normal * inner), jnp.sum(grad * normal, axis=1, keepdims=True)


def finish_second(terms, middle, cotangent, gain):
    def kernel(*refs):
        middle_ref, cotangent_ref, gain_ref, grad_ref, attn_ref, gain_out = refs[len(terms) :]
        norm_grad, gain_part = norm_back(
            middle_ref[...], gain_ref[...], summed(refs[: len(terms)])
        )
        grad = cotangent_ref[...].T.astype(jnp.float32) + norm_grad
        grad_ref[...] = grad
        attn_ref[...] = grad.astype(jnp.bfloat16)
        gain_out[...] = gain_part

    shape = middle.shape
    return finish(
        kernel,
        list(terms) + [middle, cotangent, gain],
        [
            jax.ShapeDtypeStruct(shape, jnp.float32),
            jax.ShapeDtypeStruct(shape, jnp.bfloat16),
            jax.ShapeDtypeStruct((shape[0], 1), jnp.float32),
        ],
    )


def finish_first(terms, inputs_t, grad_middle, gain):
    def kernel(*refs):
        inputs_ref, grad_ref, gain_ref, out_ref, gain_out = refs[len(terms) :]
        norm_grad, gain_part = norm_back(
            inputs_ref[...].astype(jnp.float32), gain_ref[...], summed(refs[: len(terms)])
        )
        out_ref[...] = (grad_ref[...] + norm_grad).T
        gain_out[...] = gain_part

    width, own = inputs_t.shape
    return finish(
        kernel,
        list(terms) + [inputs_t, grad_middle, gain],
        [
            jax.ShapeDtypeStruct((own, width), jnp.float32),
            jax.ShapeDtypeStruct((width, 1), jnp.float32),
        ],
    )


def finish_output(terms, middle):
    def kernel(*refs):
        middle_ref, out_ref = refs[len(terms) :]
        out_ref[...] = (middle_ref[...].T + summed(refs[: len(terms)])).astype(jnp.bfloat16)

    return finish(
        kernel, list(terms) + [middle], [jax.ShapeDtypeStruct(terms[0].shape, jnp.bfloat16)]
    )[0]


def sum_teams(product, parts, kind):
    def kernel(own_ref, *refs):
        total = own_ref[0].astype(jnp.float32)
        for ref in refs[:-1]:
            total = total + ref[...].astype(jnp.float32)
        refs[-1][...] = total.astype(kind)

    shape = product.shape[1:]
    return call(
        kernel,
        (1,),
        [pl.BlockSpec((1,) + shape, lambda p: (0, 0, 0))] + [fixed(part) for part in parts],
        pl.BlockSpec(shape, lambda p: (0, 0)),
        jax.ShapeDtypeStruct(shape, kind),
    )(product, *parts)


def rope_tables(positions):
    half_dim = HEAD_DIM // 2
    frequency = rope_base ** (-(jnp.arange(half_dim, dtype=jnp.float32) * 2.0 / HEAD_DIM))
    angles = frequency[:, None] * positions.astype(jnp.float32)[None, :]
    angles = jnp.concatenate([angles, angles], axis=0)
    return (jnp.cos(angles), jnp.sin(angles))


def per_device(
    inputs,
    positions,
    norm_first,
    query_weight,
    key_weight,
    value_weight,
    out_weight,
    norm_second,
    gate_weight,
    up_weight,
    down_weight,
    cotangent,
):
    grid = Grid()
    member, teams = grid.member, grid.teams
    chip, core = member // 2, member % 2
    own, width = inputs.shape
    tokens = own * TEAM
    rows = query_weight.shape[0]
    unit_rows = down_weight.shape[0]
    units = unit_rows * teams
    longest = own * grid.count // 4
    steps_back = min((longest - 2) // tokens + 1, teams - 1)
    bf16, f32 = jnp.bfloat16, jnp.float32
    order = Order(jnp.zeros((8, 128), jnp.int32))

    def dynamic(array, index, axis=0):
        return lax.dynamic_index_in_dim(array, index, axis, keepdims=False)

    def by_member(weight):
        return jnp.transpose(weight.reshape(rows, TEAM, -1), (1, 0, 2))

    def units_by_member(weight):
        blocks = jnp.transpose(weight.reshape(rows, teams, TEAM, unit_rows), (2, 0, 1, 3))
        return blocks.reshape(TEAM, rows, units)

    gains = jnp.pad(jnp.stack([norm_first, norm_second], axis=1), ((0, 0), (0, LANES - 2)))
    columns = jnp.concatenate(
        [
            by_member(query_weight),
            by_member(key_weight),
            by_member(value_weight),
            jnp.broadcast_to(gains[None], (TEAM, rows, LANES)),
            units_by_member(gate_weight),
            units_by_member(up_weight),
        ],
        axis=-1,
    )
    attn_wide = LINED + LANES
    columns = columns.reshape(TEAM // 2, 2, rows, attn_wide + 2 * units)
    position_chips = jnp.stack(grid.chips(positions))
    all_positions = jnp.concatenate([position_chips, grid.turn(position_chips, 1)]).reshape(tokens)
    inputs_t = inputs.T
    columns, inputs_t = order.step(columns, inputs_t)
    pairs = [
        dynamic(columns, chip)
        if other == 0
        else grid.turn(dynamic(columns, chip ^ other), 2 * other)
        for other in range(4)
    ]
    inputs_two = [grid.turn(inputs_t, 2), grid.turn(inputs_t, 4)]
    cosine, sine_table = rope_tables(all_positions)
    block_index = steps_back * TEAM + (
        jnp.array([relative(p) for p in range(TEAM)], jnp.int32) ^ member
    )
    token_index = (block_index[:, None] * own + jnp.arange(own, dtype=jnp.int32)).reshape(tokens)
    starts = token_index - all_positions
    low = jnp.concatenate([starts[::own] // BLOCK, member[None]]).astype(jnp.int32)
    starts = starts[None]
    third = width // 3
    down_thirds = jnp.concatenate(
        [down_weight[:, part * third : (part + 1) * third] for part in range(3)], axis=0
    ).reshape(TEAM, rows, third)
    cosine, sine_table, starts, low, down_thirds, pairs, inputs_two, inputs_t = order.step(
        cosine, sine_table, starts, low, down_thirds, pairs, inputs_two, inputs_t
    )
    inputs_three = grid.turn(inputs_t, 6)
    pairs = jnp.stack(pairs)
    pairs_keep, pairs_give = dynamic(pairs, core, 1), dynamic(pairs, 1 - core, 1)
    team_rows = jnp.concatenate([pairs_keep, grid.turn(pairs_give, 1)], axis=0)
    attn_rows, team_rows, out_weight = order.step(
        team_rows[..., :attn_wide], team_rows, out_weight
    )
    attn_z = grid.spread(attn_rows)
    inputs_others = [grid.turn(block, 1) for block in [inputs_t] + inputs_two]
    attn_z, inputs_three = order.step(attn_z, inputs_three)
    inputs_others = inputs_others + [grid.turn(inputs_three, 1)]
    inputs_team = [inputs_t] + inputs_two + [inputs_three] + inputs_others
    out_own = grid.to_members(out_weight)
    attn_w = place_rows(grid, attn_z, 0, attn_wide).reshape(width, attn_wide)
    attn_w, inputs_team, out_own = order.step(attn_w, inputs_team, out_own)

    out_z = grid.spread(out_own)
    normed_first, queries, own_piece = project(inputs_team, attn_w, cosine, sine_table)
    own_piece, out_z, cotangent, attn_w = order.step(own_piece, out_z, cotangent, attn_w)
    arrived = [grid.shift(own_piece, step, False) for step in range(1, steps_back + 1)]
    cotangent_chips = grid.chips(cotangent)
    out_rows = place_rows(grid, [block[None] for block in out_z], 0, width)
    out_rows = out_rows.reshape(Q_WIDTH, width)
    gain_first = attn_w[:, LINED : LINED + 1].astype(f32)
    gain_second = attn_w[:, LINED + 1 : LINED + 2].astype(f32)
    mixer_own = jnp.concatenate([team_rows[..., attn_wide:], down_thirds], axis=-1)
    arrived, out_rows, gain_first, gain_second, mixer_own = order.step(
        arrived, out_rows, gain_first, gain_second, mixer_own
    )

    mixer_hops = [grid.both_ways(mixer_own, mixer_own)]

    def next_hop():
        mixer_hops[-1] = order.step(mixer_hops[-1])
        if len(mixer_hops) < teams - 1:
            mixer_hops.append(grid.both_ways(*mixer_hops[-1]))

    pieces = [own_piece] + arrived
    attended, normalizer = attend(low, starts, queries, pieces, 0, OWN_KV)
    keep, give = project_out(attended, out_rows)
    give, cotangent_chips, mixer_hops[0] = order.step(give, cotangent_chips, mixer_hops[0])
    other = grid.turn(give, 1)
    if len(mixer_hops) < teams - 1:
        mixer_hops.append(grid.both_ways(*mixer_hops[-1]))
    other = order.step(other)
    total, blocks = combine(keep, other, 1)
    blocks = order.step(blocks)
    terms = grid.send_chips(blocks)
    cotangent_stack = order.step(jnp.stack(cotangent_chips))
    terms, mixer_hops[-1] = order.step(terms, mixer_hops[-1])
    if len(mixer_hops) < teams - 1:
        mixer_hops.append(grid.both_ways(*mixer_hops[-1]))
    cotangent_other = grid.turn(cotangent_stack, 1)
    middle, normed_second = finish_middle([total] + terms, inputs_t, gain_second)
    normed_second, cotangent_other = order.step(normed_second, cotangent_other)
    cotangent_team = [cotangent_stack, cotangent_other]
    second_chips = grid.chips(normed_second)
    while len(mixer_hops) < teams - 1:
        next_hop()
    second_chips, mixer_hops[-1] = order.step(second_chips, mixer_hops[-1])
    second_team = grid.gather_team(second_chips)
    mixer_w, down_w = place_mixer(grid, mixer_own, mixer_hops, units, unit_rows)
    mixer_w = mixer_w.reshape(width, 2 * units)
    down_w = down_w.reshape(units, width)
    mixer_w, down_w, second_team = order.step(mixer_w, down_w, second_team)

    early = max(1, teams // 2)

    def send_teams(product, first, last):
        return [grid.shift(product[steps], steps) for steps in range(first, last)]

    hidden, grads = mixer_forward(second_team, cotangent_team, mixer_w, down_w)
    keep, give = mixer_backward(grads, mixer_w)
    give, grads = order.step(give, grads)
    other = order.step(grid.turn(give, 1))
    total, blocks = combine(keep, other, 1)
    blocks, hidden, grads = order.step(blocks, hidden, grads)
    terms = grid.send_chips(blocks)
    mixer_part = token_product(grid, second_team, grads, True, 2 * units)
    mixer_part, hidden = order.step(mixer_part, hidden)
    mixer_parts = send_teams(mixer_part, 1, early + 1)
    down_part = down_product(grid, hidden, cotangent_team)
    terms, down_part = order.step(terms, down_part)
    grad_middle, grad_attn, second_part = finish_second(
        [total] + terms, middle, cotangent, gain_second
    )
    grad_attn, hidden = order.step(grad_attn, hidden)
    attn_chips = grid.chips(grad_attn)
    out_keep, out_give = mixer_output(hidden, down_w)
    attn_chips, out_give, mixer_parts = order.step(attn_chips, out_give, mixer_parts)
    late_parts = send_teams(mixer_part, early + 1, teams)
    attn_team = order.step(grid.gather_team(attn_chips))

    grad_attended, out_part = project_out_back(grid, attn_team, out_rows, attended)
    grad_attended, down_part, out_give = order.step(grad_attended, down_part, out_give)
    down_parts = send_teams(down_part, 1, early + 1)
    out_other = grid.turn(out_give, 1)
    query_rot, own_grads, back_grads = attend_back(
        low, starts, queries, grad_attended, attended, normalizer, pieces, 0, OWN_KV
    )
    query_rot, own_grads, back_grads, late_parts, out_other = order.step(
        query_rot, own_grads, back_grads, late_parts, out_other
    )
    returned = [
        grid.shift(back_grads[step - 1], -step, False) for step in range(1, steps_back + 1)
    ]
    out_total, out_blocks = combine(out_keep, out_other, 0)
    out_blocks = order.step(out_blocks)
    out_terms = grid.send_chips(out_blocks)
    mixer_total = sum_teams(mixer_part, mixer_parts + late_parts, bf16)
    returned, down_parts, mixer_total = order.step(returned, down_parts, mixer_total)
    down_late = send_teams(down_part, early + 1, teams)
    keep, give, attn_part = project_back(
        grid, normed_first, query_rot, own_grads, returned, cosine, sine_table, attn_w
    )
    attn_part, give, out_terms, down_late = order.step(attn_part, give, out_terms, down_late)
    other = grid.turn(give, 1)
    attn_parts = send_teams(attn_part, 1, early + 1)
    other = order.step(other)
    total, blocks = combine(keep, other, 1)
    blocks, out_part = order.step(blocks, out_part)
    terms = grid.send_chips(blocks)
    outputs = finish_output([out_total] + out_terms, middle)
    down_grad = sum_teams(down_part, down_parts + down_late, f32)
    attn_parts, outputs, down_grad = order.step(attn_parts, outputs, down_grad)
    attn_late = send_teams(attn_part, early + 1, teams)
    out_parts = send_teams(out_part, 1, teams)

    def members_rows(total):
        blocks = total.reshape(TEAM // 2, 2, rows, -1)
        return dynamic(blocks, core, 1), grid.turn(dynamic(blocks, 1 - core, 1), 1)

    def owner_columns(mine, others):
        both = jnp.stack([mine, others])
        first = jnp.where(core == 0, both[0], both[1])
        second = jnp.where(core == 0, both[1], both[0])
        both = jnp.stack([first, second], axis=1)
        found = [
            dynamic(both, chip) if other == 0 else grid.turn(dynamic(both, chip ^ other), 2 * other)
            for other in range(4)
        ]
        return found

    def in_order(found):
        stacked = jnp.stack(found)
        return jnp.stack([dynamic(stacked, chip ^ other) for other in range(4)]).reshape(
            (TEAM,) + found[0].shape[1:]
        )

    mixer_mine, mixer_others = members_rows(mixer_total)
    mixer_mine, mixer_others, terms = order.step(mixer_mine, mixer_others, terms)
    mixer_found = owner_columns(mixer_mine, mixer_others)
    input_grad, first_part = finish_first([total] + terms, inputs_t, grad_middle, gain_first)
    gain_parts = jnp.concatenate([first_part, second_part], axis=1).T
    attn_late, gain_parts, out_parts = order.step(attn_late, gain_parts, out_parts)
    attn_total = sum_teams(attn_part, attn_parts + attn_late, bf16)
    out_own = sum_teams(out_part, out_parts, bf16)
    attn_mine, attn_others = members_rows(attn_total)
    gain_parts = gain_parts + grid.turn(gain_parts, 1)
    attn_mine, attn_others, gain_parts, out_own = order.step(
        attn_mine, attn_others, gain_parts, out_own
    )
    attn_found = owner_columns(attn_mine, attn_others)
    out_grad = grid.to_owners(out_own).astype(f32)
    gain_parts = gain_parts + grid.turn(gain_parts, 2)
    mixer_found, gain_parts = order.step(mixer_found, gain_parts)
    mixer_columns = in_order(mixer_found)

    def whole_units(blocks):
        blocks = blocks.reshape(TEAM, rows, teams, unit_rows)
        return jnp.transpose(blocks, (1, 2, 0, 3)).reshape(rows, TEAM * units).astype(f32)

    def whole(blocks):
        return jnp.transpose(blocks, (1, 0, 2)).reshape(rows, -1).astype(f32)

    gate_grad = whole_units(mixer_columns[..., :units])
    up_grad = whole_units(mixer_columns[..., units:])
    gain_parts = gain_parts + grid.turn(gain_parts, 4)
    gain_blocks = gain_parts.reshape(2, teams, TEAM, rows)
    gain_sums = dynamic(dynamic(gain_blocks, grid.team, 1), member, 1)
    for steps in range(1, teams):
        block = dynamic(dynamic(gain_blocks, (grid.team + steps) % teams, 1), member, 1)
        gain_sums = gain_sums + grid.shift(block, steps)
    attn_found, gain_sums = order.step(attn_found, gain_sums)
    attn_columns = in_order(attn_found)
    gain_sums = gain_sums + order.token[0, 0].astype(f32)
    return (
        outputs,
        input_grad,
        gain_sums[0],
        whole(attn_columns[..., :Q_WIDTH]),
        whole(attn_columns[..., Q_WIDTH : Q_WIDTH + KV_WIDTH]),
        whole(attn_columns[..., Q_WIDTH + KV_WIDTH :]),
        out_grad,
        gain_sums[1],
        gate_grad,
        up_grad,
        down_grad,
    )


def solution(mesh):
    matrix, vector = P("dev", None), P("dev")
    in_specs = (matrix, vector, vector) + (matrix,) * 4 + (vector,) + (matrix,) * 4
    out_specs = (matrix, matrix, vector) + (matrix,) * 4 + (vector,) + (matrix,) * 3
    return jax.shard_map(
        per_device, mesh=mesh, in_specs=in_specs, out_specs=out_specs, check_vma=False
    )
```

```python
import functools
import math

import jax
import jax.numpy as jnp
from jax import lax
from jax.experimental import pallas as pl
from jax.experimental.pallas import tpu as pltpu
from jax.sharding import PartitionSpec as P

HEADS = 16
KV_HEADS = 8
HEAD_DIM = 96
TEAM = 8

eps_norm = 1e-05
rope_base = 100000.0
masked_score = -1e30

OWN_HEADS = HEADS // TEAM
OWN_KV = KV_HEADS // TEAM
GROUP = HEADS // KV_HEADS
BLOCK = 256
LANES = 128
score_scale = 1.0 / math.sqrt(HEAD_DIM)
log2_scale = score_scale / math.log(2.0)
kernel_vmem = 56 * 1024 * 1024
small_cost = pl.CostEstimate(flops=1000, bytes_accessed=1000, transcendentals=0)

Q_WIDTH = OWN_HEADS * HEAD_DIM
KV_WIDTH = OWN_KV * HEAD_DIM
LINED = Q_WIDTH + 2 * KV_WIDTH


def relative(position):
    return 2 * (position % 4) + position // 4


def visible_mask(block, starts, ends):
    key = block * BLOCK + lax.broadcasted_iota(jnp.int32, (BLOCK, 1), 0)
    return (key >= starts) & (key <= ends)


def chunk_lanes(ref, chunk):
    spot = pl.ds(chunk * BLOCK, BLOCK)
    return jnp.concatenate([ref[head, :, spot] for head in range(GROUP)], axis=1)


def chunk_range(chunk, starts_ref, last):
    starts = starts_ref[:, pl.ds(chunk * BLOCK, BLOCK)]
    ends = last * BLOCK + lax.broadcasted_iota(jnp.int32, (1, BLOCK), 1)
    return (
        jnp.concatenate([starts] * GROUP, axis=1),
        jnp.concatenate([ends] * GROUP, axis=1),
    )


def attend_kernel(chunks, low_ref, starts_ref, query_ref, *refs):
    count = len(refs) - 4
    member = low_ref[TEAM]
    pieces = refs[:count]
    out_ref, norm_ref, keys, values = refs[count:]
    per_piece = pieces[0].shape[-1] // BLOCK
    for back, piece in enumerate(pieces):
        for part in range(per_piece):
            block = (count - 1 - back) * per_piece + (relative(part) ^ member)
            spot = pl.ds(part * BLOCK, BLOCK)
            keys[block] = piece[0, 0, :, spot].T
            values[block] = piece[1, 0, :, spot]
    own_block = (count - 1) * per_piece
    for place, chunk in enumerate(chunks):
        queries = chunk_lanes(query_ref, chunk)
        last = own_block + (relative(chunk) ^ member)
        starts, ends = chunk_range(chunk, starts_ref, last)

        def advance(step, running):
            top, total, summed = running
            block = last - step
            scores = (
                jnp.dot(keys[block], queries, preferred_element_type=jnp.float32) * log2_scale
            )
            scores = jnp.where(visible_mask(block, starts, ends), scores, masked_score)
            new_top = jnp.maximum(top, jnp.max(scores, axis=0, keepdims=True))
            factor = jnp.exp2(top - new_top)
            weights = jnp.exp2(scores - new_top)
            total = total * factor + jnp.sum(weights, axis=0, keepdims=True)
            summed = summed * factor + jnp.dot(
                values[block], weights.astype(jnp.bfloat16), preferred_element_type=jnp.float32
            )
            return new_top, total, summed

        lanes = GROUP * BLOCK
        top, total, summed = lax.fori_loop(
            0,
            last - low_ref[chunk] + 1,
            advance,
            (
                jnp.full((1, lanes), masked_score, jnp.float32),
                jnp.zeros((1, lanes), jnp.float32),
                jnp.zeros((HEAD_DIM, lanes), jnp.float32),
            ),
        )
        attended = summed / total
        norm = top + jnp.log2(total)
        spot = pl.ds(place * BLOCK, BLOCK)
        for head in range(GROUP):
            out_ref[head, :, spot] = attended[:, head * BLOCK : (head + 1) * BLOCK]
            norm_ref[head, :, spot] = norm[:, head * BLOCK : (head + 1) * BLOCK]


def gradient_kernel(low_ref, starts_ref, query_ref, grad_ref, *refs):
    out_refs, norm_refs, refs = refs[:4], refs[4:8], refs[8:]
    count = len(refs) - 8
    member = low_ref[TEAM]
    pieces = refs[:count]
    query_grad, own_grad, back_grad, keys, keys_t, values, key_sum, value_sum = refs[count:]
    per_piece = pieces[0].shape[-1] // BLOCK
    for back, piece in enumerate(pieces):
        for part in range(per_piece):
            block = (count - 1 - back) * per_piece + (relative(part) ^ member)
            spot = pl.ds(part * BLOCK, BLOCK)
            keys_t[block] = piece[0, 0, :, spot]
            keys[block] = piece[0, 0, :, spot].T
            values[block] = piece[1, 0, :, spot].T
    key_sum[...] = jnp.zeros_like(key_sum)
    value_sum[...] = jnp.zeros_like(value_sum)
    own_block = (count - 1) * per_piece
    rows_rows = (((1,), (1,)), ((), ()))
    for chunk in range(per_piece):
        queries = chunk_lanes(query_ref, chunk)
        grads = chunk_lanes(grad_ref, chunk)
        norm = chunk_lanes(norm_refs[chunk % 4], chunk // 4)
        delta = jnp.sum(
            grads.astype(jnp.float32) * chunk_lanes(out_refs[chunk % 4], chunk // 4),
            axis=0,
            keepdims=True,
        )
        last = own_block + (relative(chunk) ^ member)
        starts, ends = chunk_range(chunk, starts_ref, last)

        def advance(block, summed):
            scores = (
                jnp.dot(keys[block], queries, preferred_element_type=jnp.float32) * log2_scale
            )
            scores = jnp.where(visible_mask(block, starts, ends), scores - norm, masked_score)
            probs = jnp.exp2(scores)
            slopes = jnp.dot(values[block], grads, preferred_element_type=jnp.float32)
            grad_scores = (probs * (slopes - delta)).astype(jnp.bfloat16)
            key_sum[block] += lax.dot_general(
                queries, grad_scores, rows_rows, preferred_element_type=jnp.float32
            )
            value_sum[block] += lax.dot_general(
                grads, probs.astype(jnp.bfloat16), rows_rows, preferred_element_type=jnp.float32
            )
            return summed + jnp.dot(
                keys_t[block], grad_scores, preferred_element_type=jnp.float32
            )

        summed = lax.fori_loop(
            low_ref[chunk],
            last + 1,
            advance,
            jnp.zeros((HEAD_DIM, GROUP * BLOCK), jnp.float32),
        )
        spot = pl.ds(chunk * BLOCK, BLOCK)
        for head in range(GROUP):
            query_grad[head, :, spot] = (
                summed[:, head * BLOCK : (head + 1) * BLOCK] * score_scale
            )
    for back in range(count):
        for part in range(per_piece):
            block = (count - 1 - back) * per_piece + (relative(part) ^ member)
            spot = pl.ds(part * BLOCK, BLOCK)
            key_part = key_sum[block] * score_scale
            value_part = value_sum[block]
            if back == 0:
                own_grad[0, 0, :, spot] = key_part
                own_grad[1, 0, :, spot] = value_part
            else:
                back_grad[back - 1, 0, 0, :, spot] = key_part.astype(jnp.bfloat16)
                back_grad[back - 1, 1, 0, :, spot] = value_part.astype(jnp.bfloat16)


def attention_specs(tokens, pieces, first_head):
    whole = pl.BlockSpec((1, tokens), lambda head: (0, 0))
    low = pl.BlockSpec(memory_space=pltpu.SMEM)
    heads = pl.BlockSpec(
        (GROUP, HEAD_DIM, tokens), lambda head: (first_head + head, 0, 0)
    )
    norm = pl.BlockSpec((GROUP, 1, tokens), lambda head: (first_head + head, 0, 0))
    kv = pl.BlockSpec((2, 1, HEAD_DIM, tokens), lambda head: (0, first_head + head, 0, 0))
    return low, whole, heads, norm, [kv] * len(pieces)


def attend(low, starts, queries, pieces, chip):
    tokens = queries.shape[-1]
    blocks = len(pieces) * tokens // BLOCK
    chunks = (chip, chip + 4)
    wide = len(chunks) * BLOCK
    low_spec, whole, heads, norm, kv = attention_specs(tokens, pieces, 0)
    return pl.pallas_call(
        functools.partial(attend_kernel, chunks),
        grid=(OWN_KV,),
        in_specs=[low_spec, whole, heads] + kv,
        out_specs=[
            pl.BlockSpec((GROUP, HEAD_DIM, wide), lambda head: (head, 0, 0)),
            pl.BlockSpec((GROUP, 1, wide), lambda head: (head, 0, 0)),
        ],
        out_shape=[
            jax.ShapeDtypeStruct((OWN_HEADS, HEAD_DIM, wide), jnp.float32),
            jax.ShapeDtypeStruct((OWN_HEADS, 1, wide), jnp.float32),
        ],
        scratch_shapes=[
            pltpu.VMEM((blocks, BLOCK, HEAD_DIM), jnp.bfloat16),
            pltpu.VMEM((blocks, HEAD_DIM, BLOCK), jnp.bfloat16),
        ],
        compiler_params=pltpu.CompilerParams(vmem_limit_bytes=kernel_vmem),
        cost_estimate=small_cost,
    )(low, starts, queries, *pieces)


def attend_back(low, starts, queries, grads, attended, norm, pieces, first_head, count):
    tokens = queries.shape[-1]
    blocks = len(pieces) * tokens // BLOCK
    low_spec, whole, heads, norm_spec, kv = attention_specs(tokens, pieces, first_head)
    back = len(pieces) - 1
    return pl.pallas_call(
        gradient_kernel,
        grid=(count,),
        in_specs=[low_spec, whole, heads, heads]
        + [
            pl.BlockSpec((GROUP,) + block.shape[1:], lambda head: (head, 0, 0))
            for block in list(attended) + list(norm)
        ]
        + kv,
        out_specs=[
            pl.BlockSpec((GROUP, HEAD_DIM, tokens), lambda head: (head, 0, 0)),
            pl.BlockSpec((2, 1, HEAD_DIM, tokens), lambda head: (0, head, 0, 0)),
            pl.BlockSpec((back, 2, 1, HEAD_DIM, tokens), lambda head: (0, 0, head, 0, 0)),
        ],
        out_shape=[
            jax.ShapeDtypeStruct((count * GROUP, HEAD_DIM, tokens), jnp.float32),
            jax.ShapeDtypeStruct((2, count, HEAD_DIM, tokens), jnp.float32),
            jax.ShapeDtypeStruct((back, 2, count, HEAD_DIM, tokens), jnp.bfloat16),
        ],
        scratch_shapes=[
            pltpu.VMEM((blocks, BLOCK, HEAD_DIM), jnp.bfloat16),
            pltpu.VMEM((blocks, HEAD_DIM, BLOCK), jnp.bfloat16),
            pltpu.VMEM((blocks, BLOCK, HEAD_DIM), jnp.bfloat16),
            pltpu.VMEM((blocks, HEAD_DIM, BLOCK), jnp.float32),
            pltpu.VMEM((blocks, HEAD_DIM, BLOCK), jnp.float32),
        ],
        compiler_params=pltpu.CompilerParams(vmem_limit_bytes=kernel_vmem),
        cost_estimate=small_cost,
    )(low, starts, queries, grads, *attended, *norm, *pieces)

class Order:
    def __init__(self, token):
        self.token = token

    def step(self, *values):
        self.token, tied = lax.optimization_barrier((self.token, values))
        return tied[0] if len(tied) == 1 else tied


class Grid:
    def __init__(self):
        self.count = lax.axis_size("dev")
        self.teams = self.count // TEAM
        index = lax.axis_index("dev")
        self.member = index % TEAM
        self.team = index // TEAM

    def places(self):
        return jnp.stack([self.team, self.member]).astype(jnp.int32)

    def turn(self, value, bits):
        return lax.ppermute(value, "dev", [(d, d ^ bits) for d in range(self.count)])

    def shift(self, value, steps, around=True):
        pairs = []
        for device in range(self.count):
            target = device + steps * TEAM
            if around or 0 <= target < self.count:
                pairs.append((device, target % self.count))
        return lax.ppermute(value, "dev", pairs)

    def spread(self, value):
        return [value] + [self.shift(value, steps) for steps in range(1, self.teams)]

    def both_ways(self, ahead, behind):
        return self.shift(ahead, 1, False), self.shift(behind, -1, False)

    def gather_team(self, blocks):
        return list(blocks) + [self.turn(block, 1) for block in blocks]

    def chips(self, block):
        return [block] + [self.turn(block, 2 * chip) for chip in range(1, 4)]

    def to_members(self, value):
        pairs = [
            (owner, owner % self.teams * TEAM + owner // self.teams)
            for owner in range(self.count)
        ]
        return lax.ppermute(value, "dev", pairs)

    def to_owners(self, value):
        pairs = [
            (owner % self.teams * TEAM + owner // self.teams, owner)
            for owner in range(self.count)
        ]
        return lax.ppermute(value, "dev", pairs)

    def send_chips(self, blocks):
        return [self.turn(block, 2 * chip) for chip, block in enumerate(blocks, 1)]


def call(kernel, grid, in_specs, out_specs, out_shape, scratch=(), prefetch=0):
    return pl.pallas_call(
        kernel,
        out_shape=out_shape,
        grid_spec=pltpu.PrefetchScalarGridSpec(
            num_scalar_prefetch=prefetch,
            grid=grid,
            in_specs=in_specs,
            out_specs=out_specs,
            scratch_shapes=list(scratch),
        ),
        compiler_params=pltpu.CompilerParams(vmem_limit_bytes=kernel_vmem),
        cost_estimate=small_cost,
    )


def fixed(array):
    return pl.BlockSpec(array.shape, lambda *unused: (0,) * array.ndim)


def lanes_at(rows, step_width):
    return pl.BlockSpec((rows, step_width), lambda p, *unused: (0, p))


def rows_at(step_rows, width):
    return pl.BlockSpec((step_rows, width), lambda p, *unused: (p, 0))


def kept_given(rows, width, axis):
    def index(at):
        return (0, at) if axis else (at, 0)

    specs = [
        pl.BlockSpec((rows, width), lambda p, *unused: index(jnp.minimum(p, 3))),
        pl.BlockSpec((rows, width), lambda p, *unused: index(jnp.maximum(p - 4, 0))),
    ]
    shape = (rows, 4 * width) if axis else (4 * rows, width)
    shapes = [
        jax.ShapeDtypeStruct(shape, jnp.float32),
        jax.ShapeDtypeStruct(shape, jnp.bfloat16),
    ]
    return specs, shapes


def keep_or_give(position, keep_ref, give_ref, value):
    @pl.when(position < 4)
    def keep():
        keep_ref[...] = value

    @pl.when(position >= 4)
    def give():
        give_ref[...] = value.astype(give_ref.dtype)


def pick(position, refs, target):
    for number in range(TEAM):

        @pl.when(position == number)
        def move():
            if len(refs) == TEAM:
                target[...] = refs[number][...]
            else:
                target[...] = refs[number // 4][number % 4]


def dot_rows(left, right):
    return lax.dot_general(
        left, right, (((1,), (1,)), ((), ())), preferred_element_type=jnp.float32
    )


def dot(left, right):
    return jnp.dot(left, right, preferred_element_type=jnp.float32)


def place_rows(grid, blocks, start, stop):
    count = len(blocks)
    positions, rows = blocks[0].shape[:2]
    width = stop - start

    def kernel(places_ref, *refs):
        target = refs[-1]
        for number, ref in enumerate(refs[:-1]):

            @pl.when(pl.program_id(0) == number)
            def move():
                for position in range(positions):
                    at = relative(position) ^ places_ref[1] if positions > 1 else 0
                    target[0, pl.ds(at, 1)] = ref[position : position + 1, :, start:stop]

    def target_map(step, places_ref):
        return ((places_ref[0] + count - step) % count, 0, 0, 0)

    return call(
        kernel,
        (count,),
        [fixed(block) for block in blocks],
        pl.BlockSpec((1, positions, rows, width), target_map),
        jax.ShapeDtypeStruct((count, positions, rows, width), blocks[0].dtype),
        prefetch=1,
    )(grid.places(), *blocks)


def place_mixer(grid, own, hops, units, unit_rows):
    count = grid.teams
    positions, rows, wide = own.shape
    third = wide - 2 * units
    sources = [own] + [block for hop in hops for block in hop]

    def kernel(places_ref, *refs):
        mixer_ref, down_ref = refs[-2:]
        team = places_ref[0]

        def move(ref):
            for position in range(positions):
                at = relative(position) ^ places_ref[1]
                mixer_ref[0, pl.ds(at, 1)] = ref[position : position + 1, :, : 2 * units]
                row = position * rows
                while row < (position + 1) * rows:
                    part = row // unit_rows
                    stop = min((part + 1) * unit_rows, (position + 1) * rows)
                    down_ref[
                        0,
                        row - part * unit_rows : stop - part * unit_rows,
                        part * third : (part + 1) * third,
                    ] = ref[position, row - position * rows : stop - position * rows, 2 * units :]
                    row = stop

        for steps in range(count):
            here = pl.program_id(0) == steps
            if steps == 0:
                pl.when(here)(lambda: move(refs[0]))
            else:
                ahead, behind = refs[2 * steps - 1], refs[2 * (count - steps)]
                pl.when(here & (team >= steps))(lambda ahead=ahead: move(ahead))
                pl.when(here & (team < steps))(lambda behind=behind: move(behind))

    def target_map(step, places_ref):
        return (places_ref[0] + count - step) % count

    return call(
        kernel,
        (count,),
        [fixed(source) for source in sources],
        [
            pl.BlockSpec(
                (1, positions, rows, 2 * units), lambda s, p: (target_map(s, p), 0, 0, 0)
            ),
            pl.BlockSpec((1, unit_rows, 3 * third), lambda s, p: (target_map(s, p), 0, 0)),
        ],
        [
            jax.ShapeDtypeStruct((count, positions, rows, 2 * units), own.dtype),
            jax.ShapeDtypeStruct((count, unit_rows, 3 * third), own.dtype),
        ],
        prefetch=1,
    )(grid.places(), *sources)


def project(inputs_t, weights, cosine, sine_table):
    width, own = inputs_t[0].shape
    tokens = TEAM * own
    half = HEAD_DIM // 2

    def kernel(weights_ref, cosine_ref, sine_ref, *refs):
        sources = refs[:TEAM]
        normed_ref, query_ref, kv_ref, chosen, turned = refs[TEAM:]
        position = pl.program_id(0)

        @pl.when(position == 0)
        def prepare():
            turned[...] = weights_ref[:, :LINED].T

        pick(position, sources, chosen)
        values = chosen[...].astype(jnp.float32)
        scale = lax.rsqrt(jnp.mean(values * values, axis=0, keepdims=True) + eps_norm)
        gain = weights_ref[:, LINED : LINED + 1].astype(jnp.float32)
        normed = (values * scale * gain).astype(jnp.bfloat16)
        normed_ref[...] = normed
        lined = dot(turned[...], normed)
        cosines, sines = cosine_ref[...], sine_ref[...]

        def rotated(head):
            block = lined[head * HEAD_DIM : (head + 1) * HEAD_DIM]
            shifted = jnp.concatenate([-block[half:], block[:half]], axis=0)
            return (block * cosines + shifted * sines).astype(jnp.bfloat16)

        for head in range(OWN_HEADS):
            query_ref[head] = rotated(head)
        for head in range(OWN_KV):
            kv_ref[0, head] = rotated(OWN_HEADS + head)
            start = Q_WIDTH + KV_WIDTH + head * HEAD_DIM
            kv_ref[1, head] = lined[start : start + HEAD_DIM].astype(jnp.bfloat16)

    return call(
        kernel,
        (TEAM,),
        [fixed(weights), lanes_at(HEAD_DIM, own), lanes_at(HEAD_DIM, own)]
        + [fixed(block) for block in inputs_t],
        [
            lanes_at(width, own),
            pl.BlockSpec((OWN_HEADS, HEAD_DIM, own), lambda p: (0, 0, p)),
            pl.BlockSpec((2, OWN_KV, HEAD_DIM, own), lambda p: (0, 0, 0, p)),
        ],
        [
            jax.ShapeDtypeStruct((width, tokens), jnp.bfloat16),
            jax.ShapeDtypeStruct((OWN_HEADS, HEAD_DIM, tokens), jnp.bfloat16),
            jax.ShapeDtypeStruct((2, OWN_KV, HEAD_DIM, tokens), jnp.bfloat16),
        ],
        [
            pltpu.VMEM((width, own), jnp.bfloat16),
            pltpu.VMEM((LINED, width), jnp.bfloat16),
        ],
    )(weights, cosine, sine_table, *inputs_t)


def project_out(attended, out_rows):
    own = attended.shape[-1] // 2
    width = out_rows.shape[1]

    def kernel(attended_ref, rows_ref, keep_ref, give_ref, turned):
        @pl.when(pl.program_id(0) == 0)
        def prepare():
            turned[...] = rows_ref[...].T

        block = attended_ref[...].reshape(Q_WIDTH, own).astype(jnp.bfloat16)
        first_or_second(keep_ref, give_ref, dot(turned[...], block))

    return call(
        kernel,
        (2,),
        [pl.BlockSpec((OWN_HEADS, HEAD_DIM, own), lambda p: (0, 0, p)), fixed(out_rows)],
        [pl.BlockSpec((width, own), lambda p: (0, 0))] * 2,
        two_blocks(width, own),
        [pltpu.VMEM((width, Q_WIDTH), jnp.bfloat16)],
    )(attended, out_rows)


def two_blocks(width, own):
    return [
        jax.ShapeDtypeStruct((width, own), jnp.float32),
        jax.ShapeDtypeStruct((width, own), jnp.bfloat16),
    ]


def first_or_second(keep_ref, give_ref, value):
    @pl.when(pl.program_id(0) == 0)
    def keep():
        keep_ref[...] = value

    @pl.when(pl.program_id(0) == 1)
    def give():
        give_ref[...] = value.astype(jnp.bfloat16)


def mixer(chip, normed, cotangent, weights, down):
    width, own = normed[0].shape
    units = down.shape[0]

    def kernel(first_ref, second_ref, wanted_a, wanted_b, weights_ref, down_ref, *refs):
        hidden_ref, grad_ref, keep_ref, give_ref, turned, wanted = refs
        step = pl.program_id(0)

        @pl.when(step == 0)
        def first():
            turned[...] = first_ref[...].T
            wanted[...] = wanted_a[0]

        @pl.when(step == 1)
        def second():
            turned[...] = second_ref[...].T
            wanted[...] = wanted_b[0]

        gate = dot(turned[...], weights_ref[:, :units])
        up = dot(turned[...], weights_ref[:, units:])
        logistic = 1.0 / (1.0 + jnp.exp(-gate))
        silu = gate * logistic
        hidden_ref[...] = (silu * up).astype(jnp.bfloat16)
        grad_hidden = dot_rows(wanted[...], down_ref[...])
        grad_ref[:, :units] = (
            grad_hidden * up * (logistic * (1.0 + gate * (1.0 - logistic)))
        ).astype(jnp.bfloat16)
        grad_ref[:, units:] = (grad_hidden * silu).astype(jnp.bfloat16)
        term = dot_rows(weights_ref[...], grad_ref[...])

        @pl.when(step == 0)
        def keep():
            keep_ref[...] = term

        @pl.when(step == 1)
        def give():
            give_ref[...] = term.astype(jnp.bfloat16)

    block = pl.BlockSpec((1, own, width), lambda p: (chip, 0, 0))
    whole = pl.BlockSpec((width, own), lambda p: (0, 0))
    return call(
        kernel,
        (2,),
        [fixed(normed[0]), fixed(normed[1]), block, block, fixed(weights), fixed(down)],
        [rows_at(own, units), rows_at(own, 2 * units), whole, whole],
        [
            jax.ShapeDtypeStruct((2 * own, units), jnp.bfloat16),
            jax.ShapeDtypeStruct((2 * own, 2 * units), jnp.bfloat16),
            jax.ShapeDtypeStruct((width, own), jnp.float32),
            jax.ShapeDtypeStruct((width, own), jnp.bfloat16),
        ],
        [pltpu.VMEM((own, width), jnp.bfloat16), pltpu.VMEM((own, width), jnp.bfloat16)],
    )(normed[0], normed[1], cotangent[0], cotangent[1], weights, down)


def add_block(keep, arrived):
    def kernel(keep_ref, arrived_ref, out_ref):
        out_ref[...] = (keep_ref[...] + arrived_ref[...].astype(jnp.float32)).astype(jnp.bfloat16)

    rows = keep.shape[0] // 2
    part = rows_at(rows, keep.shape[1])
    return call(
        kernel, (2,), [part, part], part, jax.ShapeDtypeStruct(keep.shape, jnp.bfloat16)
    )(keep, arrived)


def pair_rows(position, refs, target):
    own = target.shape[0]
    for number in range(TEAM):

        @pl.when(position == number)
        def move():
            start = number // 4 * own
            target[...] = refs[number % 4][start : start + own]


def mixer_output(hidden, down):
    own, units = hidden[0].shape[0] // 2, hidden[0].shape[1]
    specs, shapes = kept_given(own, down.shape[1], 0)

    def kernel(down_ref, *refs):
        keep_ref, give_ref, chosen = refs[4:]
        pair_rows(pl.program_id(0), refs[:4], chosen)
        keep_or_give(pl.program_id(0), keep_ref, give_ref, dot(chosen[...], down_ref[...]))

    return call(
        kernel,
        (TEAM,),
        [fixed(down)] + [fixed(block) for block in hidden],
        specs,
        shapes,
        [pltpu.VMEM((own, units), jnp.bfloat16)],
    )(down, *hidden)


def write_teams(places_ref, total, out_ref, teams):
    rows = total.shape[0] // teams
    for team in range(teams):
        steps = (team + teams - places_ref[0]) % teams
        block = total[team * rows : (team + 1) * rows, :].astype(out_ref.dtype)
        out_ref[pl.ds(steps, 1)] = block[None]


def token_product(grid, lefts, rights):
    rows, own = lefts[0].shape
    width = rights[0].shape[1]
    teams = grid.teams

    def kernel(places_ref, *refs):
        left_refs, right_refs = refs[:TEAM], refs[TEAM : TEAM + 4]
        out_ref, total, chosen = refs[TEAM + 4 :]
        position = pl.program_id(0)
        pair_rows(position, right_refs, chosen)

        def add(value):
            @pl.when(position == 0)
            def first():
                total[...] = value

            @pl.when(position > 0)
            def later():
                total[...] += value

        for number, source in enumerate(left_refs):

            @pl.when(position == number)
            def block():
                add(dot(source[...], chosen[...]))

        @pl.when(position == TEAM - 1)
        def last():
            write_teams(places_ref, total, out_ref, teams)

    return call(
        kernel,
        (TEAM,),
        [fixed(block) for block in list(lefts) + list(rights)],
        pl.BlockSpec((teams, rows // teams, width), lambda p, *unused: (0, 0, 0)),
        jax.ShapeDtypeStruct((teams, rows // teams, width), jnp.bfloat16),
        [pltpu.VMEM((rows, width), jnp.float32), pltpu.VMEM((own, width), jnp.bfloat16)],
        prefetch=1,
    )(grid.places(), *lefts, *rights)


def down_product(grid, hidden, cotangent):
    units = hidden[0].shape[1]
    own, width = cotangent[0].shape[1:]
    teams = grid.teams

    def kernel(places_ref, *refs):
        hidden_refs, sources, (out_ref, total, wanted, chosen) = refs[:4], refs[4:6], refs[6:]
        position = pl.program_id(0)
        pick(position, sources, wanted)
        pair_rows(position, hidden_refs, chosen)
        value = dot(chosen[...].T, wanted[...])

        @pl.when(position == 0)
        def first():
            total[...] = value

        @pl.when(position > 0)
        def later():
            total[...] += value

        @pl.when(position == TEAM - 1)
        def last():
            write_teams(places_ref, total, out_ref, teams)

    return call(
        kernel,
        (TEAM,),
        [fixed(block) for block in list(hidden) + list(cotangent)],
        pl.BlockSpec((teams, units // teams, width), lambda p, *unused: (0, 0, 0)),
        jax.ShapeDtypeStruct((teams, units // teams, width), jnp.bfloat16),
        [
            pltpu.VMEM((units, width), jnp.float32),
            pltpu.VMEM((own, width), jnp.bfloat16),
            pltpu.VMEM((own, units), jnp.bfloat16),
        ],
        prefetch=1,
    )(grid.places(), *hidden, *cotangent)


def project_out_back(grid, grads, out_rows, attended):
    teams = grid.teams
    own = attended[0].shape[-1] // 2
    tokens = TEAM * own
    width = out_rows.shape[1]

    def kernel(places_ref, rows_ref, *refs):
        attended_refs, sources = refs[:4], refs[4 : 4 + TEAM]
        grad_ref, out_ref, chosen, total, wanted = refs[4 + TEAM :]
        position = pl.program_id(0)
        pick(position, sources, chosen)
        for number in range(TEAM):

            @pl.when(position == number)
            def move():
                start = number // 4 * own
                wanted[...] = attended_refs[number % 4][:, :, start : start + own].astype(
                    jnp.bfloat16
                )

        grad_ref[...] = (
            dot(rows_ref[...], chosen[...])
            .astype(jnp.bfloat16)
            .reshape(OWN_HEADS, HEAD_DIM, own)
        )
        value = dot_rows(wanted[...].reshape(Q_WIDTH, own), chosen[...])

        @pl.when(position == 0)
        def first():
            total[...] = value

        @pl.when(position > 0)
        def later():
            total[...] += value

        @pl.when(position == TEAM - 1)
        def last():
            write_teams(places_ref, total, out_ref, teams)

    heads = pl.BlockSpec((OWN_HEADS, HEAD_DIM, own), lambda p, *unused: (0, 0, p))
    shape = (teams, Q_WIDTH // teams, width)
    return call(
        kernel,
        (TEAM,),
        [fixed(out_rows)] + [fixed(block) for block in list(attended) + list(grads)],
        [heads, pl.BlockSpec(shape, lambda p, *unused: (0, 0, 0))],
        [
            jax.ShapeDtypeStruct((OWN_HEADS, HEAD_DIM, tokens), jnp.bfloat16),
            jax.ShapeDtypeStruct(shape, jnp.bfloat16),
        ],
        [
            pltpu.VMEM((width, own), jnp.bfloat16),
            pltpu.VMEM((Q_WIDTH, width), jnp.float32),
            pltpu.VMEM((OWN_HEADS, HEAD_DIM, own), jnp.bfloat16),
        ],
        prefetch=1,
    )(grid.places(), out_rows, *attended, *grads)


def project_back(chip, query_rot, own_grads, returned, cosine, sine_table, weights):
    width = weights.shape[0]
    own = query_rot.shape[-1] // TEAM
    half = HEAD_DIM // 2

    def kernel(query_ref, cosine_ref, sine_ref, weights_ref, *refs):
        kv_refs = refs[: 1 + len(returned)]
        keep_ref, give_ref, grad_ref = refs[1 + len(returned) :]
        cosines, sines = cosine_ref[...], sine_ref[...]

        def unrotated(block):
            scaled = block * sines
            shifted = jnp.concatenate([scaled[half:], -scaled[:half]], axis=0)
            return (block * cosines + shifted).astype(jnp.bfloat16)

        for head in range(OWN_HEADS):
            grad_ref[head * HEAD_DIM : (head + 1) * HEAD_DIM] = unrotated(query_ref[head])
        kv = kv_refs[0][...]
        for ref in kv_refs[1:]:
            kv = kv + ref[...].astype(jnp.float32)
        for head in range(OWN_KV):
            start = Q_WIDTH + head * HEAD_DIM
            grad_ref[start : start + HEAD_DIM] = unrotated(kv[0, head])
            start = start + KV_WIDTH
            grad_ref[start : start + HEAD_DIM] = kv[1, head].astype(jnp.bfloat16)
        first_or_second(keep_ref, give_ref, dot(weights_ref[:, :LINED], grad_ref[...]))

    def at(p):
        return chip + 4 * p

    tables = pl.BlockSpec((HEAD_DIM, own), lambda p: (0, at(p)))
    kv_heads = pl.BlockSpec((2, OWN_KV, HEAD_DIM, own), lambda p: (0, 0, 0, at(p)))
    return call(
        kernel,
        (2,),
        [
            pl.BlockSpec((OWN_HEADS, HEAD_DIM, own), lambda p: (0, 0, at(p))),
            tables,
            tables,
            fixed(weights),
        ]
        + [kv_heads] * (1 + len(returned)),
        [pl.BlockSpec((width, own), lambda p: (0, 0))] * 2 + [lanes_at(LINED, own)],
        two_blocks(width, own) + [jax.ShapeDtypeStruct((LINED, 2 * own), jnp.bfloat16)],
    )(query_rot, cosine, sine_table, weights, own_grads, *returned)


def lined_product(grid, normed, grads):
    width, tokens = normed.shape
    own = tokens // TEAM
    teams = grid.teams

    def kernel(places_ref, normed_ref, *refs):
        grad_refs, (out_ref, total, chosen) = refs[:4], refs[4:]
        position = pl.program_id(0)
        for number in range(TEAM):

            @pl.when(position == number)
            def move():
                start = number // 4 * own
                chosen[...] = grad_refs[number % 4][:, start : start + own]

        value = dot_rows(normed_ref[...], chosen[...])

        @pl.when(position == 0)
        def first():
            total[...] = value

        @pl.when(position > 0)
        def later():
            total[...] += value

        @pl.when(position == TEAM - 1)
        def last():
            write_teams(places_ref, total, out_ref, teams)

    return call(
        kernel,
        (TEAM,),
        [lanes_at(width, own)] + [fixed(block) for block in grads],
        pl.BlockSpec((teams, width // teams, LINED), lambda p, *unused: (0, 0, 0)),
        jax.ShapeDtypeStruct((teams, width // teams, LINED), jnp.bfloat16),
        [pltpu.VMEM((width, LINED), jnp.float32), pltpu.VMEM((LINED, own), jnp.bfloat16)],
        prefetch=1,
    )(grid.places(), normed, *grads)


def combine(keep, arrived, axis):
    size = keep.shape[axis] // 4
    shape = (keep.shape[0], size) if axis else (size, keep.shape[1])

    def kernel(keep_ref, arrived_ref, own_ref, *block_refs):
        position = pl.program_id(0)
        total = keep_ref[...] + arrived_ref[...].astype(jnp.float32)

        @pl.when(position == 0)
        def own():
            own_ref[...] = total

        for number, ref in enumerate(block_refs, 1):

            @pl.when(position == number)
            def other():
                ref[...] = total.astype(jnp.bfloat16)

    part = pl.BlockSpec(shape, (lambda p: (0, p)) if axis else (lambda p: (p, 0)))
    whole = pl.BlockSpec(shape, lambda p: (0, 0))
    own, *blocks = call(
        kernel,
        (4,),
        [part, part],
        [whole] * 4,
        [jax.ShapeDtypeStruct(shape, jnp.float32)]
        + [jax.ShapeDtypeStruct(shape, jnp.bfloat16)] * 3,
    )(keep, arrived)
    return own, blocks


def summed(refs):
    total = refs[0][...]
    for ref in refs[1:]:
        total = total + ref[...].astype(jnp.float32)
    return total


def finish(kernel, arrays, shapes):
    return call(
        kernel,
        (1,),
        [fixed(array) for array in arrays],
        [pl.BlockSpec(shape.shape, lambda p: (0, 0)) for shape in shapes],
        shapes,
    )(*arrays)


def finish_middle(terms, inputs_t, gain):
    def kernel(*refs):
        inputs_ref, gain_ref, middle_ref, normed_ref = refs[len(terms) :]
        middle = inputs_ref[...].astype(jnp.float32) + summed(refs[: len(terms)])
        middle_ref[...] = middle
        scale = lax.rsqrt(jnp.mean(middle * middle, axis=0, keepdims=True) + eps_norm)
        normed_ref[...] = (middle * scale * gain_ref[...]).astype(jnp.bfloat16)

    shape = inputs_t.shape
    return finish(
        kernel,
        list(terms) + [inputs_t, gain],
        [jax.ShapeDtypeStruct(shape, jnp.float32), jax.ShapeDtypeStruct(shape, jnp.bfloat16)],
    )


def norm_back(values, gain, grad):
    inverse = lax.rsqrt(jnp.mean(values * values, axis=0, keepdims=True) + eps_norm)
    normal = values * inverse
    scaled = grad * gain
    inner = jnp.mean(scaled * normal, axis=0, keepdims=True)
    return inverse * (scaled - normal * inner), jnp.sum(grad * normal, axis=1, keepdims=True)


def finish_second(terms, middle, cotangent, gain):
    def kernel(*refs):
        middle_ref, cotangent_ref, gain_ref, grad_ref, attn_ref, gain_out = refs[len(terms) :]
        norm_grad, gain_part = norm_back(
            middle_ref[...], gain_ref[...], summed(refs[: len(terms)])
        )
        grad = cotangent_ref[...].T.astype(jnp.float32) + norm_grad
        grad_ref[...] = grad
        attn_ref[...] = grad.astype(jnp.bfloat16)
        gain_out[...] = gain_part

    shape = middle.shape
    return finish(
        kernel,
        list(terms) + [middle, cotangent, gain],
        [
            jax.ShapeDtypeStruct(shape, jnp.float32),
            jax.ShapeDtypeStruct(shape, jnp.bfloat16),
            jax.ShapeDtypeStruct((shape[0], 1), jnp.float32),
        ],
    )


def finish_first(terms, inputs_t, grad_middle, gain):
    def kernel(*refs):
        inputs_ref, grad_ref, gain_ref, out_ref, gain_out = refs[len(terms) :]
        norm_grad, gain_part = norm_back(
            inputs_ref[...].astype(jnp.float32), gain_ref[...], summed(refs[: len(terms)])
        )
        out_ref[...] = (grad_ref[...] + norm_grad).T
        gain_out[...] = gain_part

    width, own = inputs_t.shape
    return finish(
        kernel,
        list(terms) + [inputs_t, grad_middle, gain],
        [
            jax.ShapeDtypeStruct((own, width), jnp.float32),
            jax.ShapeDtypeStruct((width, 1), jnp.float32),
        ],
    )


def finish_output(terms, middle):
    def kernel(*refs):
        middle_ref, out_ref = refs[len(terms) :]
        out_ref[...] = (middle_ref[...].T + summed(refs[: len(terms)])).astype(jnp.bfloat16)

    return finish(
        kernel, list(terms) + [middle], [jax.ShapeDtypeStruct(terms[0].shape, jnp.bfloat16)]
    )[0]


def sum_teams(product, parts, kind):
    def kernel(own_ref, *refs):
        total = own_ref[0].astype(jnp.float32)
        for ref in refs[:-1]:
            total = total + ref[...].astype(jnp.float32)
        refs[-1][...] = total.astype(kind)

    shape = product.shape[1:]
    return call(
        kernel,
        (1,),
        [pl.BlockSpec((1,) + shape, lambda p: (0, 0, 0))] + [fixed(part) for part in parts],
        pl.BlockSpec(shape, lambda p: (0, 0)),
        jax.ShapeDtypeStruct(shape, kind),
    )(product, *parts)


def rope_tables(positions):
    half_dim = HEAD_DIM // 2
    frequency = rope_base ** (-(jnp.arange(half_dim, dtype=jnp.float32) * 2.0 / HEAD_DIM))
    angles = frequency[:, None] * positions.astype(jnp.float32)[None, :]
    angles = jnp.concatenate([angles, angles], axis=0)
    return (jnp.cos(angles), jnp.sin(angles))


def per_device(
    inputs,
    positions,
    norm_first,
    query_weight,
    key_weight,
    value_weight,
    out_weight,
    norm_second,
    gate_weight,
    up_weight,
    down_weight,
    cotangent,
):
    grid = Grid()
    member, teams = grid.member, grid.teams
    chip, core = member // 2, member % 2
    own, width = inputs.shape
    tokens = own * TEAM
    rows = query_weight.shape[0]
    unit_rows = down_weight.shape[0]
    units = unit_rows * teams
    longest = own * grid.count // 4
    steps_back = min((longest - 2) // tokens + 1, teams - 1)
    bf16, f32 = jnp.bfloat16, jnp.float32
    order = Order(jnp.zeros((8, 128), jnp.int32))

    def dynamic(array, index, axis=0):
        return lax.dynamic_index_in_dim(array, index, axis, keepdims=False)

    def by_member(weight):
        return jnp.transpose(weight.reshape(rows, TEAM, -1), (1, 0, 2))

    def units_by_member(weight):
        blocks = jnp.transpose(weight.reshape(rows, teams, TEAM, unit_rows), (2, 0, 1, 3))
        return blocks.reshape(TEAM, rows, units)

    gains = jnp.pad(jnp.stack([norm_first, norm_second], axis=1), ((0, 0), (0, LANES - 2)))
    columns = jnp.concatenate(
        [
            by_member(query_weight),
            by_member(key_weight),
            by_member(value_weight),
            jnp.broadcast_to(gains[None], (TEAM, rows, LANES)),
            units_by_member(gate_weight),
            units_by_member(up_weight),
        ],
        axis=-1,
    )
    attn_wide = LINED + LANES
    columns = columns.reshape(TEAM // 2, 2, rows, attn_wide + 2 * units)
    position_chips = jnp.stack(grid.chips(positions))
    all_positions = jnp.concatenate([position_chips, grid.turn(position_chips, 1)]).reshape(tokens)
    inputs_t = inputs.T
    columns, inputs_t = order.step(columns, inputs_t)
    pairs = [
        dynamic(columns, chip)
        if other == 0
        else grid.turn(dynamic(columns, chip ^ other), 2 * other)
        for other in range(4)
    ]
    inputs_two = [grid.turn(inputs_t, 2), grid.turn(inputs_t, 4)]
    cosine, sine_table = rope_tables(all_positions)
    block_index = steps_back * TEAM + (
        jnp.array([relative(p) for p in range(TEAM)], jnp.int32) ^ member
    )
    token_index = (block_index[:, None] * own + jnp.arange(own, dtype=jnp.int32)).reshape(tokens)
    starts = token_index - all_positions
    low = jnp.concatenate([starts[::own] // BLOCK, member[None]]).astype(jnp.int32)
    starts = starts[None]
    third = width // 3
    down_thirds = jnp.concatenate(
        [down_weight[:, part * third : (part + 1) * third] for part in range(3)], axis=0
    ).reshape(TEAM, rows, third)
    cosine, sine_table, starts, low, down_thirds, pairs, inputs_two, inputs_t = order.step(
        cosine, sine_table, starts, low, down_thirds, pairs, inputs_two, inputs_t
    )
    inputs_three = grid.turn(inputs_t, 6)
    pairs = jnp.stack(pairs)
    pairs_keep, pairs_give = dynamic(pairs, core, 1), dynamic(pairs, 1 - core, 1)
    team_rows = jnp.concatenate([pairs_keep, grid.turn(pairs_give, 1)], axis=0)
    attn_rows, team_rows, out_weight = order.step(
        team_rows[..., :attn_wide], team_rows, out_weight
    )
    attn_z = grid.spread(attn_rows)
    inputs_others = [grid.turn(block, 1) for block in [inputs_t] + inputs_two]
    attn_z, inputs_three = order.step(attn_z, inputs_three)
    inputs_others = inputs_others + [grid.turn(inputs_three, 1)]
    inputs_team = [inputs_t] + inputs_two + [inputs_three] + inputs_others
    out_own = grid.to_members(out_weight)
    attn_w = place_rows(grid, attn_z, 0, attn_wide).reshape(width, attn_wide)
    attn_w, inputs_team, out_own = order.step(attn_w, inputs_team, out_own)

    mixer_own = jnp.concatenate([team_rows[..., attn_wide:], down_thirds], axis=-1)

    out_own, mixer_own = order.step(out_own, mixer_own)
    out_z = grid.spread(out_own)
    mixer_hops = [grid.both_ways(mixer_own, mixer_own)]

    def next_hop():
        if len(mixer_hops) < teams - 1:
            mixer_hops.append(grid.both_ways(*mixer_hops[-1]))

    normed_first, queries, own_piece = project(inputs_team, attn_w, cosine, sine_table)
    own_piece, out_z, mixer_hops[-1], attn_w, cotangent = order.step(
        own_piece, out_z, mixer_hops[-1], attn_w, cotangent
    )
    arrived = [grid.shift(own_piece, step, False) for step in range(1, steps_back + 1)]
    cotangent_chips = [cotangent, grid.turn(cotangent, 2), grid.turn(cotangent, 4)]
    out_rows = place_rows(grid, [block[None] for block in out_z], 0, width)
    out_rows = out_rows.reshape(Q_WIDTH, width)
    gain_first = attn_w[:, LINED : LINED + 1].astype(f32)
    gain_second = attn_w[:, LINED + 1 : LINED + 2].astype(f32)
    arrived, gain_first, gain_second, out_rows, cotangent_chips, mixer_hops[-1] = order.step(
        arrived, gain_first, gain_second, out_rows, cotangent_chips, mixer_hops[-1]
    )
    cotangent_chips = cotangent_chips + [grid.turn(cotangent_chips[0], 6)]
    next_hop()

    pieces = [own_piece] + arrived
    attended, normalizer = [None] * 4, [None] * 4

    def run_attention(other_chip):
        attended[other_chip], normalizer[other_chip] = attend(
            low, starts, order.step(queries), pieces, other_chip
        )
        keep, give = project_out(attended[other_chip], out_rows)
        return keep, order.step(give)

    keep_one, give = run_attention(1)
    passed_one = grid.turn(give, 1)
    keep_two, give = run_attention(2)
    passed_one, cotangent_chips = order.step(passed_one, cotangent_chips)
    passed_two = grid.turn(give, 1)
    block_one = order.step(add_block(keep_one, passed_one))
    keep_three, give = run_attention(3)
    passed_two, mixer_hops[-1] = order.step(passed_two, mixer_hops[-1])
    passed_three = grid.turn(give, 1)
    block_one, block_two = order.step(block_one, add_block(keep_two, passed_two))
    terms = [grid.turn(block_one, 2), grid.turn(block_two, 4)]
    keep_own, give = run_attention(0)
    passed_three, terms[0] = order.step(passed_three, terms[0])
    block_three = order.step(add_block(keep_three, passed_three))
    terms.append(grid.turn(block_three, 6))
    passed_own = grid.turn(give, 1)
    passed_own, cotangent_stack = order.step(passed_own, jnp.stack(cotangent_chips))
    cotangent_other = grid.turn(cotangent_stack, 1)
    terms[1], cotangent_other = order.step(terms[1], cotangent_other)
    cotangent_team = [cotangent_stack, cotangent_other]
    next_hop()
    total = keep_own
    terms = order.step([passed_own] + terms)
    middle, normed_second = finish_middle([total] + terms, inputs_t, gain_second)
    normed_second = order.step(normed_second)
    second_chips = [normed_second, grid.turn(normed_second, 2), grid.turn(normed_second, 4)]
    second_other = [grid.turn(normed_second, 1)]
    mixer_hops[-1] = order.step(mixer_hops[-1])
    while len(mixer_hops) < teams - 1:
        next_hop()
        mixer_hops[-1] = order.step(mixer_hops[-1])
    mixer_w, down_w = place_mixer(grid, mixer_own, mixer_hops, units, unit_rows)
    mixer_w = mixer_w.reshape(width, 2 * units)
    down_w = down_w.reshape(units, width)
    mixer_w, down_w, second_other[0] = order.step(mixer_w, down_w, second_other[0])

    def send_teams(product, first=1, last=teams):
        return [grid.shift(product[steps], steps) for steps in range(first, last)]

    def run_mixer(other_chip):
        hidden_part, grads_part, keep, give = mixer(
            other_chip,
            (second_chips[other_chip], second_other[other_chip]),
            cotangent_team,
            mixer_w,
            down_w,
        )
        return hidden_part, grads_part, keep, order.step(give)

    parts = [run_mixer(0)]
    passed = [grid.turn(parts[0][3], 1)]
    second_chips = order.step(second_chips)
    second_chips = second_chips + [grid.turn(second_chips[0], 6)]
    second_other += order.step([grid.turn(second_chips[1], 1), grid.turn(second_chips[2], 1)])
    parts.append(run_mixer(1))
    passed.append(grid.turn(parts[1][3], 1))
    second_chips[3], passed[0] = order.step(second_chips[3], passed[0])
    second_other.append(grid.turn(second_chips[3], 1))
    parts.append(run_mixer(2))
    passed[1], second_other[3] = order.step(passed[1], second_other[3])
    block = order.step(add_block(parts[1][2], passed[1]))
    terms = [parts[0][2], passed[0], grid.turn(block, 2)]
    second_other[3] = order.step(second_other[3])
    passed.append(grid.turn(parts[2][3], 1))
    parts.append(run_mixer(3))
    passed[2] = order.step(passed[2])
    passed.append(grid.turn(parts[3][3], 1))
    block = order.step(add_block(parts[2][2], passed[2]))
    terms.append(grid.turn(block, 4))
    passed[3] = order.step(passed[3])
    hidden, grads = [part[0] for part in parts], [part[1] for part in parts]
    block, grads, hidden = order.step(add_block(parts[3][2], passed[3]), grads, hidden)
    terms.append(grid.turn(block, 6))
    second_team = second_chips + second_other
    down_part = order.step(down_product(grid, hidden, cotangent_team))
    down_parts = send_teams(down_part, 1, 3)
    second_team, grads = order.step(second_team, grads)
    mixer_part = token_product(grid, second_team, grads)
    mixer_part, terms, down_parts = order.step(mixer_part, terms, down_parts)
    mixer_parts = send_teams(mixer_part, 1, 2)
    down_parts += send_teams(down_part, 3)
    grad_middle, grad_attn, second_part = finish_second(terms, middle, cotangent, gain_second)
    grad_attn, hidden = order.step(grad_attn, hidden)
    attn_chips = [grad_attn, grid.turn(grad_attn, 2), grid.turn(grad_attn, 4)]
    attn_chips, hidden, mixer_parts, down_parts = order.step(
        attn_chips, hidden, mixer_parts, down_parts
    )
    attn_chips = attn_chips + [grid.turn(attn_chips[0], 6)]
    mixer_parts += send_teams(mixer_part, 3)
    attn_other = [grid.turn(attn_chips[0], 1)]
    out_keep, out_give = mixer_output(hidden, down_w)
    out_give, attn_other = order.step(out_give, attn_other)
    attn_other += order.step([grid.turn(attn_chips[1], 1), grid.turn(attn_chips[2], 1)])
    attn_chips[3], mixer_parts = order.step(attn_chips[3], mixer_parts)
    mixer_late = send_teams(mixer_part, 2, 3)
    attn_other.append(order.step(grid.turn(attn_chips[3], 1)))
    attn_team = attn_chips + attn_other

    grad_attended, out_part = project_out_back(grid, attn_team, out_rows, attended)
    grad_attended, out_give = order.step(grad_attended, out_give)
    out_other = grid.turn(out_give, 1)
    query_rot, own_grads, back_grads = attend_back(
        low, starts, queries, grad_attended, attended, normalizer, pieces, 0, OWN_KV
    )
    query_rot, own_grads, back_grads, out_other, mixer_late = order.step(
        query_rot, own_grads, back_grads, out_other, mixer_late
    )
    mixer_parts = mixer_parts + mixer_late
    returned = [
        grid.shift(back_grads[step - 1], -step, False) for step in range(1, steps_back + 1)
    ]
    out_total, out_blocks = combine(out_keep, out_other, 0)
    out_blocks = order.step(out_blocks)
    out_terms = [grid.turn(out_blocks[0], 2), grid.turn(out_blocks[1], 4)]
    mixer_total = sum_teams(mixer_part, mixer_parts, bf16)
    def members_rows(total):
        blocks = total.reshape(TEAM // 2, 2, rows, -1)
        return dynamic(blocks, core, 1), grid.turn(dynamic(blocks, 1 - core, 1), 1)

    def owner_columns(mine, others):
        both = jnp.stack([mine, others])
        first = jnp.where(core == 0, both[0], both[1])
        second = jnp.where(core == 0, both[1], both[0])
        both = jnp.stack([first, second], axis=1)
        found = [
            dynamic(both, chip) if other == 0 else grid.turn(dynamic(both, chip ^ other), 2 * other)
            for other in range(4)
        ]
        return found

    def in_order(found):
        stacked = jnp.stack(found)
        return jnp.stack([dynamic(stacked, chip ^ other) for other in range(4)]).reshape(
            (TEAM,) + found[0].shape[1:]
        )

    returned, mixer_total = order.step(returned, mixer_total)
    mixer_mine, mixer_others = members_rows(mixer_total)
    lined_grads = [None] * 4

    def run_back(other_chip):
        keep, give, lined_grads[other_chip] = project_back(
            other_chip, order.step(query_rot), own_grads, returned, cosine, sine_table, attn_w
        )
        return keep, order.step(give)

    keep_one, give = run_back(1)
    passed_one = grid.turn(give, 1)
    keep_two, give = run_back(2)
    passed_one, out_terms = order.step(passed_one, out_terms)
    passed_two = grid.turn(give, 1)
    block_one = order.step(add_block(keep_one, passed_one))
    keep_three, give = run_back(3)
    passed_two, mixer_others = order.step(passed_two, mixer_others)
    passed_three = grid.turn(give, 1)
    block_one, block_two = order.step(block_one, add_block(keep_two, passed_two))
    terms = [grid.turn(block_one, 2), grid.turn(block_two, 4)]
    keep_own, give = run_back(0)
    passed_three = order.step(passed_three)
    block_three = order.step(add_block(keep_three, passed_three))
    terms.append(grid.turn(block_three, 6))
    passed_own = grid.turn(give, 1)
    attn_part = lined_product(grid, normed_first, lined_grads)
    attn_part, passed_own, terms[:2] = order.step(attn_part, passed_own, terms[:2])
    attn_parts = send_teams(attn_part)
    out_terms = out_terms + [grid.turn(out_blocks[2], 6)]
    total = keep_own
    terms = order.step([passed_own] + terms)
    down_grad = sum_teams(down_part, down_parts, f32)
    attn_parts, down_grad, out_part = order.step(attn_parts, down_grad, out_part)
    attn_total = sum_teams(attn_part, attn_parts, bf16)
    attn_mine, attn_others = members_rows(attn_total)
    out_parts = send_teams(out_part)
    outputs = finish_output([out_total] + out_terms, middle)
    attn_others, outputs = order.step(attn_others, outputs)
    mixer_found = owner_columns(mixer_mine, mixer_others)
    input_grad, first_part = finish_first([total] + terms, inputs_t, grad_middle, gain_first)
    gain_parts = jnp.concatenate([first_part, second_part], axis=1).T
    gain_parts, out_parts = order.step(gain_parts, out_parts)
    gain_other = grid.turn(gain_parts, 1)
    out_own = sum_teams(out_part, out_parts, bf16)
    mixer_found, gain_other, out_own = order.step(mixer_found, gain_other, out_own)
    gain_parts = gain_parts + gain_other
    gain_chips = [grid.turn(gain_parts, 2 * other) for other in range(1, 4)]
    gain_chips = order.step(gain_chips)
    attn_found = owner_columns(attn_mine, attn_others)
    out_grad = grid.to_owners(out_own)
    for other in gain_chips:
        gain_parts = gain_parts + other
    mixer_columns = in_order(mixer_found)

    def whole_units(blocks):
        blocks = blocks.reshape(TEAM, rows, teams, unit_rows)
        return jnp.transpose(blocks, (1, 2, 0, 3)).reshape(rows, TEAM * units).astype(f32)

    def whole(blocks):
        return jnp.transpose(blocks, (1, 0, 2)).reshape(rows, -1).astype(f32)

    gate_grad = whole_units(mixer_columns[..., :units])
    up_grad = whole_units(mixer_columns[..., units:])
    attn_found, out_grad, gain_parts = order.step(attn_found, out_grad, gain_parts)
    gain_blocks = gain_parts.reshape(2, teams, TEAM, rows)
    gain_sums = dynamic(dynamic(gain_blocks, grid.team, 1), member, 1)
    for steps in range(1, teams):
        block = dynamic(dynamic(gain_blocks, (grid.team + steps) % teams, 1), member, 1)
        gain_sums = gain_sums + grid.shift(block, steps)
    out_grad = out_grad.astype(f32)
    attn_columns = in_order(attn_found)
    gain_sums = gain_sums + order.token[0, 0].astype(f32)
    return (
        outputs,
        input_grad,
        gain_sums[0],
        whole(attn_columns[..., :Q_WIDTH]),
        whole(attn_columns[..., Q_WIDTH : Q_WIDTH + KV_WIDTH]),
        whole(attn_columns[..., Q_WIDTH + KV_WIDTH :]),
        out_grad,
        gain_sums[1],
        gate_grad,
        up_grad,
        down_grad,
    )


def solution(mesh):
    matrix, vector = P("dev", None), P("dev")
    in_specs = (matrix, vector, vector) + (matrix,) * 4 + (vector,) + (matrix,) * 4
    out_specs = (matrix, matrix, vector) + (matrix,) * 4 + (vector,) + (matrix,) * 3
    return jax.shard_map(
        per_device, mesh=mesh, in_specs=in_specs, out_specs=out_specs, check_vma=False
    )
```

```python
import math

import jax
import jax.numpy as jnp
from jax import lax
from jax.experimental import pallas as pl
from jax.experimental.pallas import tpu as pltpu
from jax.sharding import PartitionSpec as P

HEADS = 16
KV_HEADS = 8
HEAD_DIM = 96
TEAM = 8

eps_norm = 1e-05
rope_base = 100000.0
masked_score = -1e30

OWN_HEADS = HEADS // TEAM
OWN_KV = KV_HEADS // TEAM
GROUP = HEADS // KV_HEADS
BLOCK = 256
LANES = 128
score_scale = 1.0 / math.sqrt(HEAD_DIM)
log2_scale = score_scale / math.log(2.0)
kernel_vmem = 56 * 1024 * 1024
small_cost = pl.CostEstimate(flops=1000, bytes_accessed=1000, transcendentals=0)

Q_WIDTH = OWN_HEADS * HEAD_DIM
KV_WIDTH = OWN_KV * HEAD_DIM
LINED = Q_WIDTH + 2 * KV_WIDTH


def relative(position):
    return 2 * (position % 4) + position // 4


def visible_mask(block, starts, ends):
    key = block * BLOCK + lax.broadcasted_iota(jnp.int32, (BLOCK, 1), 0)
    return (key >= starts) & (key <= ends)


def chunk_lanes(ref, chunk):
    spot = pl.ds(chunk * BLOCK, BLOCK)
    return jnp.concatenate([ref[head, :, spot] for head in range(GROUP)], axis=1)


def chunk_range(chunk, starts_ref, last):
    starts = starts_ref[:, pl.ds(chunk * BLOCK, BLOCK)]
    ends = last * BLOCK + lax.broadcasted_iota(jnp.int32, (1, BLOCK), 1)
    return (
        jnp.concatenate([starts] * GROUP, axis=1),
        jnp.concatenate([ends] * GROUP, axis=1),
    )


def attend_kernel(low_ref, starts_ref, query_ref, *refs):
    count = len(refs) - 4
    member = low_ref[TEAM]
    pieces = refs[:count]
    out_ref, norm_ref, keys, values = refs[count:]
    per_piece = pieces[0].shape[-1] // BLOCK
    for back, piece in enumerate(pieces):
        for part in range(per_piece):
            block = (count - 1 - back) * per_piece + (relative(part) ^ member)
            spot = pl.ds(part * BLOCK, BLOCK)
            keys[block] = piece[0, 0, :, spot].T
            values[block] = piece[1, 0, :, spot]
    own_block = (count - 1) * per_piece
    for chunk in range(per_piece):
        queries = chunk_lanes(query_ref, chunk)
        last = own_block + (relative(chunk) ^ member)
        starts, ends = chunk_range(chunk, starts_ref, last)

        def advance(step, running):
            top, total, summed = running
            block = last - step
            scores = (
                jnp.dot(keys[block], queries, preferred_element_type=jnp.float32) * log2_scale
            )
            scores = jnp.where(visible_mask(block, starts, ends), scores, masked_score)
            new_top = jnp.maximum(top, jnp.max(scores, axis=0, keepdims=True))
            factor = jnp.exp2(top - new_top)
            weights = jnp.exp2(scores - new_top)
            total = total * factor + jnp.sum(weights, axis=0, keepdims=True)
            summed = summed * factor + jnp.dot(
                values[block], weights.astype(jnp.bfloat16), preferred_element_type=jnp.float32
            )
            return new_top, total, summed

        lanes = GROUP * BLOCK
        top, total, summed = lax.fori_loop(
            0,
            last - low_ref[chunk] + 1,
            advance,
            (
                jnp.full((1, lanes), masked_score, jnp.float32),
                jnp.zeros((1, lanes), jnp.float32),
                jnp.zeros((HEAD_DIM, lanes), jnp.float32),
            ),
        )
        attended = summed / total
        norm = top + jnp.log2(total)
        spot = pl.ds(chunk * BLOCK, BLOCK)
        for head in range(GROUP):
            out_ref[head, :, spot] = attended[:, head * BLOCK : (head + 1) * BLOCK]
            norm_ref[head, :, spot] = norm[:, head * BLOCK : (head + 1) * BLOCK]


def gradient_kernel(low_ref, starts_ref, query_ref, grad_ref, out_ref, norm_ref, *refs):
    count = len(refs) - 8
    member = low_ref[TEAM]
    pieces = refs[:count]
    query_grad, own_grad, back_grad, keys, keys_t, values, key_sum, value_sum = refs[count:]
    per_piece = pieces[0].shape[-1] // BLOCK
    for back, piece in enumerate(pieces):
        for part in range(per_piece):
            block = (count - 1 - back) * per_piece + (relative(part) ^ member)
            spot = pl.ds(part * BLOCK, BLOCK)
            keys_t[block] = piece[0, 0, :, spot]
            keys[block] = piece[0, 0, :, spot].T
            values[block] = piece[1, 0, :, spot].T
    key_sum[...] = jnp.zeros_like(key_sum)
    value_sum[...] = jnp.zeros_like(value_sum)
    own_block = (count - 1) * per_piece
    rows_rows = (((1,), (1,)), ((), ()))
    for chunk in range(per_piece):
        queries = chunk_lanes(query_ref, chunk)
        grads = chunk_lanes(grad_ref, chunk)
        norm = chunk_lanes(norm_ref, chunk)
        delta = jnp.sum(
            grads.astype(jnp.float32) * chunk_lanes(out_ref, chunk), axis=0, keepdims=True
        )
        last = own_block + (relative(chunk) ^ member)
        starts, ends = chunk_range(chunk, starts_ref, last)

        def advance(block, summed):
            scores = (
                jnp.dot(keys[block], queries, preferred_element_type=jnp.float32) * log2_scale
            )
            scores = jnp.where(visible_mask(block, starts, ends), scores - norm, masked_score)
            probs = jnp.exp2(scores)
            slopes = jnp.dot(values[block], grads, preferred_element_type=jnp.float32)
            grad_scores = (probs * (slopes - delta)).astype(jnp.bfloat16)
            key_sum[block] += lax.dot_general(
                queries, grad_scores, rows_rows, preferred_element_type=jnp.float32
            )
            value_sum[block] += lax.dot_general(
                grads, probs.astype(jnp.bfloat16), rows_rows, preferred_element_type=jnp.float32
            )
            return summed + jnp.dot(
                keys_t[block], grad_scores, preferred_element_type=jnp.float32
            )

        summed = lax.fori_loop(
            low_ref[chunk],
            last + 1,
            advance,
            jnp.zeros((HEAD_DIM, GROUP * BLOCK), jnp.float32),
        )
        spot = pl.ds(chunk * BLOCK, BLOCK)
        for head in range(GROUP):
            query_grad[head, :, spot] = (
                summed[:, head * BLOCK : (head + 1) * BLOCK] * score_scale
            )
    for back in range(count):
        for part in range(per_piece):
            block = (count - 1 - back) * per_piece + (relative(part) ^ member)
            spot = pl.ds(part * BLOCK, BLOCK)
            key_part = key_sum[block] * score_scale
            value_part = value_sum[block]
            if back == 0:
                own_grad[0, 0, :, spot] = key_part
                own_grad[1, 0, :, spot] = value_part
            else:
                back_grad[back - 1, 0, 0, :, spot] = key_part.astype(jnp.bfloat16)
                back_grad[back - 1, 1, 0, :, spot] = value_part.astype(jnp.bfloat16)


def attention_specs(tokens, pieces, first_head):
    whole = pl.BlockSpec((1, tokens), lambda head: (0, 0))
    low = pl.BlockSpec(memory_space=pltpu.SMEM)
    heads = pl.BlockSpec(
        (GROUP, HEAD_DIM, tokens), lambda head: (first_head + head, 0, 0)
    )
    norm = pl.BlockSpec((GROUP, 1, tokens), lambda head: (first_head + head, 0, 0))
    kv = pl.BlockSpec((2, 1, HEAD_DIM, tokens), lambda head: (0, first_head + head, 0, 0))
    return low, whole, heads, norm, [kv] * len(pieces)


def attend(low, starts, queries, pieces, first_head, count):
    tokens = queries.shape[-1]
    blocks = len(pieces) * tokens // BLOCK
    low_spec, whole, heads, norm, kv = attention_specs(tokens, pieces, first_head)
    return pl.pallas_call(
        attend_kernel,
        grid=(count,),
        in_specs=[low_spec, whole, heads] + kv,
        out_specs=[
            pl.BlockSpec((GROUP, HEAD_DIM, tokens), lambda head: (head, 0, 0)),
            pl.BlockSpec((GROUP, 1, tokens), lambda head: (head, 0, 0)),
        ],
        out_shape=[
            jax.ShapeDtypeStruct((count * GROUP, HEAD_DIM, tokens), jnp.float32),
            jax.ShapeDtypeStruct((count * GROUP, 1, tokens), jnp.float32),
        ],
        scratch_shapes=[
            pltpu.VMEM((blocks, BLOCK, HEAD_DIM), jnp.bfloat16),
            pltpu.VMEM((blocks, HEAD_DIM, BLOCK), jnp.bfloat16),
        ],
        compiler_params=pltpu.CompilerParams(vmem_limit_bytes=kernel_vmem),
        cost_estimate=small_cost,
    )(low, starts, queries, *pieces)


def attend_back(low, starts, queries, grads, attended, norm, pieces, first_head, count):
    tokens = queries.shape[-1]
    blocks = len(pieces) * tokens // BLOCK
    low_spec, whole, heads, norm_spec, kv = attention_specs(tokens, pieces, first_head)
    back = len(pieces) - 1
    return pl.pallas_call(
        gradient_kernel,
        grid=(count,),
        in_specs=[low_spec, whole, heads, heads, heads, norm_spec] + kv,
        out_specs=[
            pl.BlockSpec((GROUP, HEAD_DIM, tokens), lambda head: (head, 0, 0)),
            pl.BlockSpec((2, 1, HEAD_DIM, tokens), lambda head: (0, head, 0, 0)),
            pl.BlockSpec((back, 2, 1, HEAD_DIM, tokens), lambda head: (0, 0, head, 0, 0)),
        ],
        out_shape=[
            jax.ShapeDtypeStruct((count * GROUP, HEAD_DIM, tokens), jnp.float32),
            jax.ShapeDtypeStruct((2, count, HEAD_DIM, tokens), jnp.float32),
            jax.ShapeDtypeStruct((back, 2, count, HEAD_DIM, tokens), jnp.bfloat16),
        ],
        scratch_shapes=[
            pltpu.VMEM((blocks, BLOCK, HEAD_DIM), jnp.bfloat16),
            pltpu.VMEM((blocks, HEAD_DIM, BLOCK), jnp.bfloat16),
            pltpu.VMEM((blocks, BLOCK, HEAD_DIM), jnp.bfloat16),
            pltpu.VMEM((blocks, HEAD_DIM, BLOCK), jnp.float32),
            pltpu.VMEM((blocks, HEAD_DIM, BLOCK), jnp.float32),
        ],
        compiler_params=pltpu.CompilerParams(vmem_limit_bytes=kernel_vmem),
        cost_estimate=small_cost,
    )(low, starts, queries, grads, attended, norm, *pieces)

class Order:
    def __init__(self, token):
        self.token = token

    def step(self, *values):
        self.token, tied = lax.optimization_barrier((self.token, values))
        return tied[0] if len(tied) == 1 else tied


class Grid:
    def __init__(self):
        self.count = lax.axis_size("dev")
        self.teams = self.count // TEAM
        index = lax.axis_index("dev")
        self.member = index % TEAM
        self.team = index // TEAM

    def places(self):
        return jnp.stack([self.team, self.member]).astype(jnp.int32)

    def turn(self, value, bits):
        return lax.ppermute(value, "dev", [(d, d ^ bits) for d in range(self.count)])

    def shift(self, value, steps, around=True):
        pairs = []
        for device in range(self.count):
            target = device + steps * TEAM
            if around or 0 <= target < self.count:
                pairs.append((device, target % self.count))
        return lax.ppermute(value, "dev", pairs)

    def spread(self, value):
        return [value] + [self.shift(value, steps) for steps in range(1, self.teams)]

    def both_ways(self, ahead, behind):
        return self.shift(ahead, 1, False), self.shift(behind, -1, False)

    def gather_team(self, blocks):
        return list(blocks) + [self.turn(block, 1) for block in blocks]

    def chips(self, block):
        return [block] + [self.turn(block, 2 * chip) for chip in range(1, 4)]

    def to_members(self, value):
        pairs = [
            (owner, owner % self.teams * TEAM + owner // self.teams)
            for owner in range(self.count)
        ]
        return lax.ppermute(value, "dev", pairs)

    def to_owners(self, value):
        pairs = [
            (owner % self.teams * TEAM + owner // self.teams, owner)
            for owner in range(self.count)
        ]
        return lax.ppermute(value, "dev", pairs)

    def send_chips(self, blocks):
        return [self.turn(block, 2 * chip) for chip, block in enumerate(blocks, 1)]


def call(kernel, grid, in_specs, out_specs, out_shape, scratch=(), prefetch=0):
    return pl.pallas_call(
        kernel,
        out_shape=out_shape,
        grid_spec=pltpu.PrefetchScalarGridSpec(
            num_scalar_prefetch=prefetch,
            grid=grid,
            in_specs=in_specs,
            out_specs=out_specs,
            scratch_shapes=list(scratch),
        ),
        compiler_params=pltpu.CompilerParams(vmem_limit_bytes=kernel_vmem),
        cost_estimate=small_cost,
    )


def fixed(array):
    return pl.BlockSpec(array.shape, lambda *unused: (0,) * array.ndim)


def lanes_at(rows, step_width):
    return pl.BlockSpec((rows, step_width), lambda p, *unused: (0, p))


def rows_at(step_rows, width):
    return pl.BlockSpec((step_rows, width), lambda p, *unused: (p, 0))


def kept_given(rows, width, axis):
    def index(at):
        return (0, at) if axis else (at, 0)

    specs = [
        pl.BlockSpec((rows, width), lambda p, *unused: index(jnp.minimum(p, 3))),
        pl.BlockSpec((rows, width), lambda p, *unused: index(jnp.maximum(p - 4, 0))),
    ]
    shape = (rows, 4 * width) if axis else (4 * rows, width)
    shapes = [
        jax.ShapeDtypeStruct(shape, jnp.float32),
        jax.ShapeDtypeStruct(shape, jnp.bfloat16),
    ]
    return specs, shapes


def keep_or_give(position, keep_ref, give_ref, value):
    @pl.when(position < 4)
    def keep():
        keep_ref[...] = value

    @pl.when(position >= 4)
    def give():
        give_ref[...] = value.astype(give_ref.dtype)


def pick(position, refs, target):
    for number in range(TEAM):

        @pl.when(position == number)
        def move():
            if len(refs) == TEAM:
                target[...] = refs[number][...]
            else:
                target[...] = refs[number // 4][number % 4]


def dot_rows(left, right):
    return lax.dot_general(
        left, right, (((1,), (1,)), ((), ())), preferred_element_type=jnp.float32
    )


def dot(left, right):
    return jnp.dot(left, right, preferred_element_type=jnp.float32)


def place_rows(grid, blocks, start, stop):
    count = len(blocks)
    positions, rows = blocks[0].shape[:2]
    width = stop - start

    def kernel(places_ref, *refs):
        target = refs[-1]
        for number, ref in enumerate(refs[:-1]):

            @pl.when(pl.program_id(0) == number)
            def move():
                for position in range(positions):
                    at = relative(position) ^ places_ref[1] if positions > 1 else 0
                    target[0, pl.ds(at, 1)] = ref[position : position + 1, :, start:stop]

    def target_map(step, places_ref):
        return ((places_ref[0] + count - step) % count, 0, 0, 0)

    return call(
        kernel,
        (count,),
        [fixed(block) for block in blocks],
        pl.BlockSpec((1, positions, rows, width), target_map),
        jax.ShapeDtypeStruct((count, positions, rows, width), blocks[0].dtype),
        prefetch=1,
    )(grid.places(), *blocks)


def place_mixer(grid, own, hops, units, unit_rows):
    count = grid.teams
    positions, rows, wide = own.shape
    third = wide - 2 * units
    sources = [own] + [block for hop in hops for block in hop]

    def kernel(places_ref, *refs):
        mixer_ref, down_ref = refs[-2:]
        team = places_ref[0]

        def move(ref):
            for position in range(positions):
                at = relative(position) ^ places_ref[1]
                mixer_ref[0, pl.ds(at, 1)] = ref[position : position + 1, :, : 2 * units]
                row = position * rows
                while row < (position + 1) * rows:
                    part = row // unit_rows
                    stop = min((part + 1) * unit_rows, (position + 1) * rows)
                    down_ref[
                        0,
                        row - part * unit_rows : stop - part * unit_rows,
                        part * third : (part + 1) * third,
                    ] = ref[position, row - position * rows : stop - position * rows, 2 * units :]
                    row = stop

        for steps in range(count):
            here = pl.program_id(0) == steps
            if steps == 0:
                pl.when(here)(lambda: move(refs[0]))
            else:
                ahead, behind = refs[2 * steps - 1], refs[2 * (count - steps)]
                pl.when(here & (team >= steps))(lambda ahead=ahead: move(ahead))
                pl.when(here & (team < steps))(lambda behind=behind: move(behind))

    def target_map(step, places_ref):
        return (places_ref[0] + count - step) % count

    return call(
        kernel,
        (count,),
        [fixed(source) for source in sources],
        [
            pl.BlockSpec(
                (1, positions, rows, 2 * units), lambda s, p: (target_map(s, p), 0, 0, 0)
            ),
            pl.BlockSpec((1, unit_rows, 3 * third), lambda s, p: (target_map(s, p), 0, 0)),
        ],
        [
            jax.ShapeDtypeStruct((count, positions, rows, 2 * units), own.dtype),
            jax.ShapeDtypeStruct((count, unit_rows, 3 * third), own.dtype),
        ],
        prefetch=1,
    )(grid.places(), *sources)


def project(inputs_t, weights, cosine, sine_table):
    width, own = inputs_t[0].shape
    tokens = TEAM * own
    half = HEAD_DIM // 2

    def kernel(weights_ref, cosine_ref, sine_ref, *refs):
        sources = refs[:TEAM]
        normed_ref, query_ref, kv_ref, chosen, turned = refs[TEAM:]
        position = pl.program_id(0)

        @pl.when(position == 0)
        def prepare():
            turned[...] = weights_ref[:, :LINED].T

        pick(position, sources, chosen)
        values = chosen[...].astype(jnp.float32)
        scale = lax.rsqrt(jnp.mean(values * values, axis=0, keepdims=True) + eps_norm)
        gain = weights_ref[:, LINED : LINED + 1].astype(jnp.float32)
        normed = (values * scale * gain).astype(jnp.bfloat16)
        normed_ref[...] = normed
        lined = dot(turned[...], normed)
        cosines, sines = cosine_ref[...], sine_ref[...]

        def rotated(head):
            block = lined[head * HEAD_DIM : (head + 1) * HEAD_DIM]
            shifted = jnp.concatenate([-block[half:], block[:half]], axis=0)
            return (block * cosines + shifted * sines).astype(jnp.bfloat16)

        for head in range(OWN_HEADS):
            query_ref[head] = rotated(head)
        for head in range(OWN_KV):
            kv_ref[0, head] = rotated(OWN_HEADS + head)
            start = Q_WIDTH + KV_WIDTH + head * HEAD_DIM
            kv_ref[1, head] = lined[start : start + HEAD_DIM].astype(jnp.bfloat16)

    return call(
        kernel,
        (TEAM,),
        [fixed(weights), lanes_at(HEAD_DIM, own), lanes_at(HEAD_DIM, own)]
        + [fixed(block) for block in inputs_t],
        [
            lanes_at(width, own),
            pl.BlockSpec((OWN_HEADS, HEAD_DIM, own), lambda p: (0, 0, p)),
            pl.BlockSpec((2, OWN_KV, HEAD_DIM, own), lambda p: (0, 0, 0, p)),
        ],
        [
            jax.ShapeDtypeStruct((width, tokens), jnp.bfloat16),
            jax.ShapeDtypeStruct((OWN_HEADS, HEAD_DIM, tokens), jnp.bfloat16),
            jax.ShapeDtypeStruct((2, OWN_KV, HEAD_DIM, tokens), jnp.bfloat16),
        ],
        [
            pltpu.VMEM((width, own), jnp.bfloat16),
            pltpu.VMEM((LINED, width), jnp.bfloat16),
        ],
    )(weights, cosine, sine_table, *inputs_t)


def project_out(attended, out_rows):
    tokens = attended.shape[-1]
    own = tokens // TEAM
    width = out_rows.shape[1]
    specs, shapes = kept_given(width, own, 1)

    def kernel(attended_ref, rows_ref, keep_ref, give_ref, turned):
        position = pl.program_id(0)

        @pl.when(position == 0)
        def prepare():
            turned[...] = rows_ref[...].T

        block = attended_ref[...].reshape(Q_WIDTH, own).astype(jnp.bfloat16)
        keep_or_give(position, keep_ref, give_ref, dot(turned[...], block))

    return call(
        kernel,
        (TEAM,),
        [pl.BlockSpec((OWN_HEADS, HEAD_DIM, own), lambda p: (0, 0, p)), fixed(out_rows)],
        specs,
        shapes,
        [pltpu.VMEM((width, Q_WIDTH), jnp.bfloat16)],
    )(attended, out_rows)


def mixer(chip, normed, cotangent, weights, down):
    width, own = normed[0].shape
    units = down.shape[0]

    def kernel(first_ref, second_ref, wanted_a, wanted_b, weights_ref, down_ref, *refs):
        hidden_ref, grad_ref, keep_ref, give_ref, turned, wanted = refs
        step = pl.program_id(0)

        @pl.when(step == 0)
        def first():
            turned[...] = first_ref[...].T
            wanted[...] = wanted_a[0]

        @pl.when(step == 1)
        def second():
            turned[...] = second_ref[...].T
            wanted[...] = wanted_b[0]

        gate = dot(turned[...], weights_ref[:, :units])
        up = dot(turned[...], weights_ref[:, units:])
        logistic = 1.0 / (1.0 + jnp.exp(-gate))
        silu = gate * logistic
        hidden_ref[...] = (silu * up).astype(jnp.bfloat16)
        grad_hidden = dot_rows(wanted[...], down_ref[...])
        grad_ref[:, :units] = (
            grad_hidden * up * (logistic * (1.0 + gate * (1.0 - logistic)))
        ).astype(jnp.bfloat16)
        grad_ref[:, units:] = (grad_hidden * silu).astype(jnp.bfloat16)
        term = dot_rows(weights_ref[...], grad_ref[...])

        @pl.when(step == 0)
        def keep():
            keep_ref[...] = term

        @pl.when(step == 1)
        def give():
            give_ref[...] = term.astype(jnp.bfloat16)

    block = pl.BlockSpec((1, own, width), lambda p: (chip, 0, 0))
    whole = pl.BlockSpec((width, own), lambda p: (0, 0))
    return call(
        kernel,
        (2,),
        [fixed(normed[0]), fixed(normed[1]), block, block, fixed(weights), fixed(down)],
        [rows_at(own, units), rows_at(own, 2 * units), whole, whole],
        [
            jax.ShapeDtypeStruct((2 * own, units), jnp.bfloat16),
            jax.ShapeDtypeStruct((2 * own, 2 * units), jnp.bfloat16),
            jax.ShapeDtypeStruct((width, own), jnp.float32),
            jax.ShapeDtypeStruct((width, own), jnp.bfloat16),
        ],
        [pltpu.VMEM((own, width), jnp.bfloat16), pltpu.VMEM((own, width), jnp.bfloat16)],
    )(normed[0], normed[1], cotangent[0], cotangent[1], weights, down)


def add_block(keep, arrived):
    def kernel(keep_ref, arrived_ref, out_ref):
        out_ref[...] = (keep_ref[...] + arrived_ref[...].astype(jnp.float32)).astype(jnp.bfloat16)

    rows = keep.shape[0] // 2
    part = rows_at(rows, keep.shape[1])
    return call(
        kernel, (2,), [part, part], part, jax.ShapeDtypeStruct(keep.shape, jnp.bfloat16)
    )(keep, arrived)


def pair_rows(position, refs, target):
    own = target.shape[0]
    for number in range(TEAM):

        @pl.when(position == number)
        def move():
            start = number // 4 * own
            target[...] = refs[number % 4][start : start + own]


def mixer_output(hidden, down):
    own, units = hidden[0].shape[0] // 2, hidden[0].shape[1]
    specs, shapes = kept_given(own, down.shape[1], 0)

    def kernel(down_ref, *refs):
        keep_ref, give_ref, chosen = refs[4:]
        pair_rows(pl.program_id(0), refs[:4], chosen)
        keep_or_give(pl.program_id(0), keep_ref, give_ref, dot(chosen[...], down_ref[...]))

    return call(
        kernel,
        (TEAM,),
        [fixed(down)] + [fixed(block) for block in hidden],
        specs,
        shapes,
        [pltpu.VMEM((own, units), jnp.bfloat16)],
    )(down, *hidden)


def write_teams(places_ref, total, out_ref, teams):
    rows = total.shape[0] // teams
    for team in range(teams):
        steps = (team + teams - places_ref[0]) % teams
        block = total[team * rows : (team + 1) * rows, :].astype(out_ref.dtype)
        out_ref[pl.ds(steps, 1)] = block[None]


def token_product(grid, lefts, rights):
    rows, own = lefts[0].shape
    width = rights[0].shape[1]
    teams = grid.teams

    def kernel(places_ref, *refs):
        left_refs, right_refs = refs[:TEAM], refs[TEAM : TEAM + 4]
        out_ref, total, chosen = refs[TEAM + 4 :]
        position = pl.program_id(0)
        pair_rows(position, right_refs, chosen)

        def add(value):
            @pl.when(position == 0)
            def first():
                total[...] = value

            @pl.when(position > 0)
            def later():
                total[...] += value

        for number, source in enumerate(left_refs):

            @pl.when(position == number)
            def block():
                add(dot(source[...], chosen[...]))

        @pl.when(position == TEAM - 1)
        def last():
            write_teams(places_ref, total, out_ref, teams)

    return call(
        kernel,
        (TEAM,),
        [fixed(block) for block in list(lefts) + list(rights)],
        pl.BlockSpec((teams, rows // teams, width), lambda p, *unused: (0, 0, 0)),
        jax.ShapeDtypeStruct((teams, rows // teams, width), jnp.bfloat16),
        [pltpu.VMEM((rows, width), jnp.float32), pltpu.VMEM((own, width), jnp.bfloat16)],
        prefetch=1,
    )(grid.places(), *lefts, *rights)


def down_product(grid, hidden, cotangent):
    units = hidden[0].shape[1]
    own, width = cotangent[0].shape[1:]
    teams = grid.teams

    def kernel(places_ref, *refs):
        hidden_refs, sources, (out_ref, total, wanted, chosen) = refs[:4], refs[4:6], refs[6:]
        position = pl.program_id(0)
        pick(position, sources, wanted)
        pair_rows(position, hidden_refs, chosen)
        value = dot(chosen[...].T, wanted[...])

        @pl.when(position == 0)
        def first():
            total[...] = value

        @pl.when(position > 0)
        def later():
            total[...] += value

        @pl.when(position == TEAM - 1)
        def last():
            write_teams(places_ref, total, out_ref, teams)

    return call(
        kernel,
        (TEAM,),
        [fixed(block) for block in list(hidden) + list(cotangent)],
        pl.BlockSpec((teams, units // teams, width), lambda p, *unused: (0, 0, 0)),
        jax.ShapeDtypeStruct((teams, units // teams, width), jnp.bfloat16),
        [
            pltpu.VMEM((units, width), jnp.float32),
            pltpu.VMEM((own, width), jnp.bfloat16),
            pltpu.VMEM((own, units), jnp.bfloat16),
        ],
        prefetch=1,
    )(grid.places(), *hidden, *cotangent)


def project_out_back(grid, grads, out_rows, attended):
    teams = grid.teams
    tokens = attended.shape[-1]
    own = tokens // TEAM
    width = out_rows.shape[1]

    def kernel(places_ref, rows_ref, attended_ref, *refs):
        sources, (grad_ref, out_ref, chosen, total) = refs[:TEAM], refs[TEAM:]
        position = pl.program_id(0)
        pick(position, sources, chosen)
        grad_ref[...] = (
            dot(rows_ref[...], chosen[...])
            .astype(jnp.bfloat16)
            .reshape(OWN_HEADS, HEAD_DIM, own)
        )
        block = attended_ref[...].reshape(Q_WIDTH, own).astype(jnp.bfloat16)
        value = dot_rows(block, chosen[...])

        @pl.when(position == 0)
        def first():
            total[...] = value

        @pl.when(position > 0)
        def later():
            total[...] += value

        @pl.when(position == TEAM - 1)
        def last():
            write_teams(places_ref, total, out_ref, teams)

    heads = pl.BlockSpec((OWN_HEADS, HEAD_DIM, own), lambda p, *unused: (0, 0, p))
    shape = (teams, Q_WIDTH // teams, width)
    return call(
        kernel,
        (TEAM,),
        [fixed(out_rows), heads] + [fixed(block) for block in grads],
        [heads, pl.BlockSpec(shape, lambda p, *unused: (0, 0, 0))],
        [
            jax.ShapeDtypeStruct((OWN_HEADS, HEAD_DIM, tokens), jnp.bfloat16),
            jax.ShapeDtypeStruct(shape, jnp.bfloat16),
        ],
        [pltpu.VMEM((width, own), jnp.bfloat16), pltpu.VMEM((Q_WIDTH, width), jnp.float32)],
        prefetch=1,
    )(grid.places(), out_rows, attended, *grads)


def project_back(grid, normed, query_rot, own_grads, returned, cosine, sine_table, weights):
    width, tokens = normed.shape
    own = tokens // TEAM
    half = HEAD_DIM // 2
    teams = grid.teams
    specs, shapes = kept_given(width, own, 1)

    def kernel(places_ref, normed_ref, query_ref, cosine_ref, sine_ref, weights_ref, *refs):
        kv_refs = refs[: 1 + len(returned)]
        keep_ref, give_ref, out_ref, total, grad_ref = refs[1 + len(returned) :]
        position = pl.program_id(0)
        cosines, sines = cosine_ref[...], sine_ref[...]

        def unrotated(block):
            scaled = block * sines
            shifted = jnp.concatenate([scaled[half:], -scaled[:half]], axis=0)
            return (block * cosines + shifted).astype(jnp.bfloat16)

        for head in range(OWN_HEADS):
            grad_ref[head * HEAD_DIM : (head + 1) * HEAD_DIM] = unrotated(query_ref[head])
        kv = kv_refs[0][...]
        for ref in kv_refs[1:]:
            kv = kv + ref[...].astype(jnp.float32)
        for head in range(OWN_KV):
            start = Q_WIDTH + head * HEAD_DIM
            grad_ref[start : start + HEAD_DIM] = unrotated(kv[0, head])
            start = start + KV_WIDTH
            grad_ref[start : start + HEAD_DIM] = kv[1, head].astype(jnp.bfloat16)
        grad = grad_ref[...]
        keep_or_give(position, keep_ref, give_ref, dot(weights_ref[:, :LINED], grad))
        value = dot_rows(normed_ref[...], grad)

        @pl.when(position == 0)
        def first():
            total[...] = value

        @pl.when(position > 0)
        def later():
            total[...] += value

        @pl.when(position == TEAM - 1)
        def last():
            write_teams(places_ref, total, out_ref, teams)

    heads = pl.BlockSpec((OWN_HEADS, HEAD_DIM, own), lambda p, *unused: (0, 0, p))
    kv_heads = pl.BlockSpec((2, OWN_KV, HEAD_DIM, own), lambda p, *unused: (0, 0, 0, p))
    return call(
        kernel,
        (TEAM,),
        [
            lanes_at(width, own),
            heads,
            lanes_at(HEAD_DIM, own),
            lanes_at(HEAD_DIM, own),
            fixed(weights),
        ]
        + [kv_heads] * (1 + len(returned)),
        specs + [pl.BlockSpec((teams, width // teams, LINED), lambda p, *unused: (0, 0, 0))],
        shapes + [jax.ShapeDtypeStruct((teams, width // teams, LINED), jnp.bfloat16)],
        [pltpu.VMEM((width, LINED), jnp.float32), pltpu.VMEM((LINED, own), jnp.bfloat16)],
        prefetch=1,
    )(grid.places(), normed, query_rot, cosine, sine_table, weights, own_grads, *returned)


def combine(keep, arrived, axis):
    size = keep.shape[axis] // 4
    shape = (keep.shape[0], size) if axis else (size, keep.shape[1])

    def kernel(keep_ref, arrived_ref, own_ref, *block_refs):
        position = pl.program_id(0)
        total = keep_ref[...] + arrived_ref[...].astype(jnp.float32)

        @pl.when(position == 0)
        def own():
            own_ref[...] = total

        for number, ref in enumerate(block_refs, 1):

            @pl.when(position == number)
            def other():
                ref[...] = total.astype(jnp.bfloat16)

    part = pl.BlockSpec(shape, (lambda p: (0, p)) if axis else (lambda p: (p, 0)))
    whole = pl.BlockSpec(shape, lambda p: (0, 0))
    own, *blocks = call(
        kernel,
        (4,),
        [part, part],
        [whole] * 4,
        [jax.ShapeDtypeStruct(shape, jnp.float32)]
        + [jax.ShapeDtypeStruct(shape, jnp.bfloat16)] * 3,
    )(keep, arrived)
    return own, blocks


def summed(refs):
    total = refs[0][...]
    for ref in refs[1:]:
        total = total + ref[...].astype(jnp.float32)
    return total


def finish(kernel, arrays, shapes):
    return call(
        kernel,
        (1,),
        [fixed(array) for array in arrays],
        [pl.BlockSpec(shape.shape, lambda p: (0, 0)) for shape in shapes],
        shapes,
    )(*arrays)


def finish_middle(terms, inputs_t, gain):
    def kernel(*refs):
        inputs_ref, gain_ref, middle_ref, normed_ref = refs[len(terms) :]
        middle = inputs_ref[...].astype(jnp.float32) + summed(refs[: len(terms)])
        middle_ref[...] = middle
        scale = lax.rsqrt(jnp.mean(middle * middle, axis=0, keepdims=True) + eps_norm)
        normed_ref[...] = (middle * scale * gain_ref[...]).astype(jnp.bfloat16)

    shape = inputs_t.shape
    return finish(
        kernel,
        list(terms) + [inputs_t, gain],
        [jax.ShapeDtypeStruct(shape, jnp.float32), jax.ShapeDtypeStruct(shape, jnp.bfloat16)],
    )


def norm_back(values, gain, grad):
    inverse = lax.rsqrt(jnp.mean(values * values, axis=0, keepdims=True) + eps_norm)
    normal = values * inverse
    scaled = grad * gain
    inner = jnp.mean(scaled * normal, axis=0, keepdims=True)
    return inverse * (scaled - normal * inner), jnp.sum(grad * normal, axis=1, keepdims=True)


def finish_second(terms, middle, cotangent, gain):
    def kernel(*refs):
        middle_ref, cotangent_ref, gain_ref, grad_ref, attn_ref, gain_out = refs[len(terms) :]
        norm_grad, gain_part = norm_back(
            middle_ref[...], gain_ref[...], summed(refs[: len(terms)])
        )
        grad = cotangent_ref[...].T.astype(jnp.float32) + norm_grad
        grad_ref[...] = grad
        attn_ref[...] = grad.astype(jnp.bfloat16)
        gain_out[...] = gain_part

    shape = middle.shape
    return finish(
        kernel,
        list(terms) + [middle, cotangent, gain],
        [
            jax.ShapeDtypeStruct(shape, jnp.float32),
            jax.ShapeDtypeStruct(shape, jnp.bfloat16),
            jax.ShapeDtypeStruct((shape[0], 1), jnp.float32),
        ],
    )


def finish_first(terms, inputs_t, grad_middle, gain):
    def kernel(*refs):
        inputs_ref, grad_ref, gain_ref, out_ref, gain_out = refs[len(terms) :]
        norm_grad, gain_part = norm_back(
            inputs_ref[...].astype(jnp.float32), gain_ref[...], summed(refs[: len(terms)])
        )
        out_ref[...] = (grad_ref[...] + norm_grad).T
        gain_out[...] = gain_part

    width, own = inputs_t.shape
    return finish(
        kernel,
        list(terms) + [inputs_t, grad_middle, gain],
        [
            jax.ShapeDtypeStruct((own, width), jnp.float32),
            jax.ShapeDtypeStruct((width, 1), jnp.float32),
        ],
    )


def finish_output(terms, middle):
    def kernel(*refs):
        middle_ref, out_ref = refs[len(terms) :]
        out_ref[...] = (middle_ref[...].T + summed(refs[: len(terms)])).astype(jnp.bfloat16)

    return finish(
        kernel, list(terms) + [middle], [jax.ShapeDtypeStruct(terms[0].shape, jnp.bfloat16)]
    )[0]


def sum_teams(product, parts, kind):
    def kernel(own_ref, *refs):
        total = own_ref[0].astype(jnp.float32)
        for ref in refs[:-1]:
            total = total + ref[...].astype(jnp.float32)
        refs[-1][...] = total.astype(kind)

    shape = product.shape[1:]
    return call(
        kernel,
        (1,),
        [pl.BlockSpec((1,) + shape, lambda p: (0, 0, 0))] + [fixed(part) for part in parts],
        pl.BlockSpec(shape, lambda p: (0, 0)),
        jax.ShapeDtypeStruct(shape, kind),
    )(product, *parts)


def rope_tables(positions):
    half_dim = HEAD_DIM // 2
    frequency = rope_base ** (-(jnp.arange(half_dim, dtype=jnp.float32) * 2.0 / HEAD_DIM))
    angles = frequency[:, None] * positions.astype(jnp.float32)[None, :]
    angles = jnp.concatenate([angles, angles], axis=0)
    return (jnp.cos(angles), jnp.sin(angles))


def per_device(
    inputs,
    positions,
    norm_first,
    query_weight,
    key_weight,
    value_weight,
    out_weight,
    norm_second,
    gate_weight,
    up_weight,
    down_weight,
    cotangent,
):
    grid = Grid()
    member, teams = grid.member, grid.teams
    chip, core = member // 2, member % 2
    own, width = inputs.shape
    tokens = own * TEAM
    rows = query_weight.shape[0]
    unit_rows = down_weight.shape[0]
    units = unit_rows * teams
    longest = own * grid.count // 4
    steps_back = min((longest - 2) // tokens + 1, teams - 1)
    bf16, f32 = jnp.bfloat16, jnp.float32
    order = Order(jnp.zeros((8, 128), jnp.int32))

    def dynamic(array, index, axis=0):
        return lax.dynamic_index_in_dim(array, index, axis, keepdims=False)

    def by_member(weight):
        return jnp.transpose(weight.reshape(rows, TEAM, -1), (1, 0, 2))

    def units_by_member(weight):
        blocks = jnp.transpose(weight.reshape(rows, teams, TEAM, unit_rows), (2, 0, 1, 3))
        return blocks.reshape(TEAM, rows, units)

    gains = jnp.pad(jnp.stack([norm_first, norm_second], axis=1), ((0, 0), (0, LANES - 2)))
    columns = jnp.concatenate(
        [
            by_member(query_weight),
            by_member(key_weight),
            by_member(value_weight),
            jnp.broadcast_to(gains[None], (TEAM, rows, LANES)),
            units_by_member(gate_weight),
            units_by_member(up_weight),
        ],
        axis=-1,
    )
    attn_wide = LINED + LANES
    columns = columns.reshape(TEAM // 2, 2, rows, attn_wide + 2 * units)
    position_chips = jnp.stack(grid.chips(positions))
    all_positions = jnp.concatenate([position_chips, grid.turn(position_chips, 1)]).reshape(tokens)
    inputs_t = inputs.T
    columns, inputs_t = order.step(columns, inputs_t)
    pairs = [
        dynamic(columns, chip)
        if other == 0
        else grid.turn(dynamic(columns, chip ^ other), 2 * other)
        for other in range(4)
    ]
    inputs_two = [grid.turn(inputs_t, 2), grid.turn(inputs_t, 4)]
    cosine, sine_table = rope_tables(all_positions)
    block_index = steps_back * TEAM + (
        jnp.array([relative(p) for p in range(TEAM)], jnp.int32) ^ member
    )
    token_index = (block_index[:, None] * own + jnp.arange(own, dtype=jnp.int32)).reshape(tokens)
    starts = token_index - all_positions
    low = jnp.concatenate([starts[::own] // BLOCK, member[None]]).astype(jnp.int32)
    starts = starts[None]
    third = width // 3
    down_thirds = jnp.concatenate(
        [down_weight[:, part * third : (part + 1) * third] for part in range(3)], axis=0
    ).reshape(TEAM, rows, third)
    cosine, sine_table, starts, low, down_thirds, pairs, inputs_two, inputs_t = order.step(
        cosine, sine_table, starts, low, down_thirds, pairs, inputs_two, inputs_t
    )
    inputs_three = grid.turn(inputs_t, 6)
    pairs = jnp.stack(pairs)
    pairs_keep, pairs_give = dynamic(pairs, core, 1), dynamic(pairs, 1 - core, 1)
    team_rows = jnp.concatenate([pairs_keep, grid.turn(pairs_give, 1)], axis=0)
    attn_rows, team_rows, out_weight = order.step(
        team_rows[..., :attn_wide], team_rows, out_weight
    )
    attn_z = grid.spread(attn_rows)
    inputs_others = [grid.turn(block, 1) for block in [inputs_t] + inputs_two]
    attn_z, inputs_three = order.step(attn_z, inputs_three)
    inputs_others = inputs_others + [grid.turn(inputs_three, 1)]
    inputs_team = [inputs_t] + inputs_two + [inputs_three] + inputs_others
    out_own = grid.to_members(out_weight)
    attn_w = place_rows(grid, attn_z, 0, attn_wide).reshape(width, attn_wide)
    attn_w, inputs_team, out_own = order.step(attn_w, inputs_team, out_own)

    out_own, cotangent = order.step(out_own, cotangent)
    out_z = grid.spread(out_own)
    cotangent_chips = [cotangent, grid.turn(cotangent, 2), grid.turn(cotangent, 4)]
    normed_first, queries, own_piece = project(inputs_team, attn_w, cosine, sine_table)
    own_piece, out_z, attn_w = order.step(own_piece, out_z, attn_w)
    arrived = [grid.shift(own_piece, step, False) for step in range(1, steps_back + 1)]
    cotangent_chips = order.step(cotangent_chips)
    cotangent_chips = cotangent_chips + [grid.turn(cotangent_chips[0], 6)]
    out_rows = place_rows(grid, [block[None] for block in out_z], 0, width)
    out_rows = out_rows.reshape(Q_WIDTH, width)
    gain_first = attn_w[:, LINED : LINED + 1].astype(f32)
    gain_second = attn_w[:, LINED + 1 : LINED + 2].astype(f32)
    mixer_own = jnp.concatenate([team_rows[..., attn_wide:], down_thirds], axis=-1)
    arrived, gain_first, gain_second, mixer_own, out_rows = order.step(
        arrived, gain_first, gain_second, mixer_own, out_rows
    )

    mixer_hops = [grid.both_ways(mixer_own, mixer_own)]

    def next_hop():
        if len(mixer_hops) < teams - 1:
            mixer_hops.append(grid.both_ways(*mixer_hops[-1]))

    pieces = [own_piece] + arrived
    attended, normalizer = attend(low, starts, queries, pieces, 0, OWN_KV)
    keep, give = project_out(attended, out_rows)
    give, mixer_hops[0], cotangent_chips = order.step(give, mixer_hops[0], cotangent_chips)
    other = grid.turn(give, 1)
    next_hop()
    cotangent_stack = jnp.stack(cotangent_chips)
    other, cotangent_stack = order.step(other, cotangent_stack)
    cotangent_other = grid.turn(cotangent_stack, 1)
    total, blocks = combine(keep, other, 1)
    blocks, cotangent_other = order.step(blocks, cotangent_other)
    cotangent_team = [cotangent_stack, cotangent_other]
    near = [grid.turn(blocks[0], 2), grid.turn(blocks[1], 4)]
    near, far, mixer_hops[-1] = order.step(near, blocks[2], mixer_hops[-1])
    terms = near + [grid.turn(far, 6)]
    next_hop()
    terms = order.step(terms)
    middle, normed_second = finish_middle([total] + terms, inputs_t, gain_second)
    normed_second, mixer_hops[-1] = order.step(normed_second, mixer_hops[-1])
    while len(mixer_hops) < teams - 1:
        next_hop()
        mixer_hops[-1] = order.step(mixer_hops[-1])
    second_chips = [normed_second, grid.turn(normed_second, 2), grid.turn(normed_second, 4)]
    second_other = [grid.turn(normed_second, 1)]
    mixer_w, down_w = place_mixer(grid, mixer_own, mixer_hops, units, unit_rows)
    mixer_w = mixer_w.reshape(width, 2 * units)
    down_w = down_w.reshape(units, width)
    mixer_w, down_w, second_other[0] = order.step(mixer_w, down_w, second_other[0])

    def send_teams(product, first=1, last=teams):
        return [grid.shift(product[steps], steps) for steps in range(first, last)]

    def run_mixer(other_chip):
        hidden_part, grads_part, keep, give = mixer(
            other_chip,
            (second_chips[other_chip], second_other[other_chip]),
            cotangent_team,
            mixer_w,
            down_w,
        )
        return hidden_part, grads_part, keep, order.step(give)

    parts = [run_mixer(0)]
    passed = [grid.turn(parts[0][3], 1)]
    second_chips = order.step(second_chips)
    second_chips = second_chips + [grid.turn(second_chips[0], 6)]
    second_other += order.step([grid.turn(second_chips[1], 1), grid.turn(second_chips[2], 1)])
    parts.append(run_mixer(1))
    passed.append(grid.turn(parts[1][3], 1))
    second_chips[3], passed[0] = order.step(second_chips[3], passed[0])
    second_other.append(grid.turn(second_chips[3], 1))
    parts.append(run_mixer(2))
    passed[1], second_other[3] = order.step(passed[1], second_other[3])
    block = order.step(add_block(parts[1][2], passed[1]))
    terms = [parts[0][2], passed[0], grid.turn(block, 2)]
    passed.append(grid.turn(parts[2][3], 1))
    parts.append(run_mixer(3))
    passed[2] = order.step(passed[2])
    passed.append(grid.turn(parts[3][3], 1))
    block = order.step(add_block(parts[2][2], passed[2]))
    terms.append(grid.turn(block, 4))
    passed[3] = order.step(passed[3])
    hidden, grads = [part[0] for part in parts], [part[1] for part in parts]
    block, grads, hidden = order.step(add_block(parts[3][2], passed[3]), grads, hidden)
    terms.append(grid.turn(block, 6))
    second_team = second_chips + second_other
    early = max(1, teams // 2)
    mixer_part = token_product(grid, second_team, grads)
    mixer_part, hidden = order.step(mixer_part, hidden)
    mixer_parts = send_teams(mixer_part, 1, early + 1)
    down_part = down_product(grid, hidden, cotangent_team)
    terms, down_part = order.step(terms, down_part)
    grad_middle, grad_attn, second_part = finish_second(terms, middle, cotangent, gain_second)
    grad_attn, hidden = order.step(grad_attn, hidden)
    attn_chips = grid.chips(grad_attn)
    out_keep, out_give = mixer_output(hidden, down_w)
    attn_chips, out_give, mixer_parts = order.step(attn_chips, out_give, mixer_parts)
    late_parts = send_teams(mixer_part, early + 1, teams)
    attn_team = order.step(grid.gather_team(attn_chips))

    grad_attended, out_part = project_out_back(grid, attn_team, out_rows, attended)
    grad_attended, down_part, out_give = order.step(grad_attended, down_part, out_give)
    down_parts = send_teams(down_part, 1, early + 1)
    out_other = grid.turn(out_give, 1)
    query_rot, own_grads, back_grads = attend_back(
        low, starts, queries, grad_attended, attended, normalizer, pieces, 0, OWN_KV
    )
    query_rot, own_grads, back_grads, late_parts, out_other = order.step(
        query_rot, own_grads, back_grads, late_parts, out_other
    )
    returned = [
        grid.shift(back_grads[step - 1], -step, False) for step in range(1, steps_back + 1)
    ]
    out_total, out_blocks = combine(out_keep, out_other, 0)
    out_blocks = order.step(out_blocks)
    out_terms = grid.send_chips(out_blocks)
    mixer_total = sum_teams(mixer_part, mixer_parts + late_parts, bf16)
    returned, down_parts, mixer_total = order.step(returned, down_parts, mixer_total)
    down_late = send_teams(down_part, early + 1, teams)
    keep, give, attn_part = project_back(
        grid, normed_first, query_rot, own_grads, returned, cosine, sine_table, attn_w
    )
    attn_part, give, out_terms, down_late = order.step(attn_part, give, out_terms, down_late)
    other = grid.turn(give, 1)
    attn_parts = send_teams(attn_part, 1, early + 1)
    other = order.step(other)
    total, blocks = combine(keep, other, 1)
    blocks, out_part = order.step(blocks, out_part)
    terms = grid.send_chips(blocks)
    outputs = finish_output([out_total] + out_terms, middle)
    down_grad = sum_teams(down_part, down_parts + down_late, f32)
    attn_parts, outputs, down_grad = order.step(attn_parts, outputs, down_grad)
    attn_late = send_teams(attn_part, early + 1, teams)
    out_parts = send_teams(out_part, 1, teams)

    def members_rows(total):
        blocks = total.reshape(TEAM // 2, 2, rows, -1)
        return dynamic(blocks, core, 1), grid.turn(dynamic(blocks, 1 - core, 1), 1)

    def owner_columns(mine, others):
        both = jnp.stack([mine, others])
        first = jnp.where(core == 0, both[0], both[1])
        second = jnp.where(core == 0, both[1], both[0])
        both = jnp.stack([first, second], axis=1)
        found = [
            dynamic(both, chip) if other == 0 else grid.turn(dynamic(both, chip ^ other), 2 * other)
            for other in range(4)
        ]
        return found

    def in_order(found):
        stacked = jnp.stack(found)
        return jnp.stack([dynamic(stacked, chip ^ other) for other in range(4)]).reshape(
            (TEAM,) + found[0].shape[1:]
        )

    mixer_mine, mixer_others = members_rows(mixer_total)
    mixer_mine, mixer_others, terms = order.step(mixer_mine, mixer_others, terms)
    mixer_found = owner_columns(mixer_mine, mixer_others)
    input_grad, first_part = finish_first([total] + terms, inputs_t, grad_middle, gain_first)
    gain_parts = jnp.concatenate([first_part, second_part], axis=1).T
    attn_late, gain_parts, out_parts = order.step(attn_late, gain_parts, out_parts)
    attn_total = sum_teams(attn_part, attn_parts + attn_late, bf16)
    out_own = sum_teams(out_part, out_parts, bf16)
    attn_mine, attn_others = members_rows(attn_total)
    gain_parts = gain_parts + grid.turn(gain_parts, 1)
    attn_mine, attn_others, gain_parts, out_own = order.step(
        attn_mine, attn_others, gain_parts, out_own
    )
    attn_found = owner_columns(attn_mine, attn_others)
    out_grad = grid.to_owners(out_own).astype(f32)
    gain_parts = gain_parts + grid.turn(gain_parts, 2)
    mixer_found, gain_parts = order.step(mixer_found, gain_parts)
    mixer_columns = in_order(mixer_found)

    def whole_units(blocks):
        blocks = blocks.reshape(TEAM, rows, teams, unit_rows)
        return jnp.transpose(blocks, (1, 2, 0, 3)).reshape(rows, TEAM * units).astype(f32)

    def whole(blocks):
        return jnp.transpose(blocks, (1, 0, 2)).reshape(rows, -1).astype(f32)

    gate_grad = whole_units(mixer_columns[..., :units])
    up_grad = whole_units(mixer_columns[..., units:])
    gain_parts = gain_parts + grid.turn(gain_parts, 4)
    gain_blocks = gain_parts.reshape(2, teams, TEAM, rows)
    gain_sums = dynamic(dynamic(gain_blocks, grid.team, 1), member, 1)
    for steps in range(1, teams):
        block = dynamic(dynamic(gain_blocks, (grid.team + steps) % teams, 1), member, 1)
        gain_sums = gain_sums + grid.shift(block, steps)
    attn_found, gain_sums = order.step(attn_found, gain_sums)
    attn_columns = in_order(attn_found)
    gain_sums = gain_sums + order.token[0, 0].astype(f32)
    return (
        outputs,
        input_grad,
        gain_sums[0],
        whole(attn_columns[..., :Q_WIDTH]),
        whole(attn_columns[..., Q_WIDTH : Q_WIDTH + KV_WIDTH]),
        whole(attn_columns[..., Q_WIDTH + KV_WIDTH :]),
        out_grad,
        gain_sums[1],
        gate_grad,
        up_grad,
        down_grad,
    )


def solution(mesh):
    matrix, vector = P("dev", None), P("dev")
    in_specs = (matrix, vector, vector) + (matrix,) * 4 + (vector,) + (matrix,) * 4
    out_specs = (matrix, matrix, vector) + (matrix,) * 4 + (vector,) + (matrix,) * 3
    return jax.shard_map(
        per_device, mesh=mesh, in_specs=in_specs, out_specs=out_specs, check_vma=False
    )
```

```python
import math

import jax
import jax.numpy as jnp
from jax import lax
from jax.experimental import pallas as pl
from jax.experimental.pallas import tpu as pltpu
from jax.sharding import PartitionSpec as P

HEADS = 16
KV_HEADS = 8
HEAD_DIM = 96
TEAM = 8

eps_norm = 1e-05
rope_base = 100000.0
masked_score = -1e30

OWN_HEADS = HEADS // TEAM
OWN_KV = KV_HEADS // TEAM
GROUP = HEADS // KV_HEADS
BLOCK = 256
LANES = 128
score_scale = 1.0 / math.sqrt(HEAD_DIM)
log2_scale = score_scale / math.log(2.0)
kernel_vmem = 56 * 1024 * 1024
small_cost = pl.CostEstimate(flops=1000, bytes_accessed=1000, transcendentals=0)

Q_WIDTH = OWN_HEADS * HEAD_DIM
KV_WIDTH = OWN_KV * HEAD_DIM
LINED = Q_WIDTH + 2 * KV_WIDTH


def relative(position):
    return 2 * (position % 4) + position // 4


def visible_mask(block, starts, ends):
    key = block * BLOCK + lax.broadcasted_iota(jnp.int32, (BLOCK, 1), 0)
    return (key >= starts) & (key <= ends)


def chunk_lanes(ref, chunk):
    spot = pl.ds(chunk * BLOCK, BLOCK)
    return jnp.concatenate([ref[head, :, spot] for head in range(GROUP)], axis=1)


def chunk_range(chunk, starts_ref, last):
    starts = starts_ref[:, pl.ds(chunk * BLOCK, BLOCK)]
    ends = last * BLOCK + lax.broadcasted_iota(jnp.int32, (1, BLOCK), 1)
    return (
        jnp.concatenate([starts] * GROUP, axis=1),
        jnp.concatenate([ends] * GROUP, axis=1),
    )


def attend_kernel(low_ref, starts_ref, query_ref, *refs):
    count = len(refs) - 4
    member = low_ref[TEAM]
    pieces = refs[:count]
    out_ref, norm_ref, keys, values = refs[count:]
    per_piece = pieces[0].shape[-1] // BLOCK
    for back, piece in enumerate(pieces):
        for part in range(per_piece):
            block = (count - 1 - back) * per_piece + (relative(part) ^ member)
            spot = pl.ds(part * BLOCK, BLOCK)
            keys[block] = piece[0, 0, :, spot].T
            values[block] = piece[1, 0, :, spot]
    own_block = (count - 1) * per_piece
    for chunk in range(per_piece):
        queries = chunk_lanes(query_ref, chunk)
        last = own_block + (relative(chunk) ^ member)
        starts, ends = chunk_range(chunk, starts_ref, last)

        def masked(block):
            held = jnp.maximum(block, 0)
            scores = jnp.dot(keys[held], queries, preferred_element_type=jnp.float32) * log2_scale
            return held, jnp.where(visible_mask(block, starts, ends), scores, masked_score)

        def advance(step, running):
            top, total, summed = running
            one, scores = masked(last - 2 * step)
            two, more = masked(last - 2 * step - 1)
            new_top = jnp.maximum(
                top, jnp.max(jnp.maximum(scores, more), axis=0, keepdims=True)
            )
            factor = jnp.exp2(top - new_top)
            weights, others = jnp.exp2(scores - new_top), jnp.exp2(more - new_top)
            total = total * factor + jnp.sum(weights + others, axis=0, keepdims=True)
            summed = summed * factor + (
                jnp.dot(
                    values[one], weights.astype(jnp.bfloat16), preferred_element_type=jnp.float32
                )
                + jnp.dot(
                    values[two], others.astype(jnp.bfloat16), preferred_element_type=jnp.float32
                )
            )
            return new_top, total, summed

        lanes = GROUP * BLOCK
        top, total, summed = lax.fori_loop(
            0,
            (last - low_ref[chunk] + 2) // 2,
            advance,
            (
                jnp.full((1, lanes), masked_score, jnp.float32),
                jnp.zeros((1, lanes), jnp.float32),
                jnp.zeros((HEAD_DIM, lanes), jnp.float32),
            ),
        )
        attended = summed / total
        norm = top + jnp.log2(total)
        spot = pl.ds(chunk * BLOCK, BLOCK)
        for head in range(GROUP):
            out_ref[head, :, spot] = attended[:, head * BLOCK : (head + 1) * BLOCK]
            norm_ref[head, :, spot] = norm[:, head * BLOCK : (head + 1) * BLOCK]


def gradient_kernel(low_ref, starts_ref, query_ref, grad_ref, out_ref, norm_ref, *refs):
    count = len(refs) - 8
    member = low_ref[TEAM]
    pieces = refs[:count]
    query_grad, own_grad, back_grad, keys, keys_t, values, key_sum, value_sum = refs[count:]
    per_piece = pieces[0].shape[-1] // BLOCK
    for back, piece in enumerate(pieces):
        for part in range(per_piece):
            block = (count - 1 - back) * per_piece + (relative(part) ^ member)
            spot = pl.ds(part * BLOCK, BLOCK)
            keys_t[block] = piece[0, 0, :, spot]
            keys[block] = piece[0, 0, :, spot].T
            values[block] = piece[1, 0, :, spot].T
    key_sum[...] = jnp.zeros_like(key_sum)
    value_sum[...] = jnp.zeros_like(value_sum)
    own_block = (count - 1) * per_piece
    rows_rows = (((1,), (1,)), ((), ()))
    for chunk in range(per_piece):
        queries = chunk_lanes(query_ref, chunk)
        grads = chunk_lanes(grad_ref, chunk)
        norm = chunk_lanes(norm_ref, chunk)
        delta = jnp.sum(
            grads.astype(jnp.float32) * chunk_lanes(out_ref, chunk), axis=0, keepdims=True
        )
        last = own_block + (relative(chunk) ^ member)
        starts, ends = chunk_range(chunk, starts_ref, last)

        def part(block):
            held = jnp.minimum(block, last)
            scores = jnp.dot(keys[held], queries, preferred_element_type=jnp.float32) * log2_scale
            scores = jnp.where(visible_mask(block, starts, ends), scores - norm, masked_score)
            probs = jnp.exp2(scores)
            slopes = jnp.dot(values[held], grads, preferred_element_type=jnp.float32)
            grad_scores = (probs * (slopes - delta)).astype(jnp.bfloat16)
            return held, probs.astype(jnp.bfloat16), grad_scores

        def advance(step, summed):
            found = [part(low_ref[chunk] + 2 * step), part(low_ref[chunk] + 2 * step + 1)]
            for held, probs, grad_scores in found:
                key_sum[held] += lax.dot_general(
                    queries, grad_scores, rows_rows, preferred_element_type=jnp.float32
                )
                value_sum[held] += lax.dot_general(
                    grads, probs, rows_rows, preferred_element_type=jnp.float32
                )
                summed = summed + jnp.dot(
                    keys_t[held], grad_scores, preferred_element_type=jnp.float32
                )
            return summed

        summed = lax.fori_loop(
            0,
            (last - low_ref[chunk] + 2) // 2,
            advance,
            jnp.zeros((HEAD_DIM, GROUP * BLOCK), jnp.float32),
        )
        spot = pl.ds(chunk * BLOCK, BLOCK)
        for head in range(GROUP):
            query_grad[head, :, spot] = (
                summed[:, head * BLOCK : (head + 1) * BLOCK] * score_scale
            )
    for back in range(count):
        for part in range(per_piece):
            block = (count - 1 - back) * per_piece + (relative(part) ^ member)
            spot = pl.ds(part * BLOCK, BLOCK)
            key_part = key_sum[block] * score_scale
            value_part = value_sum[block]
            if back == 0:
                own_grad[0, 0, :, spot] = key_part
                own_grad[1, 0, :, spot] = value_part
            else:
                back_grad[back - 1, 0, 0, :, spot] = key_part.astype(jnp.bfloat16)
                back_grad[back - 1, 1, 0, :, spot] = value_part.astype(jnp.bfloat16)


def attention_specs(tokens, pieces, first_head):
    whole = pl.BlockSpec((1, tokens), lambda head: (0, 0))
    low = pl.BlockSpec(memory_space=pltpu.SMEM)
    heads = pl.BlockSpec(
        (GROUP, HEAD_DIM, tokens), lambda head: (first_head + head, 0, 0)
    )
    norm = pl.BlockSpec((GROUP, 1, tokens), lambda head: (first_head + head, 0, 0))
    kv = pl.BlockSpec((2, 1, HEAD_DIM, tokens), lambda head: (0, first_head + head, 0, 0))
    return low, whole, heads, norm, [kv] * len(pieces)


def attend(low, starts, queries, pieces, first_head, count):
    tokens = queries.shape[-1]
    blocks = len(pieces) * tokens // BLOCK
    low_spec, whole, heads, norm, kv = attention_specs(tokens, pieces, first_head)
    return pl.pallas_call(
        attend_kernel,
        grid=(count,),
        in_specs=[low_spec, whole, heads] + kv,
        out_specs=[
            pl.BlockSpec((GROUP, HEAD_DIM, tokens), lambda head: (head, 0, 0)),
            pl.BlockSpec((GROUP, 1, tokens), lambda head: (head, 0, 0)),
        ],
        out_shape=[
            jax.ShapeDtypeStruct((count * GROUP, HEAD_DIM, tokens), jnp.float32),
            jax.ShapeDtypeStruct((count * GROUP, 1, tokens), jnp.float32),
        ],
        scratch_shapes=[
            pltpu.VMEM((blocks, BLOCK, HEAD_DIM), jnp.bfloat16),
            pltpu.VMEM((blocks, HEAD_DIM, BLOCK), jnp.bfloat16),
        ],
        compiler_params=pltpu.CompilerParams(vmem_limit_bytes=kernel_vmem),
        cost_estimate=small_cost,
    )(low, starts, queries, *pieces)


def attend_back(low, starts, queries, grads, attended, norm, pieces, first_head, count):
    tokens = queries.shape[-1]
    blocks = len(pieces) * tokens // BLOCK
    low_spec, whole, heads, norm_spec, kv = attention_specs(tokens, pieces, first_head)
    back = len(pieces) - 1
    return pl.pallas_call(
        gradient_kernel,
        grid=(count,),
        in_specs=[low_spec, whole, heads, heads, heads, norm_spec] + kv,
        out_specs=[
            pl.BlockSpec((GROUP, HEAD_DIM, tokens), lambda head: (head, 0, 0)),
            pl.BlockSpec((2, 1, HEAD_DIM, tokens), lambda head: (0, head, 0, 0)),
            pl.BlockSpec((back, 2, 1, HEAD_DIM, tokens), lambda head: (0, 0, head, 0, 0)),
        ],
        out_shape=[
            jax.ShapeDtypeStruct((count * GROUP, HEAD_DIM, tokens), jnp.float32),
            jax.ShapeDtypeStruct((2, count, HEAD_DIM, tokens), jnp.float32),
            jax.ShapeDtypeStruct((back, 2, count, HEAD_DIM, tokens), jnp.bfloat16),
        ],
        scratch_shapes=[
            pltpu.VMEM((blocks, BLOCK, HEAD_DIM), jnp.bfloat16),
            pltpu.VMEM((blocks, HEAD_DIM, BLOCK), jnp.bfloat16),
            pltpu.VMEM((blocks, BLOCK, HEAD_DIM), jnp.bfloat16),
            pltpu.VMEM((blocks, HEAD_DIM, BLOCK), jnp.float32),
            pltpu.VMEM((blocks, HEAD_DIM, BLOCK), jnp.float32),
        ],
        compiler_params=pltpu.CompilerParams(vmem_limit_bytes=kernel_vmem),
        cost_estimate=small_cost,
    )(low, starts, queries, grads, attended, norm, *pieces)

class Order:
    def __init__(self, token):
        self.token = token

    def step(self, *values):
        self.token, tied = lax.optimization_barrier((self.token, values))
        return tied[0] if len(tied) == 1 else tied


class Grid:
    def __init__(self):
        self.count = lax.axis_size("dev")
        self.teams = self.count // TEAM
        index = lax.axis_index("dev")
        self.member = index % TEAM
        self.team = index // TEAM

    def places(self):
        return jnp.stack([self.team, self.member]).astype(jnp.int32)

    def turn(self, value, bits):
        return lax.ppermute(value, "dev", [(d, d ^ bits) for d in range(self.count)])

    def shift(self, value, steps, around=True):
        pairs = []
        for device in range(self.count):
            target = device + steps * TEAM
            if around or 0 <= target < self.count:
                pairs.append((device, target % self.count))
        return lax.ppermute(value, "dev", pairs)

    def spread(self, value):
        return [value] + [self.shift(value, steps) for steps in range(1, self.teams)]

    def both_ways(self, ahead, behind):
        return self.shift(ahead, 1, False), self.shift(behind, -1, False)

    def gather_team(self, blocks):
        return list(blocks) + [self.turn(block, 1) for block in blocks]

    def chips(self, block):
        return [block] + [self.turn(block, 2 * chip) for chip in range(1, 4)]

    def to_members(self, value):
        pairs = [
            (owner, owner % self.teams * TEAM + owner // self.teams)
            for owner in range(self.count)
        ]
        return lax.ppermute(value, "dev", pairs)

    def to_owners(self, value):
        pairs = [
            (owner % self.teams * TEAM + owner // self.teams, owner)
            for owner in range(self.count)
        ]
        return lax.ppermute(value, "dev", pairs)

    def send_chips(self, blocks):
        return [self.turn(block, 2 * chip) for chip, block in enumerate(blocks, 1)]


def call(kernel, grid, in_specs, out_specs, out_shape, scratch=(), prefetch=0):
    return pl.pallas_call(
        kernel,
        out_shape=out_shape,
        grid_spec=pltpu.PrefetchScalarGridSpec(
            num_scalar_prefetch=prefetch,
            grid=grid,
            in_specs=in_specs,
            out_specs=out_specs,
            scratch_shapes=list(scratch),
        ),
        compiler_params=pltpu.CompilerParams(vmem_limit_bytes=kernel_vmem),
        cost_estimate=small_cost,
    )


def fixed(array):
    return pl.BlockSpec(array.shape, lambda *unused: (0,) * array.ndim)


def lanes_at(rows, step_width):
    return pl.BlockSpec((rows, step_width), lambda p, *unused: (0, p))


def rows_at(step_rows, width):
    return pl.BlockSpec((step_rows, width), lambda p, *unused: (p, 0))


def kept_given(rows, width, axis):
    def index(at):
        return (0, at) if axis else (at, 0)

    specs = [
        pl.BlockSpec((rows, width), lambda p, *unused: index(jnp.minimum(p, 3))),
        pl.BlockSpec((rows, width), lambda p, *unused: index(jnp.maximum(p - 4, 0))),
    ]
    shape = (rows, 4 * width) if axis else (4 * rows, width)
    shapes = [
        jax.ShapeDtypeStruct(shape, jnp.float32),
        jax.ShapeDtypeStruct(shape, jnp.bfloat16),
    ]
    return specs, shapes


def keep_or_give(position, keep_ref, give_ref, value):
    @pl.when(position < 4)
    def keep():
        keep_ref[...] = value

    @pl.when(position >= 4)
    def give():
        give_ref[...] = value.astype(give_ref.dtype)


def pick(position, refs, target):
    for number in range(TEAM):

        @pl.when(position == number)
        def move():
            if len(refs) == TEAM:
                target[...] = refs[number][...]
            else:
                target[...] = refs[number // 4][number % 4]


def dot_rows(left, right):
    return lax.dot_general(
        left, right, (((1,), (1,)), ((), ())), preferred_element_type=jnp.float32
    )


def dot(left, right):
    return jnp.dot(left, right, preferred_element_type=jnp.float32)


def place_rows(grid, blocks, start, stop):
    count = len(blocks)
    positions, rows = blocks[0].shape[:2]
    width = stop - start

    def kernel(places_ref, *refs):
        target = refs[-1]
        for number, ref in enumerate(refs[:-1]):

            @pl.when(pl.program_id(0) == number)
            def move():
                for position in range(positions):
                    at = relative(position) ^ places_ref[1] if positions > 1 else 0
                    target[0, pl.ds(at, 1)] = ref[position : position + 1, :, start:stop]

    def target_map(step, places_ref):
        return ((places_ref[0] + count - step) % count, 0, 0, 0)

    return call(
        kernel,
        (count,),
        [fixed(block) for block in blocks],
        pl.BlockSpec((1, positions, rows, width), target_map),
        jax.ShapeDtypeStruct((count, positions, rows, width), blocks[0].dtype),
        prefetch=1,
    )(grid.places(), *blocks)


def place_mixer(grid, own, hops, units, unit_rows):
    count = grid.teams
    positions, rows, wide = own.shape
    third = wide - 2 * units
    sources = [own] + [block for hop in hops for block in hop]

    def kernel(places_ref, *refs):
        mixer_ref, down_ref = refs[-2:]
        team = places_ref[0]

        def move(ref):
            for position in range(positions):
                at = relative(position) ^ places_ref[1]
                mixer_ref[0, pl.ds(at, 1)] = ref[position : position + 1, :, : 2 * units]
                row = position * rows
                while row < (position + 1) * rows:
                    part = row // unit_rows
                    stop = min((part + 1) * unit_rows, (position + 1) * rows)
                    down_ref[
                        0,
                        row - part * unit_rows : stop - part * unit_rows,
                        part * third : (part + 1) * third,
                    ] = ref[position, row - position * rows : stop - position * rows, 2 * units :]
                    row = stop

        for steps in range(count):
            here = pl.program_id(0) == steps
            if steps == 0:
                pl.when(here)(lambda: move(refs[0]))
            else:
                ahead, behind = refs[2 * steps - 1], refs[2 * (count - steps)]
                pl.when(here & (team >= steps))(lambda ahead=ahead: move(ahead))
                pl.when(here & (team < steps))(lambda behind=behind: move(behind))

    def target_map(step, places_ref):
        return (places_ref[0] + count - step) % count

    return call(
        kernel,
        (count,),
        [fixed(source) for source in sources],
        [
            pl.BlockSpec(
                (1, positions, rows, 2 * units), lambda s, p: (target_map(s, p), 0, 0, 0)
            ),
            pl.BlockSpec((1, unit_rows, 3 * third), lambda s, p: (target_map(s, p), 0, 0)),
        ],
        [
            jax.ShapeDtypeStruct((count, positions, rows, 2 * units), own.dtype),
            jax.ShapeDtypeStruct((count, unit_rows, 3 * third), own.dtype),
        ],
        prefetch=1,
    )(grid.places(), *sources)


def project(inputs_t, weights, cosine, sine_table):
    width, own = inputs_t[0].shape
    tokens = TEAM * own
    half = HEAD_DIM // 2

    def kernel(weights_ref, cosine_ref, sine_ref, *refs):
        sources = refs[:TEAM]
        normed_ref, query_ref, kv_ref, chosen, turned = refs[TEAM:]
        position = pl.program_id(0)

        @pl.when(position == 0)
        def prepare():
            turned[...] = weights_ref[:, :LINED].T

        pick(position, sources, chosen)
        values = chosen[...].astype(jnp.float32)
        scale = lax.rsqrt(jnp.mean(values * values, axis=0, keepdims=True) + eps_norm)
        gain = weights_ref[:, LINED : LINED + 1].astype(jnp.float32)
        normed = (values * scale * gain).astype(jnp.bfloat16)
        normed_ref[...] = normed
        lined = dot(turned[...], normed)
        cosines, sines = cosine_ref[...], sine_ref[...]

        def rotated(head):
            block = lined[head * HEAD_DIM : (head + 1) * HEAD_DIM]
            shifted = jnp.concatenate([-block[half:], block[:half]], axis=0)
            return (block * cosines + shifted * sines).astype(jnp.bfloat16)

        for head in range(OWN_HEADS):
            query_ref[head] = rotated(head)
        for head in range(OWN_KV):
            kv_ref[0, head] = rotated(OWN_HEADS + head)
            start = Q_WIDTH + KV_WIDTH + head * HEAD_DIM
            kv_ref[1, head] = lined[start : start + HEAD_DIM].astype(jnp.bfloat16)

    return call(
        kernel,
        (TEAM,),
        [fixed(weights), lanes_at(HEAD_DIM, own), lanes_at(HEAD_DIM, own)]
        + [fixed(block) for block in inputs_t],
        [
            lanes_at(width, own),
            pl.BlockSpec((OWN_HEADS, HEAD_DIM, own), lambda p: (0, 0, p)),
            pl.BlockSpec((2, OWN_KV, HEAD_DIM, own), lambda p: (0, 0, 0, p)),
        ],
        [
            jax.ShapeDtypeStruct((width, tokens), jnp.bfloat16),
            jax.ShapeDtypeStruct((OWN_HEADS, HEAD_DIM, tokens), jnp.bfloat16),
            jax.ShapeDtypeStruct((2, OWN_KV, HEAD_DIM, tokens), jnp.bfloat16),
        ],
        [
            pltpu.VMEM((width, own), jnp.bfloat16),
            pltpu.VMEM((LINED, width), jnp.bfloat16),
        ],
    )(weights, cosine, sine_table, *inputs_t)


def project_out(attended, out_rows):
    tokens = attended.shape[-1]
    own = tokens // TEAM
    width = out_rows.shape[1]
    specs, shapes = kept_given(width, own, 1)

    def kernel(attended_ref, rows_ref, keep_ref, give_ref, turned):
        position = pl.program_id(0)

        @pl.when(position == 0)
        def prepare():
            turned[...] = rows_ref[...].T

        block = attended_ref[...].reshape(Q_WIDTH, own).astype(jnp.bfloat16)
        keep_or_give(position, keep_ref, give_ref, dot(turned[...], block))

    return call(
        kernel,
        (TEAM,),
        [pl.BlockSpec((OWN_HEADS, HEAD_DIM, own), lambda p: (0, 0, p)), fixed(out_rows)],
        specs,
        shapes,
        [pltpu.VMEM((width, Q_WIDTH), jnp.bfloat16)],
    )(attended, out_rows)


def mixer(chip, normed, cotangent, weights, down):
    width, own = normed[0].shape
    units = down.shape[0]

    def kernel(first_ref, second_ref, wanted_a, wanted_b, weights_ref, down_ref, *refs):
        hidden_ref, grad_ref, keep_ref, give_ref, turned, wanted = refs
        step = pl.program_id(0)

        @pl.when(step == 0)
        def first():
            turned[...] = first_ref[...].T
            wanted[...] = wanted_a[0]

        @pl.when(step == 1)
        def second():
            turned[...] = second_ref[...].T
            wanted[...] = wanted_b[0]

        gate = dot(turned[...], weights_ref[:, :units])
        up = dot(turned[...], weights_ref[:, units:])
        logistic = 1.0 / (1.0 + jnp.exp(-gate))
        silu = gate * logistic
        hidden_ref[...] = (silu * up).astype(jnp.bfloat16)
        grad_hidden = dot_rows(wanted[...], down_ref[...])
        grad_ref[:, :units] = (
            grad_hidden * up * (logistic * (1.0 + gate * (1.0 - logistic)))
        ).astype(jnp.bfloat16)
        grad_ref[:, units:] = (grad_hidden * silu).astype(jnp.bfloat16)
        term = dot_rows(weights_ref[...], grad_ref[...])

        @pl.when(step == 0)
        def keep():
            keep_ref[...] = term

        @pl.when(step == 1)
        def give():
            give_ref[...] = term.astype(jnp.bfloat16)

    block = pl.BlockSpec((1, own, width), lambda p: (chip, 0, 0))
    whole = pl.BlockSpec((width, own), lambda p: (0, 0))
    return call(
        kernel,
        (2,),
        [fixed(normed[0]), fixed(normed[1]), block, block, fixed(weights), fixed(down)],
        [rows_at(own, units), rows_at(own, 2 * units), whole, whole],
        [
            jax.ShapeDtypeStruct((2 * own, units), jnp.bfloat16),
            jax.ShapeDtypeStruct((2 * own, 2 * units), jnp.bfloat16),
            jax.ShapeDtypeStruct((width, own), jnp.float32),
            jax.ShapeDtypeStruct((width, own), jnp.bfloat16),
        ],
        [pltpu.VMEM((own, width), jnp.bfloat16), pltpu.VMEM((own, width), jnp.bfloat16)],
    )(normed[0], normed[1], cotangent[0], cotangent[1], weights, down)


def add_block(keep, arrived):
    def kernel(keep_ref, arrived_ref, out_ref):
        out_ref[...] = (keep_ref[...] + arrived_ref[...].astype(jnp.float32)).astype(jnp.bfloat16)

    rows = keep.shape[0] // 2
    part = rows_at(rows, keep.shape[1])
    return call(
        kernel, (2,), [part, part], part, jax.ShapeDtypeStruct(keep.shape, jnp.bfloat16)
    )(keep, arrived)


def pair_rows(position, refs, target):
    own = target.shape[0]
    for number in range(TEAM):

        @pl.when(position == number)
        def move():
            start = number // 4 * own
            target[...] = refs[number % 4][start : start + own]


def mixer_output(hidden, down):
    own, units = hidden[0].shape[0] // 2, hidden[0].shape[1]
    specs, shapes = kept_given(own, down.shape[1], 0)

    def kernel(down_ref, *refs):
        keep_ref, give_ref, chosen = refs[4:]
        pair_rows(pl.program_id(0), refs[:4], chosen)
        keep_or_give(pl.program_id(0), keep_ref, give_ref, dot(chosen[...], down_ref[...]))

    return call(
        kernel,
        (TEAM,),
        [fixed(down)] + [fixed(block) for block in hidden],
        specs,
        shapes,
        [pltpu.VMEM((own, units), jnp.bfloat16)],
    )(down, *hidden)


def write_teams(places_ref, total, out_ref, teams):
    rows = total.shape[0] // teams
    for team in range(teams):
        steps = (team + teams - places_ref[0]) % teams
        block = total[team * rows : (team + 1) * rows, :].astype(out_ref.dtype)
        out_ref[pl.ds(steps, 1)] = block[None]


def token_product(grid, lefts, rights):
    rows, own = lefts[0].shape
    width = rights[0].shape[1]
    teams = grid.teams

    def kernel(places_ref, *refs):
        left_refs, right_refs = refs[:TEAM], refs[TEAM : TEAM + 4]
        out_ref, total, chosen = refs[TEAM + 4 :]
        position = pl.program_id(0)
        pair_rows(position, right_refs, chosen)

        def add(value):
            @pl.when(position == 0)
            def first():
                total[...] = value

            @pl.when(position > 0)
            def later():
                total[...] += value

        for number, source in enumerate(left_refs):

            @pl.when(position == number)
            def block():
                add(dot(source[...], chosen[...]))

        @pl.when(position == TEAM - 1)
        def last():
            write_teams(places_ref, total, out_ref, teams)

    return call(
        kernel,
        (TEAM,),
        [fixed(block) for block in list(lefts) + list(rights)],
        pl.BlockSpec((teams, rows // teams, width), lambda p, *unused: (0, 0, 0)),
        jax.ShapeDtypeStruct((teams, rows // teams, width), jnp.bfloat16),
        [pltpu.VMEM((rows, width), jnp.float32), pltpu.VMEM((own, width), jnp.bfloat16)],
        prefetch=1,
    )(grid.places(), *lefts, *rights)


def down_product(grid, hidden, cotangent):
    units = hidden[0].shape[1]
    own, width = cotangent[0].shape[1:]
    teams = grid.teams

    def kernel(places_ref, *refs):
        hidden_refs, sources, (out_ref, total, wanted, chosen) = refs[:4], refs[4:6], refs[6:]
        position = pl.program_id(0)
        pick(position, sources, wanted)
        pair_rows(position, hidden_refs, chosen)
        value = dot(chosen[...].T, wanted[...])

        @pl.when(position == 0)
        def first():
            total[...] = value

        @pl.when(position > 0)
        def later():
            total[...] += value

        @pl.when(position == TEAM - 1)
        def last():
            write_teams(places_ref, total, out_ref, teams)

    return call(
        kernel,
        (TEAM,),
        [fixed(block) for block in list(hidden) + list(cotangent)],
        pl.BlockSpec((teams, units // teams, width), lambda p, *unused: (0, 0, 0)),
        jax.ShapeDtypeStruct((teams, units // teams, width), jnp.bfloat16),
        [
            pltpu.VMEM((units, width), jnp.float32),
            pltpu.VMEM((own, width), jnp.bfloat16),
            pltpu.VMEM((own, units), jnp.bfloat16),
        ],
        prefetch=1,
    )(grid.places(), *hidden, *cotangent)


def project_out_back(grid, grads, out_rows, attended):
    teams = grid.teams
    tokens = attended.shape[-1]
    own = tokens // TEAM
    width = out_rows.shape[1]

    def kernel(places_ref, rows_ref, attended_ref, *refs):
        sources, (grad_ref, out_ref, chosen, total) = refs[:TEAM], refs[TEAM:]
        position = pl.program_id(0)
        pick(position, sources, chosen)
        grad_ref[...] = (
            dot(rows_ref[...], chosen[...])
            .astype(jnp.bfloat16)
            .reshape(OWN_HEADS, HEAD_DIM, own)
        )
        block = attended_ref[...].reshape(Q_WIDTH, own).astype(jnp.bfloat16)
        value = dot_rows(block, chosen[...])

        @pl.when(position == 0)
        def first():
            total[...] = value

        @pl.when(position > 0)
        def later():
            total[...] += value

        @pl.when(position == TEAM - 1)
        def last():
            write_teams(places_ref, total, out_ref, teams)

    heads = pl.BlockSpec((OWN_HEADS, HEAD_DIM, own), lambda p, *unused: (0, 0, p))
    shape = (teams, Q_WIDTH // teams, width)
    return call(
        kernel,
        (TEAM,),
        [fixed(out_rows), heads] + [fixed(block) for block in grads],
        [heads, pl.BlockSpec(shape, lambda p, *unused: (0, 0, 0))],
        [
            jax.ShapeDtypeStruct((OWN_HEADS, HEAD_DIM, tokens), jnp.bfloat16),
            jax.ShapeDtypeStruct(shape, jnp.bfloat16),
        ],
        [pltpu.VMEM((width, own), jnp.bfloat16), pltpu.VMEM((Q_WIDTH, width), jnp.float32)],
        prefetch=1,
    )(grid.places(), out_rows, attended, *grads)


def project_back(grid, normed, query_rot, own_grads, returned, cosine, sine_table, weights):
    width, tokens = normed.shape
    own = tokens // TEAM
    half = HEAD_DIM // 2
    teams = grid.teams
    specs, shapes = kept_given(width, own, 1)

    def kernel(places_ref, normed_ref, query_ref, cosine_ref, sine_ref, weights_ref, *refs):
        kv_refs = refs[: 1 + len(returned)]
        keep_ref, give_ref, out_ref, total, grad_ref = refs[1 + len(returned) :]
        position = pl.program_id(0)
        cosines, sines = cosine_ref[...], sine_ref[...]

        def unrotated(block):
            scaled = block * sines
            shifted = jnp.concatenate([scaled[half:], -scaled[:half]], axis=0)
            return (block * cosines + shifted).astype(jnp.bfloat16)

        for head in range(OWN_HEADS):
            grad_ref[head * HEAD_DIM : (head + 1) * HEAD_DIM] = unrotated(query_ref[head])
        kv = kv_refs[0][...]
        for ref in kv_refs[1:]:
            kv = kv + ref[...].astype(jnp.float32)
        for head in range(OWN_KV):
            start = Q_WIDTH + head * HEAD_DIM
            grad_ref[start : start + HEAD_DIM] = unrotated(kv[0, head])
            start = start + KV_WIDTH
            grad_ref[start : start + HEAD_DIM] = kv[1, head].astype(jnp.bfloat16)
        grad = grad_ref[...]
        keep_or_give(position, keep_ref, give_ref, dot(weights_ref[:, :LINED], grad))
        value = dot_rows(normed_ref[...], grad)

        @pl.when(position == 0)
        def first():
            total[...] = value

        @pl.when(position > 0)
        def later():
            total[...] += value

        @pl.when(position == TEAM - 1)
        def last():
            write_teams(places_ref, total, out_ref, teams)

    heads = pl.BlockSpec((OWN_HEADS, HEAD_DIM, own), lambda p, *unused: (0, 0, p))
    kv_heads = pl.BlockSpec((2, OWN_KV, HEAD_DIM, own), lambda p, *unused: (0, 0, 0, p))
    return call(
        kernel,
        (TEAM,),
        [
            lanes_at(width, own),
            heads,
            lanes_at(HEAD_DIM, own),
            lanes_at(HEAD_DIM, own),
            fixed(weights),
        ]
        + [kv_heads] * (1 + len(returned)),
        specs + [pl.BlockSpec((teams, width // teams, LINED), lambda p, *unused: (0, 0, 0))],
        shapes + [jax.ShapeDtypeStruct((teams, width // teams, LINED), jnp.bfloat16)],
        [pltpu.VMEM((width, LINED), jnp.float32), pltpu.VMEM((LINED, own), jnp.bfloat16)],
        prefetch=1,
    )(grid.places(), normed, query_rot, cosine, sine_table, weights, own_grads, *returned)


def combine(keep, arrived, axis):
    size = keep.shape[axis] // 4
    shape = (keep.shape[0], size) if axis else (size, keep.shape[1])

    def kernel(keep_ref, arrived_ref, own_ref, *block_refs):
        position = pl.program_id(0)
        total = keep_ref[...] + arrived_ref[...].astype(jnp.float32)

        @pl.when(position == 0)
        def own():
            own_ref[...] = total

        for number, ref in enumerate(block_refs, 1):

            @pl.when(position == number)
            def other():
                ref[...] = total.astype(jnp.bfloat16)

    part = pl.BlockSpec(shape, (lambda p: (0, p)) if axis else (lambda p: (p, 0)))
    whole = pl.BlockSpec(shape, lambda p: (0, 0))
    own, *blocks = call(
        kernel,
        (4,),
        [part, part],
        [whole] * 4,
        [jax.ShapeDtypeStruct(shape, jnp.float32)]
        + [jax.ShapeDtypeStruct(shape, jnp.bfloat16)] * 3,
    )(keep, arrived)
    return own, blocks


def summed(refs):
    total = refs[0][...]
    for ref in refs[1:]:
        total = total + ref[...].astype(jnp.float32)
    return total


def finish(kernel, arrays, shapes):
    return call(
        kernel,
        (1,),
        [fixed(array) for array in arrays],
        [pl.BlockSpec(shape.shape, lambda p: (0, 0)) for shape in shapes],
        shapes,
    )(*arrays)


def finish_middle(terms, inputs_t, gain):
    def kernel(*refs):
        inputs_ref, gain_ref, middle_ref, normed_ref = refs[len(terms) :]
        middle = inputs_ref[...].astype(jnp.float32) + summed(refs[: len(terms)])
        middle_ref[...] = middle
        scale = lax.rsqrt(jnp.mean(middle * middle, axis=0, keepdims=True) + eps_norm)
        normed_ref[...] = (middle * scale * gain_ref[...]).astype(jnp.bfloat16)

    shape = inputs_t.shape
    return finish(
        kernel,
        list(terms) + [inputs_t, gain],
        [jax.ShapeDtypeStruct(shape, jnp.float32), jax.ShapeDtypeStruct(shape, jnp.bfloat16)],
    )


def norm_back(values, gain, grad):
    inverse = lax.rsqrt(jnp.mean(values * values, axis=0, keepdims=True) + eps_norm)
    normal = values * inverse
    scaled = grad * gain
    inner = jnp.mean(scaled * normal, axis=0, keepdims=True)
    return inverse * (scaled - normal * inner), jnp.sum(grad * normal, axis=1, keepdims=True)


def finish_second(terms, middle, cotangent, gain):
    def kernel(*refs):
        middle_ref, cotangent_ref, gain_ref, grad_ref, attn_ref, gain_out = refs[len(terms) :]
        norm_grad, gain_part = norm_back(
            middle_ref[...], gain_ref[...], summed(refs[: len(terms)])
        )
        grad = cotangent_ref[...].T.astype(jnp.float32) + norm_grad
        grad_ref[...] = grad
        attn_ref[...] = grad.astype(jnp.bfloat16)
        gain_out[...] = gain_part

    shape = middle.shape
    return finish(
        kernel,
        list(terms) + [middle, cotangent, gain],
        [
            jax.ShapeDtypeStruct(shape, jnp.float32),
            jax.ShapeDtypeStruct(shape, jnp.bfloat16),
            jax.ShapeDtypeStruct((shape[0], 1), jnp.float32),
        ],
    )


def finish_first(terms, inputs_t, grad_middle, gain):
    def kernel(*refs):
        inputs_ref, grad_ref, gain_ref, out_ref, gain_out = refs[len(terms) :]
        norm_grad, gain_part = norm_back(
            inputs_ref[...].astype(jnp.float32), gain_ref[...], summed(refs[: len(terms)])
        )
        out_ref[...] = (grad_ref[...] + norm_grad).T
        gain_out[...] = gain_part

    width, own = inputs_t.shape
    return finish(
        kernel,
        list(terms) + [inputs_t, grad_middle, gain],
        [
            jax.ShapeDtypeStruct((own, width), jnp.float32),
            jax.ShapeDtypeStruct((width, 1), jnp.float32),
        ],
    )


def finish_output(terms, middle):
    def kernel(*refs):
        middle_ref, out_ref = refs[len(terms) :]
        out_ref[...] = (middle_ref[...].T + summed(refs[: len(terms)])).astype(jnp.bfloat16)

    return finish(
        kernel, list(terms) + [middle], [jax.ShapeDtypeStruct(terms[0].shape, jnp.bfloat16)]
    )[0]


def sum_teams(product, parts, kind):
    def kernel(own_ref, *refs):
        total = own_ref[0].astype(jnp.float32)
        for ref in refs[:-1]:
            total = total + ref[...].astype(jnp.float32)
        refs[-1][...] = total.astype(kind)

    shape = product.shape[1:]
    return call(
        kernel,
        (1,),
        [pl.BlockSpec((1,) + shape, lambda p: (0, 0, 0))] + [fixed(part) for part in parts],
        pl.BlockSpec(shape, lambda p: (0, 0)),
        jax.ShapeDtypeStruct(shape, kind),
    )(product, *parts)


def rope_tables(positions):
    half_dim = HEAD_DIM // 2
    frequency = rope_base ** (-(jnp.arange(half_dim, dtype=jnp.float32) * 2.0 / HEAD_DIM))
    angles = frequency[:, None] * positions.astype(jnp.float32)[None, :]
    angles = jnp.concatenate([angles, angles], axis=0)
    return (jnp.cos(angles), jnp.sin(angles))


def per_device(
    inputs,
    positions,
    norm_first,
    query_weight,
    key_weight,
    value_weight,
    out_weight,
    norm_second,
    gate_weight,
    up_weight,
    down_weight,
    cotangent,
):
    grid = Grid()
    member, teams = grid.member, grid.teams
    chip, core = member // 2, member % 2
    own, width = inputs.shape
    tokens = own * TEAM
    rows = query_weight.shape[0]
    unit_rows = down_weight.shape[0]
    units = unit_rows * teams
    longest = own * grid.count // 4
    steps_back = min((longest - 2) // tokens + 1, teams - 1)
    bf16, f32 = jnp.bfloat16, jnp.float32
    order = Order(jnp.zeros((8, 128), jnp.int32))

    def dynamic(array, index, axis=0):
        return lax.dynamic_index_in_dim(array, index, axis, keepdims=False)

    def by_member(weight):
        return jnp.transpose(weight.reshape(rows, TEAM, -1), (1, 0, 2))

    def units_by_member(weight):
        blocks = jnp.transpose(weight.reshape(rows, teams, TEAM, unit_rows), (2, 0, 1, 3))
        return blocks.reshape(TEAM, rows, units)

    gains = jnp.pad(jnp.stack([norm_first, norm_second], axis=1), ((0, 0), (0, LANES - 2)))
    columns = jnp.concatenate(
        [
            by_member(query_weight),
            by_member(key_weight),
            by_member(value_weight),
            jnp.broadcast_to(gains[None], (TEAM, rows, LANES)),
            units_by_member(gate_weight),
            units_by_member(up_weight),
        ],
        axis=-1,
    )
    attn_wide = LINED + LANES
    columns = columns.reshape(TEAM // 2, 2, rows, attn_wide + 2 * units)
    position_chips = jnp.stack(grid.chips(positions))
    all_positions = jnp.concatenate([position_chips, grid.turn(position_chips, 1)]).reshape(tokens)
    inputs_t = inputs.T
    columns, inputs_t = order.step(columns, inputs_t)
    pairs = [
        dynamic(columns, chip)
        if other == 0
        else grid.turn(dynamic(columns, chip ^ other), 2 * other)
        for other in range(4)
    ]
    inputs_two = [grid.turn(inputs_t, 2), grid.turn(inputs_t, 4)]
    cosine, sine_table = rope_tables(all_positions)
    block_index = steps_back * TEAM + (
        jnp.array([relative(p) for p in range(TEAM)], jnp.int32) ^ member
    )
    token_index = (block_index[:, None] * own + jnp.arange(own, dtype=jnp.int32)).reshape(tokens)
    starts = token_index - all_positions
    low = jnp.concatenate([starts[::own] // BLOCK, member[None]]).astype(jnp.int32)
    starts = starts[None]
    third = width // 3
    down_thirds = jnp.concatenate(
        [down_weight[:, part * third : (part + 1) * third] for part in range(3)], axis=0
    ).reshape(TEAM, rows, third)
    cosine, sine_table, starts, low, down_thirds, pairs, inputs_two, inputs_t = order.step(
        cosine, sine_table, starts, low, down_thirds, pairs, inputs_two, inputs_t
    )
    inputs_three = grid.turn(inputs_t, 6)
    pairs = jnp.stack(pairs)
    pairs_keep, pairs_give = dynamic(pairs, core, 1), dynamic(pairs, 1 - core, 1)
    team_rows = jnp.concatenate([pairs_keep, grid.turn(pairs_give, 1)], axis=0)
    attn_rows, team_rows, out_weight = order.step(
        team_rows[..., :attn_wide], team_rows, out_weight
    )
    attn_z = grid.spread(attn_rows)
    inputs_others = [grid.turn(block, 1) for block in [inputs_t] + inputs_two]
    attn_z, inputs_three = order.step(attn_z, inputs_three)
    inputs_others = inputs_others + [grid.turn(inputs_three, 1)]
    inputs_team = [inputs_t] + inputs_two + [inputs_three] + inputs_others
    out_own = grid.to_members(out_weight)
    attn_w = place_rows(grid, attn_z, 0, attn_wide).reshape(width, attn_wide)
    attn_w, inputs_team, out_own = order.step(attn_w, inputs_team, out_own)

    out_own, cotangent = order.step(out_own, cotangent)
    out_z = grid.spread(out_own)
    cotangent_chips = [cotangent, grid.turn(cotangent, 2), grid.turn(cotangent, 4)]
    normed_first, queries, own_piece = project(inputs_team, attn_w, cosine, sine_table)
    own_piece, out_z, attn_w = order.step(own_piece, out_z, attn_w)
    arrived = [grid.shift(own_piece, step, False) for step in range(1, steps_back + 1)]
    cotangent_chips = order.step(cotangent_chips)
    cotangent_chips = cotangent_chips + [grid.turn(cotangent_chips[0], 6)]
    out_rows = place_rows(grid, [block[None] for block in out_z], 0, width)
    out_rows = out_rows.reshape(Q_WIDTH, width)
    gain_first = attn_w[:, LINED : LINED + 1].astype(f32)
    gain_second = attn_w[:, LINED + 1 : LINED + 2].astype(f32)
    mixer_own = jnp.concatenate([team_rows[..., attn_wide:], down_thirds], axis=-1)
    arrived, gain_first, gain_second, mixer_own, out_rows = order.step(
        arrived, gain_first, gain_second, mixer_own, out_rows
    )

    mixer_hops = [grid.both_ways(mixer_own, mixer_own)]

    def next_hop():
        if len(mixer_hops) < teams - 1:
            mixer_hops.append(grid.both_ways(*mixer_hops[-1]))

    pieces = [own_piece] + arrived
    attended, normalizer = attend(low, starts, queries, pieces, 0, OWN_KV)
    keep, give = project_out(attended, out_rows)
    give, mixer_hops[0], cotangent_chips = order.step(give, mixer_hops[0], cotangent_chips)
    other = grid.turn(give, 1)
    next_hop()
    cotangent_stack = jnp.stack(cotangent_chips)
    other, cotangent_stack = order.step(other, cotangent_stack)
    cotangent_other = grid.turn(cotangent_stack, 1)
    total, blocks = combine(keep, other, 1)
    blocks, cotangent_other = order.step(blocks, cotangent_other)
    cotangent_team = [cotangent_stack, cotangent_other]
    near = [grid.turn(blocks[0], 2), grid.turn(blocks[1], 4)]
    near, far, mixer_hops[-1] = order.step(near, blocks[2], mixer_hops[-1])
    terms = near + [grid.turn(far, 6)]
    next_hop()
    terms = order.step(terms)
    middle, normed_second = finish_middle([total] + terms, inputs_t, gain_second)
    normed_second, mixer_hops[-1] = order.step(normed_second, mixer_hops[-1])
    while len(mixer_hops) < teams - 1:
        next_hop()
        mixer_hops[-1] = order.step(mixer_hops[-1])
    second_chips = [normed_second, grid.turn(normed_second, 2), grid.turn(normed_second, 4)]
    second_other = [grid.turn(normed_second, 1)]
    mixer_w, down_w = place_mixer(grid, mixer_own, mixer_hops, units, unit_rows)
    mixer_w = mixer_w.reshape(width, 2 * units)
    down_w = down_w.reshape(units, width)
    mixer_w, down_w, second_other[0] = order.step(mixer_w, down_w, second_other[0])

    def send_teams(product, first=1, last=teams):
        return [grid.shift(product[steps], steps) for steps in range(first, last)]

    def run_mixer(other_chip):
        hidden_part, grads_part, keep, give = mixer(
            other_chip,
            (second_chips[other_chip], second_other[other_chip]),
            cotangent_team,
            mixer_w,
            down_w,
        )
        return hidden_part, grads_part, keep, order.step(give)

    parts = [run_mixer(0)]
    passed = [grid.turn(parts[0][3], 1)]
    second_chips = order.step(second_chips)
    second_chips = second_chips + [grid.turn(second_chips[0], 6)]
    second_other += order.step([grid.turn(second_chips[1], 1), grid.turn(second_chips[2], 1)])
    parts.append(run_mixer(1))
    passed.append(grid.turn(parts[1][3], 1))
    second_chips[3], passed[0] = order.step(second_chips[3], passed[0])
    second_other.append(grid.turn(second_chips[3], 1))
    parts.append(run_mixer(2))
    passed[1], second_other[3] = order.step(passed[1], second_other[3])
    block = order.step(add_block(parts[1][2], passed[1]))
    terms = [parts[0][2], passed[0], grid.turn(block, 2)]
    passed.append(grid.turn(parts[2][3], 1))
    parts.append(run_mixer(3))
    passed[2] = order.step(passed[2])
    passed.append(grid.turn(parts[3][3], 1))
    block = order.step(add_block(parts[2][2], passed[2]))
    terms.append(grid.turn(block, 4))
    passed[3] = order.step(passed[3])
    hidden, grads = [part[0] for part in parts], [part[1] for part in parts]
    block, grads, hidden = order.step(add_block(parts[3][2], passed[3]), grads, hidden)
    terms.append(grid.turn(block, 6))
    second_team = second_chips + second_other
    early = max(1, teams // 2)
    mixer_part = token_product(grid, second_team, grads)
    mixer_part, hidden = order.step(mixer_part, hidden)
    mixer_parts = send_teams(mixer_part, 1, early + 1)
    down_part = down_product(grid, hidden, cotangent_team)
    terms, down_part = order.step(terms, down_part)
    grad_middle, grad_attn, second_part = finish_second(terms, middle, cotangent, gain_second)
    grad_attn, hidden = order.step(grad_attn, hidden)
    attn_chips = grid.chips(grad_attn)
    out_keep, out_give = mixer_output(hidden, down_w)
    attn_chips, out_give, mixer_parts = order.step(attn_chips, out_give, mixer_parts)
    late_parts = send_teams(mixer_part, early + 1, teams)
    attn_team = order.step(grid.gather_team(attn_chips))

    grad_attended, out_part = project_out_back(grid, attn_team, out_rows, attended)
    grad_attended, down_part, out_give = order.step(grad_attended, down_part, out_give)
    down_late = send_teams(down_part, early + 1, teams)
    out_other = grid.turn(out_give, 1)
    query_rot, own_grads, back_grads = attend_back(
        low, starts, queries, grad_attended, attended, normalizer, pieces, 0, OWN_KV
    )
    query_rot, own_grads, back_grads, late_parts, down_late, out_other = order.step(
        query_rot, own_grads, back_grads, late_parts, down_late, out_other
    )
    returned = [
        grid.shift(back_grads[step - 1], -step, False) for step in range(1, steps_back + 1)
    ]
    out_total, out_blocks = combine(out_keep, out_other, 0)
    out_blocks = order.step(out_blocks)
    out_terms = grid.send_chips(out_blocks)
    mixer_total = sum_teams(mixer_part, mixer_parts + late_parts, bf16)
    def members_rows(total):
        blocks = total.reshape(TEAM // 2, 2, rows, -1)
        return dynamic(blocks, core, 1), grid.turn(dynamic(blocks, 1 - core, 1), 1)

    def owner_columns(mine, others):
        both = jnp.stack([mine, others])
        first = jnp.where(core == 0, both[0], both[1])
        second = jnp.where(core == 0, both[1], both[0])
        both = jnp.stack([first, second], axis=1)
        found = [
            dynamic(both, chip) if other == 0 else grid.turn(dynamic(both, chip ^ other), 2 * other)
            for other in range(4)
        ]
        return found

    def in_order(found):
        stacked = jnp.stack(found)
        return jnp.stack([dynamic(stacked, chip ^ other) for other in range(4)]).reshape(
            (TEAM,) + found[0].shape[1:]
        )

    returned, mixer_total = order.step(returned, mixer_total)
    down_parts = send_teams(down_part, 1, early + 1)
    mixer_mine, mixer_others = members_rows(mixer_total)
    keep, give, attn_part = project_back(
        grid, normed_first, query_rot, own_grads, returned, cosine, sine_table, attn_w
    )
    attn_part, give, out_terms, down_parts, mixer_others = order.step(
        attn_part, give, out_terms, down_parts, mixer_others
    )
    other = grid.turn(give, 1)
    mixer_found = owner_columns(mixer_mine, mixer_others)
    other = order.step(other)
    total, blocks = combine(keep, other, 1)
    blocks, mixer_found, out_part = order.step(blocks, mixer_found, out_part)
    terms = grid.send_chips(blocks)
    attn_parts = send_teams(attn_part, 1, early + 1)
    outputs = finish_output([out_total] + out_terms, middle)
    down_grad = sum_teams(down_part, down_parts + down_late, f32)
    mixer_columns = in_order(mixer_found)
    attn_parts, outputs, down_grad = order.step(attn_parts, outputs, down_grad)
    attn_late = send_teams(attn_part, early + 1, teams)
    terms, attn_late = order.step(terms, attn_late)
    out_parts = send_teams(out_part, 1, teams)
    input_grad, first_part = finish_first([total] + terms, inputs_t, grad_middle, gain_first)
    gain_parts = jnp.concatenate([first_part, second_part], axis=1).T
    attn_total = sum_teams(attn_part, attn_parts + attn_late, bf16)
    attn_mine, attn_others = members_rows(attn_total)
    gain_parts, attn_total = order.step(gain_parts, attn_total)
    gain_other = grid.turn(gain_parts, 1)
    gain_other, attn_others, out_parts = order.step(gain_other, attn_others, out_parts)
    gain_parts = gain_parts + gain_other
    gain_parts = order.step(gain_parts)
    gain_chips = [grid.turn(gain_parts, 2 * other) for other in range(1, 4)]
    out_own = sum_teams(out_part, out_parts, bf16)
    gain_chips, out_own = order.step(gain_chips, out_own)
    for other in gain_chips:
        gain_parts = gain_parts + other
    attn_found = owner_columns(attn_mine, attn_others)
    out_grad = grid.to_owners(out_own)

    def whole_units(blocks):
        blocks = blocks.reshape(TEAM, rows, teams, unit_rows)
        return jnp.transpose(blocks, (1, 2, 0, 3)).reshape(rows, TEAM * units).astype(f32)

    def whole(blocks):
        return jnp.transpose(blocks, (1, 0, 2)).reshape(rows, -1).astype(f32)

    gate_grad = whole_units(mixer_columns[..., :units])
    up_grad = whole_units(mixer_columns[..., units:])
    attn_found, out_grad, gain_parts = order.step(attn_found, out_grad, gain_parts)
    gain_blocks = gain_parts.reshape(2, teams, TEAM, rows)
    gain_sums = dynamic(dynamic(gain_blocks, grid.team, 1), member, 1)
    for steps in range(1, teams):
        block = dynamic(dynamic(gain_blocks, (grid.team + steps) % teams, 1), member, 1)
        gain_sums = gain_sums + grid.shift(block, steps)
    out_grad = out_grad.astype(f32)
    attn_columns = in_order(attn_found)
    gain_sums = gain_sums + order.token[0, 0].astype(f32)
    return (
        outputs,
        input_grad,
        gain_sums[0],
        whole(attn_columns[..., :Q_WIDTH]),
        whole(attn_columns[..., Q_WIDTH : Q_WIDTH + KV_WIDTH]),
        whole(attn_columns[..., Q_WIDTH + KV_WIDTH :]),
        out_grad,
        gain_sums[1],
        gate_grad,
        up_grad,
        down_grad,
    )


def solution(mesh):
    matrix, vector = P("dev", None), P("dev")
    in_specs = (matrix, vector, vector) + (matrix,) * 4 + (vector,) + (matrix,) * 4
    out_specs = (matrix, matrix, vector) + (matrix,) * 4 + (vector,) + (matrix,) * 3
    return jax.shard_map(
        per_device, mesh=mesh, in_specs=in_specs, out_specs=out_specs, check_vma=False
    )
```

```python
import math

import jax
import jax.numpy as jnp
from jax import lax
from jax.experimental import pallas as pl
from jax.experimental.pallas import tpu as pltpu
from jax.sharding import PartitionSpec as P

HEADS = 16
KV_HEADS = 8
HEAD_DIM = 96
TEAM = 8

eps_norm = 1e-05
rope_base = 100000.0
masked_score = -1e30

OWN_HEADS = HEADS // TEAM
OWN_KV = KV_HEADS // TEAM
GROUP = HEADS // KV_HEADS
BLOCK = 256
LANES = 128
score_scale = 1.0 / math.sqrt(HEAD_DIM)
log2_scale = score_scale / math.log(2.0)
kernel_vmem = 56 * 1024 * 1024
small_cost = pl.CostEstimate(flops=1000, bytes_accessed=1000, transcendentals=0)

Q_WIDTH = OWN_HEADS * HEAD_DIM
KV_WIDTH = OWN_KV * HEAD_DIM
LINED = Q_WIDTH + 2 * KV_WIDTH


def relative(position):
    return 2 * (position % 4) + position // 4


def visible_mask(block, starts, ends):
    key = block * BLOCK + lax.broadcasted_iota(jnp.int32, (BLOCK, 1), 0)
    return (key >= starts) & (key <= ends)


def chunk_lanes(ref, chunk):
    spot = pl.ds(chunk * BLOCK, BLOCK)
    return jnp.concatenate([ref[head, :, spot] for head in range(GROUP)], axis=1)


def chunk_range(chunk, starts_ref, last):
    starts = starts_ref[:, pl.ds(chunk * BLOCK, BLOCK)]
    ends = last * BLOCK + lax.broadcasted_iota(jnp.int32, (1, BLOCK), 1)
    return (
        jnp.concatenate([starts] * GROUP, axis=1),
        jnp.concatenate([ends] * GROUP, axis=1),
    )


def attend_kernel(low_ref, starts_ref, query_ref, *refs):
    count = len(refs) - 4
    member = low_ref[TEAM]
    pieces = refs[:count]
    out_ref, norm_ref, keys, values = refs[count:]
    per_piece = pieces[0].shape[-1] // BLOCK
    for back, piece in enumerate(pieces):
        for part in range(per_piece):
            block = (count - 1 - back) * per_piece + (relative(part) ^ member)
            spot = pl.ds(part * BLOCK, BLOCK)
            keys[block] = piece[0, 0, :, spot].T
            values[block] = piece[1, 0, :, spot]
    own_block = (count - 1) * per_piece
    for chunk in range(per_piece):
        queries = chunk_lanes(query_ref, chunk)
        last = own_block + (relative(chunk) ^ member)
        starts, ends = chunk_range(chunk, starts_ref, last)

        def masked(block):
            held = jnp.maximum(block, 0)
            scores = jnp.dot(keys[held], queries, preferred_element_type=jnp.float32) * log2_scale
            return held, jnp.where(visible_mask(block, starts, ends), scores, masked_score)

        def advance(step, running):
            top, total, summed = running
            one, scores = masked(last - 2 * step)
            two, more = masked(last - 2 * step - 1)
            new_top = jnp.maximum(
                top, jnp.max(jnp.maximum(scores, more), axis=0, keepdims=True)
            )
            factor = jnp.exp2(top - new_top)
            weights, others = jnp.exp2(scores - new_top), jnp.exp2(more - new_top)
            total = total * factor + jnp.sum(weights + others, axis=0, keepdims=True)
            summed = summed * factor + (
                jnp.dot(
                    values[one], weights.astype(jnp.bfloat16), preferred_element_type=jnp.float32
                )
                + jnp.dot(
                    values[two], others.astype(jnp.bfloat16), preferred_element_type=jnp.float32
                )
            )
            return new_top, total, summed

        lanes = GROUP * BLOCK
        top, total, summed = lax.fori_loop(
            0,
            (last - low_ref[chunk] + 2) // 2,
            advance,
            (
                jnp.full((1, lanes), masked_score, jnp.float32),
                jnp.zeros((1, lanes), jnp.float32),
                jnp.zeros((HEAD_DIM, lanes), jnp.float32),
            ),
        )
        attended = summed / total
        norm = top + jnp.log2(total)
        spot = pl.ds(chunk * BLOCK, BLOCK)
        for head in range(GROUP):
            out_ref[head, :, spot] = attended[:, head * BLOCK : (head + 1) * BLOCK]
            norm_ref[head, :, spot] = norm[:, head * BLOCK : (head + 1) * BLOCK]


def gradient_kernel(low_ref, starts_ref, query_ref, grad_ref, out_ref, norm_ref, *refs):
    count = len(refs) - 8
    member = low_ref[TEAM]
    pieces = refs[:count]
    query_grad, own_grad, back_grad, keys, keys_t, values, key_sum, value_sum = refs[count:]
    per_piece = pieces[0].shape[-1] // BLOCK
    for back, piece in enumerate(pieces):
        for part in range(per_piece):
            block = (count - 1 - back) * per_piece + (relative(part) ^ member)
            spot = pl.ds(part * BLOCK, BLOCK)
            keys_t[block] = piece[0, 0, :, spot]
            keys[block] = piece[0, 0, :, spot].T
            values[block] = piece[1, 0, :, spot].T
    key_sum[...] = jnp.zeros_like(key_sum)
    value_sum[...] = jnp.zeros_like(value_sum)
    own_block = (count - 1) * per_piece
    rows_rows = (((1,), (1,)), ((), ()))
    for chunk in range(per_piece):
        queries = chunk_lanes(query_ref, chunk)
        grads = chunk_lanes(grad_ref, chunk)
        norm = chunk_lanes(norm_ref, chunk)
        delta = jnp.sum(
            grads.astype(jnp.float32) * chunk_lanes(out_ref, chunk), axis=0, keepdims=True
        )
        last = own_block + (relative(chunk) ^ member)
        starts, ends = chunk_range(chunk, starts_ref, last)

        def part(block):
            held = jnp.minimum(block, last)
            scores = jnp.dot(keys[held], queries, preferred_element_type=jnp.float32) * log2_scale
            scores = jnp.where(visible_mask(block, starts, ends), scores - norm, masked_score)
            probs = jnp.exp2(scores)
            slopes = jnp.dot(values[held], grads, preferred_element_type=jnp.float32)
            grad_scores = (probs * (slopes - delta)).astype(jnp.bfloat16)
            return held, probs.astype(jnp.bfloat16), grad_scores

        def advance(step, summed):
            found = [part(low_ref[chunk] + 2 * step), part(low_ref[chunk] + 2 * step + 1)]
            for held, probs, grad_scores in found:
                key_sum[held] += lax.dot_general(
                    queries, grad_scores, rows_rows, preferred_element_type=jnp.float32
                )
                value_sum[held] += lax.dot_general(
                    grads, probs, rows_rows, preferred_element_type=jnp.float32
                )
                summed = summed + jnp.dot(
                    keys_t[held], grad_scores, preferred_element_type=jnp.float32
                )
            return summed

        summed = lax.fori_loop(
            0,
            (last - low_ref[chunk] + 2) // 2,
            advance,
            jnp.zeros((HEAD_DIM, GROUP * BLOCK), jnp.float32),
        )
        spot = pl.ds(chunk * BLOCK, BLOCK)
        for head in range(GROUP):
            query_grad[head, :, spot] = (
                summed[:, head * BLOCK : (head + 1) * BLOCK] * score_scale
            )
    for back in range(count):
        for part in range(per_piece):
            block = (count - 1 - back) * per_piece + (relative(part) ^ member)
            spot = pl.ds(part * BLOCK, BLOCK)
            key_part = key_sum[block] * score_scale
            value_part = value_sum[block]
            if back == 0:
                own_grad[0, 0, :, spot] = key_part
                own_grad[1, 0, :, spot] = value_part
            else:
                back_grad[back - 1, 0, 0, :, spot] = key_part.astype(jnp.bfloat16)
                back_grad[back - 1, 1, 0, :, spot] = value_part.astype(jnp.bfloat16)


def attention_specs(tokens, pieces, first_head):
    whole = pl.BlockSpec((1, tokens), lambda head: (0, 0))
    low = pl.BlockSpec(memory_space=pltpu.SMEM)
    heads = pl.BlockSpec(
        (GROUP, HEAD_DIM, tokens), lambda head: (first_head + head, 0, 0)
    )
    norm = pl.BlockSpec((GROUP, 1, tokens), lambda head: (first_head + head, 0, 0))
    kv = pl.BlockSpec((2, 1, HEAD_DIM, tokens), lambda head: (0, first_head + head, 0, 0))
    return low, whole, heads, norm, [kv] * len(pieces)


def attend(low, starts, queries, pieces, first_head, count):
    tokens = queries.shape[-1]
    blocks = len(pieces) * tokens // BLOCK
    low_spec, whole, heads, norm, kv = attention_specs(tokens, pieces, first_head)
    return pl.pallas_call(
        attend_kernel,
        grid=(count,),
        in_specs=[low_spec, whole, heads] + kv,
        out_specs=[
            pl.BlockSpec((GROUP, HEAD_DIM, tokens), lambda head: (head, 0, 0)),
            pl.BlockSpec((GROUP, 1, tokens), lambda head: (head, 0, 0)),
        ],
        out_shape=[
            jax.ShapeDtypeStruct((count * GROUP, HEAD_DIM, tokens), jnp.float32),
            jax.ShapeDtypeStruct((count * GROUP, 1, tokens), jnp.float32),
        ],
        scratch_shapes=[
            pltpu.VMEM((blocks, BLOCK, HEAD_DIM), jnp.bfloat16),
            pltpu.VMEM((blocks, HEAD_DIM, BLOCK), jnp.bfloat16),
        ],
        compiler_params=pltpu.CompilerParams(vmem_limit_bytes=kernel_vmem),
        cost_estimate=small_cost,
    )(low, starts, queries, *pieces)


def attend_back(low, starts, queries, grads, attended, norm, pieces, first_head, count):
    tokens = queries.shape[-1]
    blocks = len(pieces) * tokens // BLOCK
    low_spec, whole, heads, norm_spec, kv = attention_specs(tokens, pieces, first_head)
    back = len(pieces) - 1
    return pl.pallas_call(
        gradient_kernel,
        grid=(count,),
        in_specs=[low_spec, whole, heads, heads, heads, norm_spec] + kv,
        out_specs=[
            pl.BlockSpec((GROUP, HEAD_DIM, tokens), lambda head: (head, 0, 0)),
            pl.BlockSpec((2, 1, HEAD_DIM, tokens), lambda head: (0, head, 0, 0)),
            pl.BlockSpec((back, 2, 1, HEAD_DIM, tokens), lambda head: (0, 0, head, 0, 0)),
        ],
        out_shape=[
            jax.ShapeDtypeStruct((count * GROUP, HEAD_DIM, tokens), jnp.float32),
            jax.ShapeDtypeStruct((2, count, HEAD_DIM, tokens), jnp.float32),
            jax.ShapeDtypeStruct((back, 2, count, HEAD_DIM, tokens), jnp.bfloat16),
        ],
        scratch_shapes=[
            pltpu.VMEM((blocks, BLOCK, HEAD_DIM), jnp.bfloat16),
            pltpu.VMEM((blocks, HEAD_DIM, BLOCK), jnp.bfloat16),
            pltpu.VMEM((blocks, BLOCK, HEAD_DIM), jnp.bfloat16),
            pltpu.VMEM((blocks, HEAD_DIM, BLOCK), jnp.float32),
            pltpu.VMEM((blocks, HEAD_DIM, BLOCK), jnp.float32),
        ],
        compiler_params=pltpu.CompilerParams(vmem_limit_bytes=kernel_vmem),
        cost_estimate=small_cost,
    )(low, starts, queries, grads, attended, norm, *pieces)

class Order:
    def __init__(self, token):
        self.token = token

    def step(self, *values):
        self.token, tied = lax.optimization_barrier((self.token, values))
        return tied[0] if len(tied) == 1 else tied


class Grid:
    def __init__(self):
        self.count = lax.axis_size("dev")
        self.teams = self.count // TEAM
        index = lax.axis_index("dev")
        self.member = index % TEAM
        self.team = index // TEAM

    def places(self):
        return jnp.stack([self.team, self.member]).astype(jnp.int32)

    def turn(self, value, bits):
        return lax.ppermute(value, "dev", [(d, d ^ bits) for d in range(self.count)])

    def shift(self, value, steps, around=True):
        pairs = []
        for device in range(self.count):
            target = device + steps * TEAM
            if around or 0 <= target < self.count:
                pairs.append((device, target % self.count))
        return lax.ppermute(value, "dev", pairs)

    def spread(self, value):
        return [value] + [self.shift(value, steps) for steps in range(1, self.teams)]

    def both_ways(self, ahead, behind):
        return self.shift(ahead, 1, False), self.shift(behind, -1, False)

    def gather_team(self, blocks):
        return list(blocks) + [self.turn(block, 1) for block in blocks]

    def chips(self, block):
        return [block] + [self.turn(block, 2 * chip) for chip in range(1, 4)]

    def to_members(self, value):
        pairs = [
            (owner, owner % self.teams * TEAM + owner // self.teams)
            for owner in range(self.count)
        ]
        return lax.ppermute(value, "dev", pairs)

    def to_owners(self, value):
        pairs = [
            (owner % self.teams * TEAM + owner // self.teams, owner)
            for owner in range(self.count)
        ]
        return lax.ppermute(value, "dev", pairs)

    def send_chips(self, blocks):
        return [self.turn(block, 2 * chip) for chip, block in enumerate(blocks, 1)]


def call(kernel, grid, in_specs, out_specs, out_shape, scratch=(), prefetch=0):
    return pl.pallas_call(
        kernel,
        out_shape=out_shape,
        grid_spec=pltpu.PrefetchScalarGridSpec(
            num_scalar_prefetch=prefetch,
            grid=grid,
            in_specs=in_specs,
            out_specs=out_specs,
            scratch_shapes=list(scratch),
        ),
        compiler_params=pltpu.CompilerParams(vmem_limit_bytes=kernel_vmem),
        cost_estimate=small_cost,
    )


def fixed(array):
    return pl.BlockSpec(array.shape, lambda *unused: (0,) * array.ndim)


def lanes_at(rows, step_width):
    return pl.BlockSpec((rows, step_width), lambda p, *unused: (0, p))


def rows_at(step_rows, width):
    return pl.BlockSpec((step_rows, width), lambda p, *unused: (p, 0))


def kept_given(rows, width, axis):
    def index(at):
        return (0, at) if axis else (at, 0)

    specs = [
        pl.BlockSpec((rows, width), lambda p, *unused: index(jnp.minimum(p, 3))),
        pl.BlockSpec((rows, width), lambda p, *unused: index(jnp.maximum(p - 4, 0))),
    ]
    shape = (rows, 4 * width) if axis else (4 * rows, width)
    shapes = [
        jax.ShapeDtypeStruct(shape, jnp.float32),
        jax.ShapeDtypeStruct(shape, jnp.bfloat16),
    ]
    return specs, shapes


def keep_or_give(position, keep_ref, give_ref, value):
    @pl.when(position < 4)
    def keep():
        keep_ref[...] = value

    @pl.when(position >= 4)
    def give():
        give_ref[...] = value.astype(give_ref.dtype)


def pick(position, refs, target):
    for number in range(TEAM):

        @pl.when(position == number)
        def move():
            if len(refs) == TEAM:
                target[...] = refs[number][...]
            else:
                target[...] = refs[number // 4][number % 4]


def dot_rows(left, right):
    return lax.dot_general(
        left, right, (((1,), (1,)), ((), ())), preferred_element_type=jnp.float32
    )


def dot(left, right):
    return jnp.dot(left, right, preferred_element_type=jnp.float32)


def place_rows(grid, blocks, start, stop):
    count = len(blocks)
    positions, rows = blocks[0].shape[:2]
    width = stop - start

    def kernel(places_ref, *refs):
        target = refs[-1]
        for number, ref in enumerate(refs[:-1]):

            @pl.when(pl.program_id(0) == number)
            def move():
                for position in range(positions):
                    at = relative(position) ^ places_ref[1] if positions > 1 else 0
                    target[0, pl.ds(at, 1)] = ref[position : position + 1, :, start:stop]

    def target_map(step, places_ref):
        return ((places_ref[0] + count - step) % count, 0, 0, 0)

    return call(
        kernel,
        (count,),
        [fixed(block) for block in blocks],
        pl.BlockSpec((1, positions, rows, width), target_map),
        jax.ShapeDtypeStruct((count, positions, rows, width), blocks[0].dtype),
        prefetch=1,
    )(grid.places(), *blocks)


def place_mixer(grid, own, hops, units, unit_rows):
    count = grid.teams
    positions, rows, wide = own.shape
    third = wide - 2 * units
    sources = [own] + [block for hop in hops for block in hop]

    def kernel(places_ref, *refs):
        mixer_ref, down_ref = refs[-2:]
        team = places_ref[0]

        def move(ref):
            for position in range(positions):
                at = relative(position) ^ places_ref[1]
                mixer_ref[0, pl.ds(at, 1)] = ref[position : position + 1, :, : 2 * units]
                row = position * rows
                while row < (position + 1) * rows:
                    part = row // unit_rows
                    stop = min((part + 1) * unit_rows, (position + 1) * rows)
                    down_ref[
                        0,
                        row - part * unit_rows : stop - part * unit_rows,
                        part * third : (part + 1) * third,
                    ] = ref[position, row - position * rows : stop - position * rows, 2 * units :]
                    row = stop

        for steps in range(count):
            here = pl.program_id(0) == steps
            if steps == 0:
                pl.when(here)(lambda: move(refs[0]))
            else:
                ahead, behind = refs[2 * steps - 1], refs[2 * (count - steps)]
                pl.when(here & (team >= steps))(lambda ahead=ahead: move(ahead))
                pl.when(here & (team < steps))(lambda behind=behind: move(behind))

    def target_map(step, places_ref):
        return (places_ref[0] + count - step) % count

    return call(
        kernel,
        (count,),
        [fixed(source) for source in sources],
        [
            pl.BlockSpec(
                (1, positions, rows, 2 * units), lambda s, p: (target_map(s, p), 0, 0, 0)
            ),
            pl.BlockSpec((1, unit_rows, 3 * third), lambda s, p: (target_map(s, p), 0, 0)),
        ],
        [
            jax.ShapeDtypeStruct((count, positions, rows, 2 * units), own.dtype),
            jax.ShapeDtypeStruct((count, unit_rows, 3 * third), own.dtype),
        ],
        prefetch=1,
    )(grid.places(), *sources)


def project(inputs_t, weights, cosine, sine_table):
    width, own = inputs_t[0].shape
    tokens = TEAM * own
    half = HEAD_DIM // 2

    def kernel(weights_ref, cosine_ref, sine_ref, *refs):
        sources = refs[:TEAM]
        normed_ref, query_ref, kv_ref, chosen, turned = refs[TEAM:]
        position = pl.program_id(0)

        @pl.when(position == 0)
        def prepare():
            turned[...] = weights_ref[:, :LINED].T

        pick(position, sources, chosen)
        values = chosen[...].astype(jnp.float32)
        scale = lax.rsqrt(jnp.mean(values * values, axis=0, keepdims=True) + eps_norm)
        gain = weights_ref[:, LINED : LINED + 1].astype(jnp.float32)
        normed = (values * scale * gain).astype(jnp.bfloat16)
        normed_ref[...] = normed
        lined = dot(turned[...], normed)
        cosines, sines = cosine_ref[...], sine_ref[...]

        def rotated(head):
            block = lined[head * HEAD_DIM : (head + 1) * HEAD_DIM]
            shifted = jnp.concatenate([-block[half:], block[:half]], axis=0)
            return (block * cosines + shifted * sines).astype(jnp.bfloat16)

        for head in range(OWN_HEADS):
            query_ref[head] = rotated(head)
        for head in range(OWN_KV):
            kv_ref[0, head] = rotated(OWN_HEADS + head)
            start = Q_WIDTH + KV_WIDTH + head * HEAD_DIM
            kv_ref[1, head] = lined[start : start + HEAD_DIM].astype(jnp.bfloat16)

    return call(
        kernel,
        (TEAM,),
        [fixed(weights), lanes_at(HEAD_DIM, own), lanes_at(HEAD_DIM, own)]
        + [fixed(block) for block in inputs_t],
        [
            lanes_at(width, own),
            pl.BlockSpec((OWN_HEADS, HEAD_DIM, own), lambda p: (0, 0, p)),
            pl.BlockSpec((2, OWN_KV, HEAD_DIM, own), lambda p: (0, 0, 0, p)),
        ],
        [
            jax.ShapeDtypeStruct((width, tokens), jnp.bfloat16),
            jax.ShapeDtypeStruct((OWN_HEADS, HEAD_DIM, tokens), jnp.bfloat16),
            jax.ShapeDtypeStruct((2, OWN_KV, HEAD_DIM, tokens), jnp.bfloat16),
        ],
        [
            pltpu.VMEM((width, own), jnp.bfloat16),
            pltpu.VMEM((LINED, width), jnp.bfloat16),
        ],
    )(weights, cosine, sine_table, *inputs_t)


def project_out(attended, out_rows):
    tokens = attended.shape[-1]
    own = tokens // TEAM
    width = out_rows.shape[1]
    specs, shapes = kept_given(width, own, 1)

    def kernel(attended_ref, rows_ref, keep_ref, give_ref, turned):
        position = pl.program_id(0)

        @pl.when(position == 0)
        def prepare():
            turned[...] = rows_ref[...].T

        block = attended_ref[...].reshape(Q_WIDTH, own).astype(jnp.bfloat16)
        keep_or_give(position, keep_ref, give_ref, dot(turned[...], block))

    return call(
        kernel,
        (TEAM,),
        [pl.BlockSpec((OWN_HEADS, HEAD_DIM, own), lambda p: (0, 0, p)), fixed(out_rows)],
        specs,
        shapes,
        [pltpu.VMEM((width, Q_WIDTH), jnp.bfloat16)],
    )(attended, out_rows)


def mixer(chip, normed, cotangent, weights, down):
    width, own = normed[0].shape
    units = down.shape[0]

    def kernel(first_ref, second_ref, wanted_a, wanted_b, weights_ref, down_ref, *refs):
        hidden_ref, grad_ref, keep_ref, give_ref, turned, wanted = refs
        step = pl.program_id(0)

        @pl.when(step == 0)
        def first():
            turned[...] = first_ref[...].T
            wanted[...] = wanted_a[0]

        @pl.when(step == 1)
        def second():
            turned[...] = second_ref[...].T
            wanted[...] = wanted_b[0]

        gate = dot(turned[...], weights_ref[:, :units])
        up = dot(turned[...], weights_ref[:, units:])
        logistic = 1.0 / (1.0 + jnp.exp(-gate))
        silu = gate * logistic
        hidden_ref[...] = (silu * up).astype(jnp.bfloat16)
        grad_hidden = dot_rows(wanted[...], down_ref[...])
        grad_ref[:, :units] = (
            grad_hidden * up * (logistic * (1.0 + gate * (1.0 - logistic)))
        ).astype(jnp.bfloat16)
        grad_ref[:, units:] = (grad_hidden * silu).astype(jnp.bfloat16)
        term = dot_rows(weights_ref[...], grad_ref[...])

        @pl.when(step == 0)
        def keep():
            keep_ref[...] = term

        @pl.when(step == 1)
        def give():
            give_ref[...] = term.astype(jnp.bfloat16)

    block = pl.BlockSpec((1, own, width), lambda p: (chip, 0, 0))
    whole = pl.BlockSpec((width, own), lambda p: (0, 0))
    return call(
        kernel,
        (2,),
        [fixed(normed[0]), fixed(normed[1]), block, block, fixed(weights), fixed(down)],
        [rows_at(own, units), rows_at(own, 2 * units), whole, whole],
        [
            jax.ShapeDtypeStruct((2 * own, units), jnp.bfloat16),
            jax.ShapeDtypeStruct((2 * own, 2 * units), jnp.bfloat16),
            jax.ShapeDtypeStruct((width, own), jnp.float32),
            jax.ShapeDtypeStruct((width, own), jnp.bfloat16),
        ],
        [pltpu.VMEM((own, width), jnp.bfloat16), pltpu.VMEM((own, width), jnp.bfloat16)],
    )(normed[0], normed[1], cotangent[0], cotangent[1], weights, down)


def add_block(keep, arrived):
    def kernel(keep_ref, arrived_ref, out_ref):
        out_ref[...] = (keep_ref[...] + arrived_ref[...].astype(jnp.float32)).astype(jnp.bfloat16)

    rows = keep.shape[0] // 2
    part = rows_at(rows, keep.shape[1])
    return call(
        kernel, (2,), [part, part], part, jax.ShapeDtypeStruct(keep.shape, jnp.bfloat16)
    )(keep, arrived)


def pair_rows(position, refs, target):
    own = target.shape[0]
    for number in range(TEAM):

        @pl.when(position == number)
        def move():
            start = number // 4 * own
            target[...] = refs[number % 4][start : start + own]


def mixer_output(hidden, down):
    own, units = hidden[0].shape[0] // 2, hidden[0].shape[1]
    specs, shapes = kept_given(own, down.shape[1], 0)

    def kernel(down_ref, *refs):
        keep_ref, give_ref, chosen = refs[4:]
        pair_rows(pl.program_id(0), refs[:4], chosen)
        keep_or_give(pl.program_id(0), keep_ref, give_ref, dot(chosen[...], down_ref[...]))

    return call(
        kernel,
        (TEAM,),
        [fixed(down)] + [fixed(block) for block in hidden],
        specs,
        shapes,
        [pltpu.VMEM((own, units), jnp.bfloat16)],
    )(down, *hidden)


def write_teams(places_ref, total, out_ref, teams):
    rows = total.shape[0] // teams
    for team in range(teams):
        steps = (team + teams - places_ref[0]) % teams
        block = total[team * rows : (team + 1) * rows, :].astype(out_ref.dtype)
        out_ref[pl.ds(steps, 1)] = block[None]


def token_product(grid, lefts, rights):
    rows, own = lefts[0].shape
    width = rights[0].shape[1]
    teams = grid.teams

    def kernel(places_ref, *refs):
        left_refs, right_refs = refs[:TEAM], refs[TEAM : TEAM + 4]
        out_ref, total, chosen = refs[TEAM + 4 :]
        position = pl.program_id(0)
        pair_rows(position, right_refs, chosen)

        def add(value):
            @pl.when(position == 0)
            def first():
                total[...] = value

            @pl.when(position > 0)
            def later():
                total[...] += value

        for number, source in enumerate(left_refs):

            @pl.when(position == number)
            def block():
                add(dot(source[...], chosen[...]))

        @pl.when(position == TEAM - 1)
        def last():
            write_teams(places_ref, total, out_ref, teams)

    return call(
        kernel,
        (TEAM,),
        [fixed(block) for block in list(lefts) + list(rights)],
        pl.BlockSpec((teams, rows // teams, width), lambda p, *unused: (0, 0, 0)),
        jax.ShapeDtypeStruct((teams, rows // teams, width), jnp.bfloat16),
        [pltpu.VMEM((rows, width), jnp.float32), pltpu.VMEM((own, width), jnp.bfloat16)],
        prefetch=1,
    )(grid.places(), *lefts, *rights)


def down_product(grid, hidden, cotangent):
    units = hidden[0].shape[1]
    own, width = cotangent[0].shape[1:]
    teams = grid.teams

    def kernel(places_ref, *refs):
        hidden_refs, sources, (out_ref, total, wanted, chosen) = refs[:4], refs[4:6], refs[6:]
        position = pl.program_id(0)
        pick(position, sources, wanted)
        pair_rows(position, hidden_refs, chosen)
        value = dot(chosen[...].T, wanted[...])

        @pl.when(position == 0)
        def first():
            total[...] = value

        @pl.when(position > 0)
        def later():
            total[...] += value

        @pl.when(position == TEAM - 1)
        def last():
            write_teams(places_ref, total, out_ref, teams)

    return call(
        kernel,
        (TEAM,),
        [fixed(block) for block in list(hidden) + list(cotangent)],
        pl.BlockSpec((teams, units // teams, width), lambda p, *unused: (0, 0, 0)),
        jax.ShapeDtypeStruct((teams, units // teams, width), jnp.bfloat16),
        [
            pltpu.VMEM((units, width), jnp.float32),
            pltpu.VMEM((own, width), jnp.bfloat16),
            pltpu.VMEM((own, units), jnp.bfloat16),
        ],
        prefetch=1,
    )(grid.places(), *hidden, *cotangent)


def project_out_back(grid, grads, out_rows, attended):
    teams = grid.teams
    tokens = attended.shape[-1]
    own = tokens // TEAM
    width = out_rows.shape[1]

    def kernel(places_ref, rows_ref, attended_ref, *refs):
        sources, (grad_ref, out_ref, chosen, total) = refs[:TEAM], refs[TEAM:]
        position = pl.program_id(0)
        pick(position, sources, chosen)
        grad_ref[...] = (
            dot(rows_ref[...], chosen[...])
            .astype(jnp.bfloat16)
            .reshape(OWN_HEADS, HEAD_DIM, own)
        )
        block = attended_ref[...].reshape(Q_WIDTH, own).astype(jnp.bfloat16)
        value = dot_rows(block, chosen[...])

        @pl.when(position == 0)
        def first():
            total[...] = value

        @pl.when(position > 0)
        def later():
            total[...] += value

        @pl.when(position == TEAM - 1)
        def last():
            write_teams(places_ref, total, out_ref, teams)

    heads = pl.BlockSpec((OWN_HEADS, HEAD_DIM, own), lambda p, *unused: (0, 0, p))
    shape = (teams, Q_WIDTH // teams, width)
    return call(
        kernel,
        (TEAM,),
        [fixed(out_rows), heads] + [fixed(block) for block in grads],
        [heads, pl.BlockSpec(shape, lambda p, *unused: (0, 0, 0))],
        [
            jax.ShapeDtypeStruct((OWN_HEADS, HEAD_DIM, tokens), jnp.bfloat16),
            jax.ShapeDtypeStruct(shape, jnp.bfloat16),
        ],
        [pltpu.VMEM((width, own), jnp.bfloat16), pltpu.VMEM((Q_WIDTH, width), jnp.float32)],
        prefetch=1,
    )(grid.places(), out_rows, attended, *grads)


def project_back(grid, normed, query_rot, own_grads, returned, cosine, sine_table, weights):
    width, tokens = normed.shape
    own = tokens // TEAM
    half = HEAD_DIM // 2
    teams = grid.teams
    specs, shapes = kept_given(width, own, 1)

    def kernel(places_ref, normed_ref, query_ref, cosine_ref, sine_ref, weights_ref, *refs):
        kv_refs = refs[: 1 + len(returned)]
        keep_ref, give_ref, out_ref, total, grad_ref = refs[1 + len(returned) :]
        position = pl.program_id(0)
        cosines, sines = cosine_ref[...], sine_ref[...]

        def unrotated(block):
            scaled = block * sines
            shifted = jnp.concatenate([scaled[half:], -scaled[:half]], axis=0)
            return (block * cosines + shifted).astype(jnp.bfloat16)

        for head in range(OWN_HEADS):
            grad_ref[head * HEAD_DIM : (head + 1) * HEAD_DIM] = unrotated(query_ref[head])
        kv = kv_refs[0][...]
        for ref in kv_refs[1:]:
            kv = kv + ref[...].astype(jnp.float32)
        for head in range(OWN_KV):
            start = Q_WIDTH + head * HEAD_DIM
            grad_ref[start : start + HEAD_DIM] = unrotated(kv[0, head])
            start = start + KV_WIDTH
            grad_ref[start : start + HEAD_DIM] = kv[1, head].astype(jnp.bfloat16)
        grad = grad_ref[...]
        keep_or_give(position, keep_ref, give_ref, dot(weights_ref[:, :LINED], grad))
        value = dot_rows(normed_ref[...], grad)

        @pl.when(position == 0)
        def first():
            total[...] = value

        @pl.when(position > 0)
        def later():
            total[...] += value

        @pl.when(position == TEAM - 1)
        def last():
            write_teams(places_ref, total, out_ref, teams)

    heads = pl.BlockSpec((OWN_HEADS, HEAD_DIM, own), lambda p, *unused: (0, 0, p))
    kv_heads = pl.BlockSpec((2, OWN_KV, HEAD_DIM, own), lambda p, *unused: (0, 0, 0, p))
    return call(
        kernel,
        (TEAM,),
        [
            lanes_at(width, own),
            heads,
            lanes_at(HEAD_DIM, own),
            lanes_at(HEAD_DIM, own),
            fixed(weights),
        ]
        + [kv_heads] * (1 + len(returned)),
        specs + [pl.BlockSpec((teams, width // teams, LINED), lambda p, *unused: (0, 0, 0))],
        shapes + [jax.ShapeDtypeStruct((teams, width // teams, LINED), jnp.bfloat16)],
        [pltpu.VMEM((width, LINED), jnp.float32), pltpu.VMEM((LINED, own), jnp.bfloat16)],
        prefetch=1,
    )(grid.places(), normed, query_rot, cosine, sine_table, weights, own_grads, *returned)


def combine(keep, arrived, axis):
    size = keep.shape[axis] // 4
    shape = (keep.shape[0], size) if axis else (size, keep.shape[1])

    def kernel(keep_ref, arrived_ref, own_ref, *block_refs):
        position = pl.program_id(0)
        total = keep_ref[...] + arrived_ref[...].astype(jnp.float32)

        @pl.when(position == 0)
        def own():
            own_ref[...] = total

        for number, ref in enumerate(block_refs, 1):

            @pl.when(position == number)
            def other():
                ref[...] = total.astype(jnp.bfloat16)

    part = pl.BlockSpec(shape, (lambda p: (0, p)) if axis else (lambda p: (p, 0)))
    whole = pl.BlockSpec(shape, lambda p: (0, 0))
    own, *blocks = call(
        kernel,
        (4,),
        [part, part],
        [whole] * 4,
        [jax.ShapeDtypeStruct(shape, jnp.float32)]
        + [jax.ShapeDtypeStruct(shape, jnp.bfloat16)] * 3,
    )(keep, arrived)
    return own, blocks


def summed(refs):
    total = refs[0][...]
    for ref in refs[1:]:
        total = total + ref[...].astype(jnp.float32)
    return total


def finish(kernel, arrays, shapes):
    return call(
        kernel,
        (1,),
        [fixed(array) for array in arrays],
        [pl.BlockSpec(shape.shape, lambda p: (0, 0)) for shape in shapes],
        shapes,
    )(*arrays)


def finish_middle(terms, inputs_t, gain):
    def kernel(*refs):
        inputs_ref, gain_ref, middle_ref, normed_ref = refs[len(terms) :]
        middle = inputs_ref[...].astype(jnp.float32) + summed(refs[: len(terms)])
        middle_ref[...] = middle
        scale = lax.rsqrt(jnp.mean(middle * middle, axis=0, keepdims=True) + eps_norm)
        normed_ref[...] = (middle * scale * gain_ref[...]).astype(jnp.bfloat16)

    shape = inputs_t.shape
    return finish(
        kernel,
        list(terms) + [inputs_t, gain],
        [jax.ShapeDtypeStruct(shape, jnp.float32), jax.ShapeDtypeStruct(shape, jnp.bfloat16)],
    )


def norm_back(values, gain, grad):
    inverse = lax.rsqrt(jnp.mean(values * values, axis=0, keepdims=True) + eps_norm)
    normal = values * inverse
    scaled = grad * gain
    inner = jnp.mean(scaled * normal, axis=0, keepdims=True)
    return inverse * (scaled - normal * inner), jnp.sum(grad * normal, axis=1, keepdims=True)


def finish_second(terms, middle, cotangent, gain):
    def kernel(*refs):
        middle_ref, cotangent_ref, gain_ref, grad_ref, attn_ref, gain_out = refs[len(terms) :]
        norm_grad, gain_part = norm_back(
            middle_ref[...], gain_ref[...], summed(refs[: len(terms)])
        )
        grad = cotangent_ref[...].T.astype(jnp.float32) + norm_grad
        grad_ref[...] = grad
        attn_ref[...] = grad.astype(jnp.bfloat16)
        gain_out[...] = gain_part

    shape = middle.shape
    return finish(
        kernel,
        list(terms) + [middle, cotangent, gain],
        [
            jax.ShapeDtypeStruct(shape, jnp.float32),
            jax.ShapeDtypeStruct(shape, jnp.bfloat16),
            jax.ShapeDtypeStruct((shape[0], 1), jnp.float32),
        ],
    )


def finish_first(terms, inputs_t, grad_middle, gain):
    def kernel(*refs):
        inputs_ref, grad_ref, gain_ref, out_ref, gain_out = refs[len(terms) :]
        norm_grad, gain_part = norm_back(
            inputs_ref[...].astype(jnp.float32), gain_ref[...], summed(refs[: len(terms)])
        )
        out_ref[...] = (grad_ref[...] + norm_grad).T
        gain_out[...] = gain_part

    width, own = inputs_t.shape
    return finish(
        kernel,
        list(terms) + [inputs_t, grad_middle, gain],
        [
            jax.ShapeDtypeStruct((own, width), jnp.float32),
            jax.ShapeDtypeStruct((width, 1), jnp.float32),
        ],
    )


def finish_output(terms, middle):
    def kernel(*refs):
        middle_ref, out_ref = refs[len(terms) :]
        out_ref[...] = (middle_ref[...].T + summed(refs[: len(terms)])).astype(jnp.bfloat16)

    return finish(
        kernel, list(terms) + [middle], [jax.ShapeDtypeStruct(terms[0].shape, jnp.bfloat16)]
    )[0]


def sum_teams(product, parts, kind):
    def kernel(own_ref, *refs):
        total = own_ref[0].astype(jnp.float32)
        for ref in refs[:-1]:
            total = total + ref[...].astype(jnp.float32)
        refs[-1][...] = total.astype(kind)

    shape = product.shape[1:]
    return call(
        kernel,
        (1,),
        [pl.BlockSpec((1,) + shape, lambda p: (0, 0, 0))] + [fixed(part) for part in parts],
        pl.BlockSpec(shape, lambda p: (0, 0)),
        jax.ShapeDtypeStruct(shape, kind),
    )(product, *parts)


def rope_tables(positions):
    half_dim = HEAD_DIM // 2
    frequency = rope_base ** (-(jnp.arange(half_dim, dtype=jnp.float32) * 2.0 / HEAD_DIM))
    angles = frequency[:, None] * positions.astype(jnp.float32)[None, :]
    angles = jnp.concatenate([angles, angles], axis=0)
    return (jnp.cos(angles), jnp.sin(angles))


def per_device(
    inputs,
    positions,
    norm_first,
    query_weight,
    key_weight,
    value_weight,
    out_weight,
    norm_second,
    gate_weight,
    up_weight,
    down_weight,
    cotangent,
):
    grid = Grid()
    member, teams = grid.member, grid.teams
    chip, core = member // 2, member % 2
    own, width = inputs.shape
    tokens = own * TEAM
    rows = query_weight.shape[0]
    unit_rows = down_weight.shape[0]
    units = unit_rows * teams
    longest = own * grid.count // 4
    steps_back = min((longest - 2) // tokens + 1, teams - 1)
    bf16, f32 = jnp.bfloat16, jnp.float32
    order = Order(jnp.zeros((8, 128), jnp.int32))

    def dynamic(array, index, axis=0):
        return lax.dynamic_index_in_dim(array, index, axis, keepdims=False)

    def by_member(weight):
        return jnp.transpose(weight.reshape(rows, TEAM, -1), (1, 0, 2))

    def units_by_member(weight):
        blocks = jnp.transpose(weight.reshape(rows, teams, TEAM, unit_rows), (2, 0, 1, 3))
        return blocks.reshape(TEAM, rows, units)

    gains = jnp.pad(jnp.stack([norm_first, norm_second], axis=1), ((0, 0), (0, LANES - 2)))
    columns = jnp.concatenate(
        [
            by_member(query_weight),
            by_member(key_weight),
            by_member(value_weight),
            jnp.broadcast_to(gains[None], (TEAM, rows, LANES)),
            units_by_member(gate_weight),
            units_by_member(up_weight),
        ],
        axis=-1,
    )
    attn_wide = LINED + LANES
    columns = columns.reshape(TEAM // 2, 2, rows, attn_wide + 2 * units)
    position_chips = jnp.stack(grid.chips(positions))
    all_positions = jnp.concatenate([position_chips, grid.turn(position_chips, 1)]).reshape(tokens)
    inputs_t = inputs.T
    columns, inputs_t = order.step(columns, inputs_t)
    pairs = [
        dynamic(columns, chip)
        if other == 0
        else grid.turn(dynamic(columns, chip ^ other), 2 * other)
        for other in range(4)
    ]
    inputs_two = [grid.turn(inputs_t, 2), grid.turn(inputs_t, 4)]
    cosine, sine_table = rope_tables(all_positions)
    block_index = steps_back * TEAM + (
        jnp.array([relative(p) for p in range(TEAM)], jnp.int32) ^ member
    )
    token_index = (block_index[:, None] * own + jnp.arange(own, dtype=jnp.int32)).reshape(tokens)
    starts = token_index - all_positions
    low = jnp.concatenate([starts[::own] // BLOCK, member[None]]).astype(jnp.int32)
    starts = starts[None]
    third = width // 3
    down_thirds = jnp.concatenate(
        [down_weight[:, part * third : (part + 1) * third] for part in range(3)], axis=0
    ).reshape(TEAM, rows, third)
    cosine, sine_table, starts, low, down_thirds, pairs, inputs_two, inputs_t, out_weight = (
        order.step(
            cosine, sine_table, starts, low, down_thirds, pairs, inputs_two, inputs_t, out_weight
        )
    )
    inputs_three = grid.turn(inputs_t, 6)
    out_own = grid.to_members(out_weight)
    pairs = jnp.stack(pairs)
    pairs_keep, pairs_give = dynamic(pairs, core, 1), dynamic(pairs, 1 - core, 1)
    team_rows = jnp.concatenate([pairs_keep, grid.turn(pairs_give, 1)], axis=0)
    attn_rows, team_rows = order.step(team_rows[..., :attn_wide], team_rows)
    attn_z = grid.spread(attn_rows)
    inputs_others = [grid.turn(block, 1) for block in [inputs_t] + inputs_two]
    attn_z, inputs_three, out_own = order.step(attn_z, inputs_three, out_own)
    inputs_others = inputs_others + [grid.turn(inputs_three, 1)]
    inputs_team = [inputs_t] + inputs_two + [inputs_three] + inputs_others
    attn_w = place_rows(grid, attn_z, 0, attn_wide).reshape(width, attn_wide)
    attn_w, inputs_team = order.step(attn_w, inputs_team)

    normed_first, queries, own_piece = project(inputs_team, attn_w, cosine, sine_table)
    own_piece, out_own, attn_w = order.step(own_piece, out_own, attn_w)
    arrived = [grid.shift(own_piece, step, False) for step in range(1, steps_back + 1)]
    out_z = grid.spread(out_own)
    gain_first = attn_w[:, LINED : LINED + 1].astype(f32)
    gain_second = attn_w[:, LINED + 1 : LINED + 2].astype(f32)
    mixer_own = jnp.concatenate([team_rows[..., attn_wide:], down_thirds], axis=-1)
    arrived, gain_first, gain_second, mixer_own, out_z, cotangent = order.step(
        arrived, gain_first, gain_second, mixer_own, out_z, cotangent
    )

    mixer_hops = [grid.both_ways(mixer_own, mixer_own)]

    def next_hop():
        if len(mixer_hops) < teams - 1:
            mixer_hops.append(grid.both_ways(*mixer_hops[-1]))

    cotangent_chips = grid.chips(cotangent)
    out_rows = place_rows(grid, [block[None] for block in out_z], 0, width)
    out_rows = out_rows.reshape(Q_WIDTH, width)
    pieces = [own_piece] + arrived
    attended, normalizer = attend(low, starts, queries, pieces, 0, OWN_KV)
    keep, give = project_out(attended, out_rows)
    give, mixer_hops[0], cotangent_chips = order.step(give, mixer_hops[0], cotangent_chips)
    other = grid.turn(give, 1)
    next_hop()
    cotangent_stack = jnp.stack(cotangent_chips)
    other, cotangent_stack = order.step(other, cotangent_stack)
    cotangent_other = grid.turn(cotangent_stack, 1)
    total, blocks = combine(keep, other, 1)
    blocks, cotangent_other = order.step(blocks, cotangent_other)
    cotangent_team = [cotangent_stack, cotangent_other]
    near = [grid.turn(blocks[0], 2), grid.turn(blocks[1], 4)]
    near, far, mixer_hops[-1] = order.step(near, blocks[2], mixer_hops[-1])
    terms = near + [grid.turn(far, 6)]
    next_hop()
    terms = order.step(terms)
    middle, normed_second = finish_middle([total] + terms, inputs_t, gain_second)
    normed_second, mixer_hops[-1] = order.step(normed_second, mixer_hops[-1])
    while len(mixer_hops) < teams - 1:
        next_hop()
        mixer_hops[-1] = order.step(mixer_hops[-1])
    second_chips = [normed_second, grid.turn(normed_second, 2), grid.turn(normed_second, 4)]
    second_other = [grid.turn(normed_second, 1)]
    mixer_w, down_w = place_mixer(grid, mixer_own, mixer_hops, units, unit_rows)
    mixer_w = mixer_w.reshape(width, 2 * units)
    down_w = down_w.reshape(units, width)
    mixer_w, down_w, second_other[0] = order.step(mixer_w, down_w, second_other[0])

    def send_teams(product, first=1, last=teams):
        return [grid.shift(product[steps], steps) for steps in range(first, last)]

    def run_mixer(other_chip):
        hidden_part, grads_part, keep, give = mixer(
            other_chip,
            (second_chips[other_chip], second_other[other_chip]),
            cotangent_team,
            mixer_w,
            down_w,
        )
        return hidden_part, grads_part, keep, order.step(give)

    parts = [run_mixer(0)]
    passed = [grid.turn(parts[0][3], 1)]
    second_chips = order.step(second_chips)
    second_chips = second_chips + [grid.turn(second_chips[0], 6)]
    second_other += order.step([grid.turn(second_chips[1], 1), grid.turn(second_chips[2], 1)])
    parts.append(run_mixer(1))
    passed.append(grid.turn(parts[1][3], 1))
    second_chips[3], passed[0] = order.step(second_chips[3], passed[0])
    second_other.append(grid.turn(second_chips[3], 1))
    parts.append(run_mixer(2))
    passed[1], second_other[3] = order.step(passed[1], second_other[3])
    block = order.step(add_block(parts[1][2], passed[1]))
    terms = [parts[0][2], passed[0], grid.turn(block, 2)]
    passed.append(grid.turn(parts[2][3], 1))
    parts.append(run_mixer(3))
    passed[2] = order.step(passed[2])
    passed.append(grid.turn(parts[3][3], 1))
    block = order.step(add_block(parts[2][2], passed[2]))
    terms.append(grid.turn(block, 4))
    passed[3] = order.step(passed[3])
    hidden, grads = [part[0] for part in parts], [part[1] for part in parts]
    block, grads, hidden = order.step(add_block(parts[3][2], passed[3]), grads, hidden)
    terms.append(grid.turn(block, 6))
    second_team = second_chips + second_other
    early = max(1, teams // 2)
    mixer_part = token_product(grid, second_team, grads)
    mixer_part, hidden = order.step(mixer_part, hidden)
    mixer_parts = send_teams(mixer_part, 1, early + 1)
    down_part = down_product(grid, hidden, cotangent_team)
    terms, down_part = order.step(terms, down_part)
    grad_middle, grad_attn, second_part = finish_second(terms, middle, cotangent, gain_second)
    grad_attn, hidden = order.step(grad_attn, hidden)
    attn_chips = grid.chips(grad_attn)
    out_keep, out_give = mixer_output(hidden, down_w)
    attn_chips, out_give, mixer_parts = order.step(attn_chips, out_give, mixer_parts)
    late_parts = send_teams(mixer_part, early + 1, teams)
    attn_team = order.step(grid.gather_team(attn_chips))

    grad_attended, out_part = project_out_back(grid, attn_team, out_rows, attended)
    grad_attended, down_part, out_give = order.step(grad_attended, down_part, out_give)
    down_late = send_teams(down_part, early + 1, teams)
    out_other = grid.turn(out_give, 1)
    query_rot, own_grads, back_grads = attend_back(
        low, starts, queries, grad_attended, attended, normalizer, pieces, 0, OWN_KV
    )
    query_rot, own_grads, back_grads, late_parts, down_late, out_other = order.step(
        query_rot, own_grads, back_grads, late_parts, down_late, out_other
    )
    returned = [
        grid.shift(back_grads[step - 1], -step, False) for step in range(1, steps_back + 1)
    ]
    out_total, out_blocks = combine(out_keep, out_other, 0)
    out_blocks = order.step(out_blocks)
    out_terms = grid.send_chips(out_blocks)
    mixer_total = sum_teams(mixer_part, mixer_parts + late_parts, bf16)
    def members_rows(total):
        blocks = total.reshape(TEAM // 2, 2, rows, -1)
        return dynamic(blocks, core, 1), grid.turn(dynamic(blocks, 1 - core, 1), 1)

    def owner_columns(mine, others):
        both = jnp.stack([mine, others])
        first = jnp.where(core == 0, both[0], both[1])
        second = jnp.where(core == 0, both[1], both[0])
        both = jnp.stack([first, second], axis=1)
        found = [
            dynamic(both, chip) if other == 0 else grid.turn(dynamic(both, chip ^ other), 2 * other)
            for other in range(4)
        ]
        return found

    def in_order(found):
        stacked = jnp.stack(found)
        return jnp.stack([dynamic(stacked, chip ^ other) for other in range(4)]).reshape(
            (TEAM,) + found[0].shape[1:]
        )

    returned, mixer_total = order.step(returned, mixer_total)
    down_parts = send_teams(down_part, 1, early + 1)
    mixer_mine, mixer_others = members_rows(mixer_total)
    keep, give, attn_part = project_back(
        grid, normed_first, query_rot, own_grads, returned, cosine, sine_table, attn_w
    )
    attn_part, give, out_terms, down_parts, mixer_others = order.step(
        attn_part, give, out_terms, down_parts, mixer_others
    )
    other = grid.turn(give, 1)
    mixer_found = owner_columns(mixer_mine, mixer_others)
    other = order.step(other)
    total, blocks = combine(keep, other, 1)
    blocks, mixer_found, out_part = order.step(blocks, mixer_found, out_part)
    terms = grid.send_chips(blocks)
    attn_parts = send_teams(attn_part, 1, early + 1)
    outputs = finish_output([out_total] + out_terms, middle)
    down_grad = sum_teams(down_part, down_parts + down_late, f32)
    mixer_columns = in_order(mixer_found)
    attn_parts, outputs, down_grad = order.step(attn_parts, outputs, down_grad)
    attn_late = send_teams(attn_part, early + 1, teams)
    terms, attn_late = order.step(terms, attn_late)
    out_parts = send_teams(out_part, 1, teams)
    input_grad, first_part = finish_first([total] + terms, inputs_t, grad_middle, gain_first)
    gain_parts = jnp.concatenate([first_part, second_part], axis=1).T
    attn_total = sum_teams(attn_part, attn_parts + attn_late, bf16)
    attn_mine, attn_others = members_rows(attn_total)
    gain_parts, attn_total = order.step(gain_parts, attn_total)
    gain_other = grid.turn(gain_parts, 1)
    gain_other, attn_others, out_parts = order.step(gain_other, attn_others, out_parts)
    gain_parts = gain_parts + gain_other
    gain_parts = order.step(gain_parts)
    gain_chips = [grid.turn(gain_parts, 2 * other) for other in range(1, 4)]
    out_own = sum_teams(out_part, out_parts, bf16)
    gain_chips, out_own = order.step(gain_chips, out_own)
    for other in gain_chips:
        gain_parts = gain_parts + other
    attn_found = owner_columns(attn_mine, attn_others)
    out_grad = grid.to_owners(out_own)

    def whole_units(blocks):
        blocks = blocks.reshape(TEAM, rows, teams, unit_rows)
        return jnp.transpose(blocks, (1, 2, 0, 3)).reshape(rows, TEAM * units).astype(f32)

    def whole(blocks):
        return jnp.transpose(blocks, (1, 0, 2)).reshape(rows, -1).astype(f32)

    gate_grad = whole_units(mixer_columns[..., :units])
    up_grad = whole_units(mixer_columns[..., units:])
    attn_found, out_grad, gain_parts = order.step(attn_found, out_grad, gain_parts)
    gain_blocks = gain_parts.reshape(2, teams, TEAM, rows)
    gain_sums = dynamic(dynamic(gain_blocks, grid.team, 1), member, 1)
    for steps in range(1, teams):
        block = dynamic(dynamic(gain_blocks, (grid.team + steps) % teams, 1), member, 1)
        gain_sums = gain_sums + grid.shift(block, steps)
    out_grad = out_grad.astype(f32)
    attn_columns = in_order(attn_found)
    gain_sums = gain_sums + order.token[0, 0].astype(f32)
    return (
        outputs,
        input_grad,
        gain_sums[0],
        whole(attn_columns[..., :Q_WIDTH]),
        whole(attn_columns[..., Q_WIDTH : Q_WIDTH + KV_WIDTH]),
        whole(attn_columns[..., Q_WIDTH + KV_WIDTH :]),
        out_grad,
        gain_sums[1],
        gate_grad,
        up_grad,
        down_grad,
    )


def solution(mesh):
    matrix, vector = P("dev", None), P("dev")
    in_specs = (matrix, vector, vector) + (matrix,) * 4 + (vector,) + (matrix,) * 4
    out_specs = (matrix, matrix, vector) + (matrix,) * 4 + (vector,) + (matrix,) * 3
    return jax.shard_map(
        per_device, mesh=mesh, in_specs=in_specs, out_specs=out_specs, check_vma=False
    )
```

```python
import math

import jax
import jax.numpy as jnp
from jax import lax
from jax.experimental import pallas as pl
from jax.experimental.pallas import tpu as pltpu
from jax.sharding import PartitionSpec as P

HEADS = 16
KV_HEADS = 8
HEAD_DIM = 96
TEAM = 8

eps_norm = 1e-05
rope_base = 100000.0
masked_score = -1e30

OWN_HEADS = HEADS // TEAM
OWN_KV = KV_HEADS // TEAM
GROUP = HEADS // KV_HEADS
BLOCK = 256
LANES = 128
score_scale = 1.0 / math.sqrt(HEAD_DIM)
log2_scale = score_scale / math.log(2.0)
kernel_vmem = 56 * 1024 * 1024
small_cost = pl.CostEstimate(flops=1000, bytes_accessed=1000, transcendentals=0)

Q_WIDTH = OWN_HEADS * HEAD_DIM
KV_WIDTH = OWN_KV * HEAD_DIM
LINED = Q_WIDTH + 2 * KV_WIDTH


def relative(position):
    return 2 * (position % 4) + position // 4


def visible_mask(block, starts, ends):
    key = block * BLOCK + lax.broadcasted_iota(jnp.int32, (BLOCK, 1), 0)
    return (key >= starts) & (key <= ends)


def chunk_lanes(ref, chunk):
    spot = pl.ds(chunk * BLOCK, BLOCK)
    return jnp.concatenate([ref[head, :, spot] for head in range(GROUP)], axis=1)


def chunk_range(chunk, starts_ref, last):
    starts = starts_ref[:, pl.ds(chunk * BLOCK, BLOCK)]
    ends = last * BLOCK + lax.broadcasted_iota(jnp.int32, (1, BLOCK), 1)
    return (
        jnp.concatenate([starts] * GROUP, axis=1),
        jnp.concatenate([ends] * GROUP, axis=1),
    )


def attend_kernel(low_ref, starts_ref, query_ref, *refs):
    count = len(refs) - 4
    member = low_ref[TEAM]
    pieces = refs[:count]
    out_ref, norm_ref, keys, values = refs[count:]
    per_piece = pieces[0].shape[-1] // BLOCK
    for back, piece in enumerate(pieces):
        for part in range(per_piece):
            block = (count - 1 - back) * per_piece + (relative(part) ^ member)
            spot = pl.ds(part * BLOCK, BLOCK)
            keys[block] = piece[0, 0, :, spot].T
            values[block] = piece[1, 0, :, spot]
    own_block = (count - 1) * per_piece
    for chunk in range(per_piece):
        queries = chunk_lanes(query_ref, chunk)
        last = own_block + (relative(chunk) ^ member)
        starts, ends = chunk_range(chunk, starts_ref, last)

        def masked(block):
            held = jnp.maximum(block, 0)
            scores = jnp.dot(keys[held], queries, preferred_element_type=jnp.float32) * log2_scale
            return held, jnp.where(visible_mask(block, starts, ends), scores, masked_score)

        def advance(step, running):
            top, total, summed = running
            one, scores = masked(last - 2 * step)
            two, more = masked(last - 2 * step - 1)
            new_top = jnp.maximum(
                top, jnp.max(jnp.maximum(scores, more), axis=0, keepdims=True)
            )
            factor = jnp.exp2(top - new_top)
            weights, others = jnp.exp2(scores - new_top), jnp.exp2(more - new_top)
            total = total * factor + jnp.sum(weights + others, axis=0, keepdims=True)
            summed = summed * factor + (
                jnp.dot(
                    values[one], weights.astype(jnp.bfloat16), preferred_element_type=jnp.float32
                )
                + jnp.dot(
                    values[two], others.astype(jnp.bfloat16), preferred_element_type=jnp.float32
                )
            )
            return new_top, total, summed

        lanes = GROUP * BLOCK
        top, total, summed = lax.fori_loop(
            0,
            (last - low_ref[chunk] + 2) // 2,
            advance,
            (
                jnp.full((1, lanes), masked_score, jnp.float32),
                jnp.zeros((1, lanes), jnp.float32),
                jnp.zeros((HEAD_DIM, lanes), jnp.float32),
            ),
        )
        attended = summed / total
        norm = top + jnp.log2(total)
        spot = pl.ds(chunk * BLOCK, BLOCK)
        for head in range(GROUP):
            out_ref[head, :, spot] = attended[:, head * BLOCK : (head + 1) * BLOCK]
            norm_ref[head, :, spot] = norm[:, head * BLOCK : (head + 1) * BLOCK]


def gradient_kernel(low_ref, starts_ref, query_ref, grad_ref, out_ref, norm_ref, *refs):
    count = len(refs) - 8
    member = low_ref[TEAM]
    pieces = refs[:count]
    query_grad, own_grad, back_grad, keys, keys_t, values, key_sum, value_sum = refs[count:]
    per_piece = pieces[0].shape[-1] // BLOCK
    for back, piece in enumerate(pieces):
        for part in range(per_piece):
            block = (count - 1 - back) * per_piece + (relative(part) ^ member)
            spot = pl.ds(part * BLOCK, BLOCK)
            keys_t[block] = piece[0, 0, :, spot]
            keys[block] = piece[0, 0, :, spot].T
            values[block] = piece[1, 0, :, spot].T
    key_sum[...] = jnp.zeros_like(key_sum)
    value_sum[...] = jnp.zeros_like(value_sum)
    own_block = (count - 1) * per_piece
    rows_rows = (((1,), (1,)), ((), ()))
    for chunk in range(per_piece):
        queries = chunk_lanes(query_ref, chunk)
        grads = chunk_lanes(grad_ref, chunk)
        norm = chunk_lanes(norm_ref, chunk)
        delta = jnp.sum(
            grads.astype(jnp.float32) * chunk_lanes(out_ref, chunk), axis=0, keepdims=True
        )
        last = own_block + (relative(chunk) ^ member)
        starts, ends = chunk_range(chunk, starts_ref, last)

        def part(block):
            held = jnp.minimum(block, last)
            scores = jnp.dot(keys[held], queries, preferred_element_type=jnp.float32) * log2_scale
            scores = jnp.where(visible_mask(block, starts, ends), scores - norm, masked_score)
            probs = jnp.exp2(scores)
            slopes = jnp.dot(values[held], grads, preferred_element_type=jnp.float32)
            grad_scores = (probs * (slopes - delta)).astype(jnp.bfloat16)
            return held, probs.astype(jnp.bfloat16), grad_scores

        def advance(step, summed):
            found = [part(low_ref[chunk] + 2 * step), part(low_ref[chunk] + 2 * step + 1)]
            for held, probs, grad_scores in found:
                key_sum[held] += lax.dot_general(
                    queries, grad_scores, rows_rows, preferred_element_type=jnp.float32
                )
                value_sum[held] += lax.dot_general(
                    grads, probs, rows_rows, preferred_element_type=jnp.float32
                )
                summed = summed + jnp.dot(
                    keys_t[held], grad_scores, preferred_element_type=jnp.float32
                )
            return summed

        summed = lax.fori_loop(
            0,
            (last - low_ref[chunk] + 2) // 2,
            advance,
            jnp.zeros((HEAD_DIM, GROUP * BLOCK), jnp.float32),
        )
        spot = pl.ds(chunk * BLOCK, BLOCK)
        for head in range(GROUP):
            query_grad[head, :, spot] = (
                summed[:, head * BLOCK : (head + 1) * BLOCK] * score_scale
            )
    for back in range(count):
        for part in range(per_piece):
            block = (count - 1 - back) * per_piece + (relative(part) ^ member)
            spot = pl.ds(part * BLOCK, BLOCK)
            key_part = key_sum[block] * score_scale
            value_part = value_sum[block]
            if back == 0:
                own_grad[0, 0, :, spot] = key_part
                own_grad[1, 0, :, spot] = value_part
            else:
                back_grad[back - 1, 0, 0, :, spot] = key_part.astype(jnp.bfloat16)
                back_grad[back - 1, 1, 0, :, spot] = value_part.astype(jnp.bfloat16)


def attention_specs(tokens, pieces, first_head):
    whole = pl.BlockSpec((1, tokens), lambda head: (0, 0))
    low = pl.BlockSpec(memory_space=pltpu.SMEM)
    heads = pl.BlockSpec(
        (GROUP, HEAD_DIM, tokens), lambda head: (first_head + head, 0, 0)
    )
    norm = pl.BlockSpec((GROUP, 1, tokens), lambda head: (first_head + head, 0, 0))
    kv = pl.BlockSpec((2, 1, HEAD_DIM, tokens), lambda head: (0, first_head + head, 0, 0))
    return low, whole, heads, norm, [kv] * len(pieces)


def attend(low, starts, queries, pieces, first_head, count):
    tokens = queries.shape[-1]
    blocks = len(pieces) * tokens // BLOCK
    low_spec, whole, heads, norm, kv = attention_specs(tokens, pieces, first_head)
    return pl.pallas_call(
        attend_kernel,
        grid=(count,),
        in_specs=[low_spec, whole, heads] + kv,
        out_specs=[
            pl.BlockSpec((GROUP, HEAD_DIM, tokens), lambda head: (head, 0, 0)),
            pl.BlockSpec((GROUP, 1, tokens), lambda head: (head, 0, 0)),
        ],
        out_shape=[
            jax.ShapeDtypeStruct((count * GROUP, HEAD_DIM, tokens), jnp.float32),
            jax.ShapeDtypeStruct((count * GROUP, 1, tokens), jnp.float32),
        ],
        scratch_shapes=[
            pltpu.VMEM((blocks, BLOCK, HEAD_DIM), jnp.bfloat16),
            pltpu.VMEM((blocks, HEAD_DIM, BLOCK), jnp.bfloat16),
        ],
        compiler_params=pltpu.CompilerParams(vmem_limit_bytes=kernel_vmem),
        cost_estimate=small_cost,
    )(low, starts, queries, *pieces)


def attend_back(low, starts, queries, grads, attended, norm, pieces, first_head, count):
    tokens = queries.shape[-1]
    blocks = len(pieces) * tokens // BLOCK
    low_spec, whole, heads, norm_spec, kv = attention_specs(tokens, pieces, first_head)
    back = len(pieces) - 1
    return pl.pallas_call(
        gradient_kernel,
        grid=(count,),
        in_specs=[low_spec, whole, heads, heads, heads, norm_spec] + kv,
        out_specs=[
            pl.BlockSpec((GROUP, HEAD_DIM, tokens), lambda head: (head, 0, 0)),
            pl.BlockSpec((2, 1, HEAD_DIM, tokens), lambda head: (0, head, 0, 0)),
            pl.BlockSpec((back, 2, 1, HEAD_DIM, tokens), lambda head: (0, 0, head, 0, 0)),
        ],
        out_shape=[
            jax.ShapeDtypeStruct((count * GROUP, HEAD_DIM, tokens), jnp.float32),
            jax.ShapeDtypeStruct((2, count, HEAD_DIM, tokens), jnp.float32),
            jax.ShapeDtypeStruct((back, 2, count, HEAD_DIM, tokens), jnp.bfloat16),
        ],
        scratch_shapes=[
            pltpu.VMEM((blocks, BLOCK, HEAD_DIM), jnp.bfloat16),
            pltpu.VMEM((blocks, HEAD_DIM, BLOCK), jnp.bfloat16),
            pltpu.VMEM((blocks, BLOCK, HEAD_DIM), jnp.bfloat16),
            pltpu.VMEM((blocks, HEAD_DIM, BLOCK), jnp.float32),
            pltpu.VMEM((blocks, HEAD_DIM, BLOCK), jnp.float32),
        ],
        compiler_params=pltpu.CompilerParams(vmem_limit_bytes=kernel_vmem),
        cost_estimate=small_cost,
    )(low, starts, queries, grads, attended, norm, *pieces)

class Order:
    def __init__(self, token):
        self.token = token

    def step(self, *values):
        self.token, tied = lax.optimization_barrier((self.token, values))
        return tied[0] if len(tied) == 1 else tied


class Grid:
    def __init__(self):
        self.count = lax.axis_size("dev")
        self.teams = self.count // TEAM
        index = lax.axis_index("dev")
        self.member = index % TEAM
        self.team = index // TEAM

    def places(self):
        return jnp.stack([self.team, self.member]).astype(jnp.int32)

    def turn(self, value, bits):
        return lax.ppermute(value, "dev", [(d, d ^ bits) for d in range(self.count)])

    def shift(self, value, steps, around=True):
        pairs = []
        for device in range(self.count):
            target = device + steps * TEAM
            if around or 0 <= target < self.count:
                pairs.append((device, target % self.count))
        return lax.ppermute(value, "dev", pairs)

    def spread(self, value):
        return [value] + [self.shift(value, steps) for steps in range(1, self.teams)]

    def both_ways(self, ahead, behind):
        return self.shift(ahead, 1, False), self.shift(behind, -1, False)

    def gather_team(self, blocks):
        return list(blocks) + [self.turn(block, 1) for block in blocks]

    def chips(self, block):
        return [block] + [self.turn(block, 2 * chip) for chip in range(1, 4)]

    def to_members(self, value):
        pairs = [
            (owner, owner % self.teams * TEAM + owner // self.teams)
            for owner in range(self.count)
        ]
        return lax.ppermute(value, "dev", pairs)

    def to_owners(self, value):
        pairs = [
            (owner % self.teams * TEAM + owner // self.teams, owner)
            for owner in range(self.count)
        ]
        return lax.ppermute(value, "dev", pairs)

    def send_chips(self, blocks):
        return [self.turn(block, 2 * chip) for chip, block in enumerate(blocks, 1)]


def call(kernel, grid, in_specs, out_specs, out_shape, scratch=(), prefetch=0):
    return pl.pallas_call(
        kernel,
        out_shape=out_shape,
        grid_spec=pltpu.PrefetchScalarGridSpec(
            num_scalar_prefetch=prefetch,
            grid=grid,
            in_specs=in_specs,
            out_specs=out_specs,
            scratch_shapes=list(scratch),
        ),
        compiler_params=pltpu.CompilerParams(vmem_limit_bytes=kernel_vmem),
        cost_estimate=small_cost,
    )


def fixed(array):
    return pl.BlockSpec(array.shape, lambda *unused: (0,) * array.ndim)


def lanes_at(rows, step_width):
    return pl.BlockSpec((rows, step_width), lambda p, *unused: (0, p))


def rows_at(step_rows, width):
    return pl.BlockSpec((step_rows, width), lambda p, *unused: (p, 0))


def kept_given(rows, width, axis):
    def index(at):
        return (0, at) if axis else (at, 0)

    specs = [
        pl.BlockSpec((rows, width), lambda p, *unused: index(jnp.minimum(p, 3))),
        pl.BlockSpec((rows, width), lambda p, *unused: index(jnp.maximum(p - 4, 0))),
    ]
    shape = (rows, 4 * width) if axis else (4 * rows, width)
    shapes = [
        jax.ShapeDtypeStruct(shape, jnp.float32),
        jax.ShapeDtypeStruct(shape, jnp.bfloat16),
    ]
    return specs, shapes


def keep_or_give(position, keep_ref, give_ref, value):
    @pl.when(position < 4)
    def keep():
        keep_ref[...] = value

    @pl.when(position >= 4)
    def give():
        give_ref[...] = value.astype(give_ref.dtype)


def pick(position, refs, target):
    for number in range(TEAM):

        @pl.when(position == number)
        def move():
            if len(refs) == TEAM:
                target[...] = refs[number][...]
            else:
                target[...] = refs[number // 4][number % 4]


def dot_rows(left, right):
    return lax.dot_general(
        left, right, (((1,), (1,)), ((), ())), preferred_element_type=jnp.float32
    )


def dot(left, right):
    return jnp.dot(left, right, preferred_element_type=jnp.float32)


def place_rows(grid, blocks, start, stop):
    count = len(blocks)
    positions, rows = blocks[0].shape[:2]
    width = stop - start

    def kernel(places_ref, *refs):
        target = refs[-1]
        for number, ref in enumerate(refs[:-1]):

            @pl.when(pl.program_id(0) == number)
            def move():
                for position in range(positions):
                    at = relative(position) ^ places_ref[1] if positions > 1 else 0
                    target[0, pl.ds(at, 1)] = ref[position : position + 1, :, start:stop]

    def target_map(step, places_ref):
        return ((places_ref[0] + count - step) % count, 0, 0, 0)

    return call(
        kernel,
        (count,),
        [fixed(block) for block in blocks],
        pl.BlockSpec((1, positions, rows, width), target_map),
        jax.ShapeDtypeStruct((count, positions, rows, width), blocks[0].dtype),
        prefetch=1,
    )(grid.places(), *blocks)


def place_mixer(grid, own, hops, units, unit_rows):
    count = grid.teams
    positions, rows, wide = own.shape
    third = wide - 2 * units
    sources = [own] + [block for hop in hops for block in hop]

    def kernel(places_ref, *refs):
        mixer_ref, down_ref = refs[-2:]
        team = places_ref[0]

        def move(ref):
            for position in range(positions):
                at = relative(position) ^ places_ref[1]
                mixer_ref[0, pl.ds(at, 1)] = ref[position : position + 1, :, : 2 * units]
                row = position * rows
                while row < (position + 1) * rows:
                    part = row // unit_rows
                    stop = min((part + 1) * unit_rows, (position + 1) * rows)
                    down_ref[
                        0,
                        row - part * unit_rows : stop - part * unit_rows,
                        part * third : (part + 1) * third,
                    ] = ref[position, row - position * rows : stop - position * rows, 2 * units :]
                    row = stop

        for steps in range(count):
            here = pl.program_id(0) == steps
            if steps == 0:
                pl.when(here)(lambda: move(refs[0]))
            else:
                ahead, behind = refs[2 * steps - 1], refs[2 * (count - steps)]
                pl.when(here & (team >= steps))(lambda ahead=ahead: move(ahead))
                pl.when(here & (team < steps))(lambda behind=behind: move(behind))

    def target_map(step, places_ref):
        return (places_ref[0] + count - step) % count

    return call(
        kernel,
        (count,),
        [fixed(source) for source in sources],
        [
            pl.BlockSpec(
                (1, positions, rows, 2 * units), lambda s, p: (target_map(s, p), 0, 0, 0)
            ),
            pl.BlockSpec((1, unit_rows, 3 * third), lambda s, p: (target_map(s, p), 0, 0)),
        ],
        [
            jax.ShapeDtypeStruct((count, positions, rows, 2 * units), own.dtype),
            jax.ShapeDtypeStruct((count, unit_rows, 3 * third), own.dtype),
        ],
        prefetch=1,
    )(grid.places(), *sources)


def project(inputs_t, weights, cosine, sine_table):
    width, own = inputs_t[0].shape
    tokens = TEAM * own
    half = HEAD_DIM // 2

    def kernel(weights_ref, cosine_ref, sine_ref, *refs):
        sources = refs[:TEAM]
        normed_ref, query_ref, kv_ref, chosen, turned = refs[TEAM:]
        position = pl.program_id(0)

        @pl.when(position == 0)
        def prepare():
            turned[...] = weights_ref[:, :LINED].T

        pick(position, sources, chosen)
        values = chosen[...].astype(jnp.float32)
        scale = lax.rsqrt(jnp.mean(values * values, axis=0, keepdims=True) + eps_norm)
        gain = weights_ref[:, LINED : LINED + 1].astype(jnp.float32)
        normed = (values * scale * gain).astype(jnp.bfloat16)
        normed_ref[...] = normed
        lined = dot(turned[...], normed)
        cosines, sines = cosine_ref[...], sine_ref[...]

        def rotated(head):
            block = lined[head * HEAD_DIM : (head + 1) * HEAD_DIM]
            shifted = jnp.concatenate([-block[half:], block[:half]], axis=0)
            return (block * cosines + shifted * sines).astype(jnp.bfloat16)

        for head in range(OWN_HEADS):
            query_ref[head] = rotated(head)
        for head in range(OWN_KV):
            kv_ref[0, head] = rotated(OWN_HEADS + head)
            start = Q_WIDTH + KV_WIDTH + head * HEAD_DIM
            kv_ref[1, head] = lined[start : start + HEAD_DIM].astype(jnp.bfloat16)

    return call(
        kernel,
        (TEAM,),
        [fixed(weights), lanes_at(HEAD_DIM, own), lanes_at(HEAD_DIM, own)]
        + [fixed(block) for block in inputs_t],
        [
            lanes_at(width, own),
            pl.BlockSpec((OWN_HEADS, HEAD_DIM, own), lambda p: (0, 0, p)),
            pl.BlockSpec((2, OWN_KV, HEAD_DIM, own), lambda p: (0, 0, 0, p)),
        ],
        [
            jax.ShapeDtypeStruct((width, tokens), jnp.bfloat16),
            jax.ShapeDtypeStruct((OWN_HEADS, HEAD_DIM, tokens), jnp.bfloat16),
            jax.ShapeDtypeStruct((2, OWN_KV, HEAD_DIM, tokens), jnp.bfloat16),
        ],
        [
            pltpu.VMEM((width, own), jnp.bfloat16),
            pltpu.VMEM((LINED, width), jnp.bfloat16),
        ],
    )(weights, cosine, sine_table, *inputs_t)


def project_out(attended, out_rows):
    tokens = attended.shape[-1]
    own = tokens // TEAM
    width = out_rows.shape[1]
    specs, shapes = kept_given(width, own, 1)

    def kernel(attended_ref, rows_ref, keep_ref, give_ref, turned):
        position = pl.program_id(0)

        @pl.when(position == 0)
        def prepare():
            turned[...] = rows_ref[...].T

        block = attended_ref[...].reshape(Q_WIDTH, own).astype(jnp.bfloat16)
        keep_or_give(position, keep_ref, give_ref, dot(turned[...], block))

    return call(
        kernel,
        (TEAM,),
        [pl.BlockSpec((OWN_HEADS, HEAD_DIM, own), lambda p: (0, 0, p)), fixed(out_rows)],
        specs,
        shapes,
        [pltpu.VMEM((width, Q_WIDTH), jnp.bfloat16)],
    )(attended, out_rows)


def mixer(chip, normed, cotangent, weights, down):
    width, own = normed[0].shape
    units = down.shape[0]

    def kernel(first_ref, second_ref, wanted_a, wanted_b, weights_ref, down_ref, *refs):
        hidden_ref, grad_ref, keep_ref, give_ref, turned, wanted = refs
        step = pl.program_id(0)

        @pl.when(step == 0)
        def first():
            turned[...] = first_ref[...].T
            wanted[...] = wanted_a[0]

        @pl.when(step == 1)
        def second():
            turned[...] = second_ref[...].T
            wanted[...] = wanted_b[0]

        gate = dot(turned[...], weights_ref[:, :units])
        up = dot(turned[...], weights_ref[:, units:])
        logistic = 1.0 / (1.0 + jnp.exp(-gate))
        silu = gate * logistic
        hidden_ref[...] = (silu * up).astype(jnp.bfloat16)
        grad_hidden = dot_rows(wanted[...], down_ref[...])
        grad_ref[:, :units] = (
            grad_hidden * up * (logistic * (1.0 + gate * (1.0 - logistic)))
        ).astype(jnp.bfloat16)
        grad_ref[:, units:] = (grad_hidden * silu).astype(jnp.bfloat16)
        term = dot_rows(weights_ref[...], grad_ref[...])

        @pl.when(step == 0)
        def keep():
            keep_ref[...] = term

        @pl.when(step == 1)
        def give():
            give_ref[...] = term.astype(jnp.bfloat16)

    block = pl.BlockSpec((1, own, width), lambda p: (chip, 0, 0))
    whole = pl.BlockSpec((width, own), lambda p: (0, 0))
    return call(
        kernel,
        (2,),
        [fixed(normed[0]), fixed(normed[1]), block, block, fixed(weights), fixed(down)],
        [rows_at(own, units), rows_at(own, 2 * units), whole, whole],
        [
            jax.ShapeDtypeStruct((2 * own, units), jnp.bfloat16),
            jax.ShapeDtypeStruct((2 * own, 2 * units), jnp.bfloat16),
            jax.ShapeDtypeStruct((width, own), jnp.float32),
            jax.ShapeDtypeStruct((width, own), jnp.bfloat16),
        ],
        [pltpu.VMEM((own, width), jnp.bfloat16), pltpu.VMEM((own, width), jnp.bfloat16)],
    )(normed[0], normed[1], cotangent[0], cotangent[1], weights, down)


def add_block(keep, arrived):
    def kernel(keep_ref, arrived_ref, out_ref):
        out_ref[...] = (keep_ref[...] + arrived_ref[...].astype(jnp.float32)).astype(jnp.bfloat16)

    rows = keep.shape[0] // 2
    part = rows_at(rows, keep.shape[1])
    return call(
        kernel, (2,), [part, part], part, jax.ShapeDtypeStruct(keep.shape, jnp.bfloat16)
    )(keep, arrived)


def pair_rows(position, refs, target):
    own = target.shape[0]
    for number in range(TEAM):

        @pl.when(position == number)
        def move():
            start = number // 4 * own
            target[...] = refs[number % 4][start : start + own]


def mixer_output(hidden, down):
    own, units = hidden[0].shape[0] // 2, hidden[0].shape[1]
    specs, shapes = kept_given(own, down.shape[1], 0)

    def kernel(down_ref, *refs):
        keep_ref, give_ref, chosen = refs[4:]
        pair_rows(pl.program_id(0), refs[:4], chosen)
        keep_or_give(pl.program_id(0), keep_ref, give_ref, dot(chosen[...], down_ref[...]))

    return call(
        kernel,
        (TEAM,),
        [fixed(down)] + [fixed(block) for block in hidden],
        specs,
        shapes,
        [pltpu.VMEM((own, units), jnp.bfloat16)],
    )(down, *hidden)


def write_teams(places_ref, total, out_ref, teams):
    rows = total.shape[0] // teams
    for team in range(teams):
        steps = (team + teams - places_ref[0]) % teams
        block = total[team * rows : (team + 1) * rows, :].astype(out_ref.dtype)
        out_ref[pl.ds(steps, 1)] = block[None]


def token_product(grid, lefts, rights):
    rows, own = lefts[0].shape
    width = rights[0].shape[1]
    teams = grid.teams

    def kernel(places_ref, *refs):
        left_refs, right_refs = refs[:TEAM], refs[TEAM : TEAM + 4]
        out_ref, total, chosen = refs[TEAM + 4 :]
        position = pl.program_id(0)
        pair_rows(position, right_refs, chosen)

        def add(value):
            @pl.when(position == 0)
            def first():
                total[...] = value

            @pl.when(position > 0)
            def later():
                total[...] += value

        for number, source in enumerate(left_refs):

            @pl.when(position == number)
            def block():
                add(dot(source[...], chosen[...]))

        @pl.when(position == TEAM - 1)
        def last():
            write_teams(places_ref, total, out_ref, teams)

    return call(
        kernel,
        (TEAM,),
        [fixed(block) for block in list(lefts) + list(rights)],
        pl.BlockSpec((teams, rows // teams, width), lambda p, *unused: (0, 0, 0)),
        jax.ShapeDtypeStruct((teams, rows // teams, width), jnp.bfloat16),
        [pltpu.VMEM((rows, width), jnp.float32), pltpu.VMEM((own, width), jnp.bfloat16)],
        prefetch=1,
    )(grid.places(), *lefts, *rights)


def down_product(grid, hidden, cotangent):
    units = hidden[0].shape[1]
    own, width = cotangent[0].shape[1:]
    teams = grid.teams

    def kernel(places_ref, *refs):
        hidden_refs, sources, (out_ref, total, wanted, chosen) = refs[:4], refs[4:6], refs[6:]
        position = pl.program_id(0)
        pick(position, sources, wanted)
        pair_rows(position, hidden_refs, chosen)
        value = dot(chosen[...].T, wanted[...])

        @pl.when(position == 0)
        def first():
            total[...] = value

        @pl.when(position > 0)
        def later():
            total[...] += value

        @pl.when(position == TEAM - 1)
        def last():
            write_teams(places_ref, total, out_ref, teams)

    return call(
        kernel,
        (TEAM,),
        [fixed(block) for block in list(hidden) + list(cotangent)],
        pl.BlockSpec((teams, units // teams, width), lambda p, *unused: (0, 0, 0)),
        jax.ShapeDtypeStruct((teams, units // teams, width), jnp.bfloat16),
        [
            pltpu.VMEM((units, width), jnp.float32),
            pltpu.VMEM((own, width), jnp.bfloat16),
            pltpu.VMEM((own, units), jnp.bfloat16),
        ],
        prefetch=1,
    )(grid.places(), *hidden, *cotangent)


def project_out_back(grid, grads, out_rows, attended):
    teams = grid.teams
    tokens = attended.shape[-1]
    own = tokens // TEAM
    width = out_rows.shape[1]

    def kernel(places_ref, rows_ref, attended_ref, *refs):
        sources, (grad_ref, out_ref, chosen, total) = refs[:TEAM], refs[TEAM:]
        position = pl.program_id(0)
        pick(position, sources, chosen)
        grad_ref[...] = (
            dot(rows_ref[...], chosen[...])
            .astype(jnp.bfloat16)
            .reshape(OWN_HEADS, HEAD_DIM, own)
        )
        block = attended_ref[...].reshape(Q_WIDTH, own).astype(jnp.bfloat16)
        value = dot_rows(block, chosen[...])

        @pl.when(position == 0)
        def first():
            total[...] = value

        @pl.when(position > 0)
        def later():
            total[...] += value

        @pl.when(position == TEAM - 1)
        def last():
            write_teams(places_ref, total, out_ref, teams)

    heads = pl.BlockSpec((OWN_HEADS, HEAD_DIM, own), lambda p, *unused: (0, 0, p))
    shape = (teams, Q_WIDTH // teams, width)
    return call(
        kernel,
        (TEAM,),
        [fixed(out_rows), heads] + [fixed(block) for block in grads],
        [heads, pl.BlockSpec(shape, lambda p, *unused: (0, 0, 0))],
        [
            jax.ShapeDtypeStruct((OWN_HEADS, HEAD_DIM, tokens), jnp.bfloat16),
            jax.ShapeDtypeStruct(shape, jnp.bfloat16),
        ],
        [pltpu.VMEM((width, own), jnp.bfloat16), pltpu.VMEM((Q_WIDTH, width), jnp.float32)],
        prefetch=1,
    )(grid.places(), out_rows, attended, *grads)


def project_back(grid, normed, query_rot, own_grads, returned, cosine, sine_table, weights):
    width, tokens = normed.shape
    own = tokens // TEAM
    half = HEAD_DIM // 2
    teams = grid.teams
    specs, shapes = kept_given(width, own, 1)

    def kernel(places_ref, normed_ref, query_ref, cosine_ref, sine_ref, weights_ref, *refs):
        kv_refs = refs[: 1 + len(returned)]
        keep_ref, give_ref, out_ref, total, grad_ref = refs[1 + len(returned) :]
        position = pl.program_id(0)
        cosines, sines = cosine_ref[...], sine_ref[...]

        def unrotated(block):
            scaled = block * sines
            shifted = jnp.concatenate([scaled[half:], -scaled[:half]], axis=0)
            return (block * cosines + shifted).astype(jnp.bfloat16)

        for head in range(OWN_HEADS):
            grad_ref[head * HEAD_DIM : (head + 1) * HEAD_DIM] = unrotated(query_ref[head])
        kv = kv_refs[0][...]
        for ref in kv_refs[1:]:
            kv = kv + ref[...].astype(jnp.float32)
        for head in range(OWN_KV):
            start = Q_WIDTH + head * HEAD_DIM
            grad_ref[start : start + HEAD_DIM] = unrotated(kv[0, head])
            start = start + KV_WIDTH
            grad_ref[start : start + HEAD_DIM] = kv[1, head].astype(jnp.bfloat16)
        grad = grad_ref[...]
        keep_or_give(position, keep_ref, give_ref, dot(weights_ref[:, :LINED], grad))
        value = dot_rows(normed_ref[...], grad)

        @pl.when(position == 0)
        def first():
            total[...] = value

        @pl.when(position > 0)
        def later():
            total[...] += value

        @pl.when(position == TEAM - 1)
        def last():
            write_teams(places_ref, total, out_ref, teams)

    heads = pl.BlockSpec((OWN_HEADS, HEAD_DIM, own), lambda p, *unused: (0, 0, p))
    kv_heads = pl.BlockSpec((2, OWN_KV, HEAD_DIM, own), lambda p, *unused: (0, 0, 0, p))
    return call(
        kernel,
        (TEAM,),
        [
            lanes_at(width, own),
            heads,
            lanes_at(HEAD_DIM, own),
            lanes_at(HEAD_DIM, own),
            fixed(weights),
        ]
        + [kv_heads] * (1 + len(returned)),
        specs + [pl.BlockSpec((teams, width // teams, LINED), lambda p, *unused: (0, 0, 0))],
        shapes + [jax.ShapeDtypeStruct((teams, width // teams, LINED), jnp.bfloat16)],
        [pltpu.VMEM((width, LINED), jnp.float32), pltpu.VMEM((LINED, own), jnp.bfloat16)],
        prefetch=1,
    )(grid.places(), normed, query_rot, cosine, sine_table, weights, own_grads, *returned)


def combine(keep, arrived, axis):
    size = keep.shape[axis] // 4
    shape = (keep.shape[0], size) if axis else (size, keep.shape[1])

    def kernel(keep_ref, arrived_ref, own_ref, *block_refs):
        position = pl.program_id(0)
        total = keep_ref[...] + arrived_ref[...].astype(jnp.float32)

        @pl.when(position == 0)
        def own():
            own_ref[...] = total

        for number, ref in enumerate(block_refs, 1):

            @pl.when(position == number)
            def other():
                ref[...] = total.astype(jnp.bfloat16)

    part = pl.BlockSpec(shape, (lambda p: (0, p)) if axis else (lambda p: (p, 0)))
    whole = pl.BlockSpec(shape, lambda p: (0, 0))
    own, *blocks = call(
        kernel,
        (4,),
        [part, part],
        [whole] * 4,
        [jax.ShapeDtypeStruct(shape, jnp.float32)]
        + [jax.ShapeDtypeStruct(shape, jnp.bfloat16)] * 3,
    )(keep, arrived)
    return own, blocks


def summed(refs):
    total = refs[0][...]
    for ref in refs[1:]:
        total = total + ref[...].astype(jnp.float32)
    return total


def finish(kernel, arrays, shapes):
    return call(
        kernel,
        (1,),
        [fixed(array) for array in arrays],
        [pl.BlockSpec(shape.shape, lambda p: (0, 0)) for shape in shapes],
        shapes,
    )(*arrays)


def finish_middle(terms, inputs_t, gain):
    def kernel(*refs):
        inputs_ref, gain_ref, middle_ref, normed_ref = refs[len(terms) :]
        middle = inputs_ref[...].astype(jnp.float32) + summed(refs[: len(terms)])
        middle_ref[...] = middle
        scale = lax.rsqrt(jnp.mean(middle * middle, axis=0, keepdims=True) + eps_norm)
        normed_ref[...] = (middle * scale * gain_ref[...]).astype(jnp.bfloat16)

    shape = inputs_t.shape
    return finish(
        kernel,
        list(terms) + [inputs_t, gain],
        [jax.ShapeDtypeStruct(shape, jnp.float32), jax.ShapeDtypeStruct(shape, jnp.bfloat16)],
    )


def norm_back(values, gain, grad):
    inverse = lax.rsqrt(jnp.mean(values * values, axis=0, keepdims=True) + eps_norm)
    normal = values * inverse
    scaled = grad * gain
    inner = jnp.mean(scaled * normal, axis=0, keepdims=True)
    return inverse * (scaled - normal * inner), jnp.sum(grad * normal, axis=1, keepdims=True)


def finish_second(terms, middle, cotangent, gain):
    def kernel(*refs):
        middle_ref, cotangent_ref, gain_ref, grad_ref, attn_ref, gain_out = refs[len(terms) :]
        norm_grad, gain_part = norm_back(
            middle_ref[...], gain_ref[...], summed(refs[: len(terms)])
        )
        grad = cotangent_ref[...].T.astype(jnp.float32) + norm_grad
        grad_ref[...] = grad
        attn_ref[...] = grad.astype(jnp.bfloat16)
        gain_out[...] = gain_part

    shape = middle.shape
    return finish(
        kernel,
        list(terms) + [middle, cotangent, gain],
        [
            jax.ShapeDtypeStruct(shape, jnp.float32),
            jax.ShapeDtypeStruct(shape, jnp.bfloat16),
            jax.ShapeDtypeStruct((shape[0], 1), jnp.float32),
        ],
    )


def finish_first(terms, inputs_t, grad_middle, gain):
    def kernel(*refs):
        inputs_ref, grad_ref, gain_ref, out_ref, gain_out = refs[len(terms) :]
        norm_grad, gain_part = norm_back(
            inputs_ref[...].astype(jnp.float32), gain_ref[...], summed(refs[: len(terms)])
        )
        out_ref[...] = (grad_ref[...] + norm_grad).T
        gain_out[...] = gain_part

    width, own = inputs_t.shape
    return finish(
        kernel,
        list(terms) + [inputs_t, grad_middle, gain],
        [
            jax.ShapeDtypeStruct((own, width), jnp.float32),
            jax.ShapeDtypeStruct((width, 1), jnp.float32),
        ],
    )


def finish_output(terms, middle):
    def kernel(*refs):
        middle_ref, out_ref = refs[len(terms) :]
        out_ref[...] = (middle_ref[...].T + summed(refs[: len(terms)])).astype(jnp.bfloat16)

    return finish(
        kernel, list(terms) + [middle], [jax.ShapeDtypeStruct(terms[0].shape, jnp.bfloat16)]
    )[0]


def sum_teams(product, parts, kind):
    def kernel(own_ref, *refs):
        total = own_ref[0].astype(jnp.float32)
        for ref in refs[:-1]:
            total = total + ref[...].astype(jnp.float32)
        refs[-1][...] = total.astype(kind)

    shape = product.shape[1:]
    return call(
        kernel,
        (1,),
        [pl.BlockSpec((1,) + shape, lambda p: (0, 0, 0))] + [fixed(part) for part in parts],
        pl.BlockSpec(shape, lambda p: (0, 0)),
        jax.ShapeDtypeStruct(shape, kind),
    )(product, *parts)


def rope_tables(positions):
    half_dim = HEAD_DIM // 2
    frequency = rope_base ** (-(jnp.arange(half_dim, dtype=jnp.float32) * 2.0 / HEAD_DIM))
    angles = frequency[:, None] * positions.astype(jnp.float32)[None, :]
    angles = jnp.concatenate([angles, angles], axis=0)
    return (jnp.cos(angles), jnp.sin(angles))


def per_device(
    inputs,
    positions,
    norm_first,
    query_weight,
    key_weight,
    value_weight,
    out_weight,
    norm_second,
    gate_weight,
    up_weight,
    down_weight,
    cotangent,
):
    grid = Grid()
    member, teams = grid.member, grid.teams
    chip, core = member // 2, member % 2
    own, width = inputs.shape
    tokens = own * TEAM
    rows = query_weight.shape[0]
    unit_rows = down_weight.shape[0]
    units = unit_rows * teams
    longest = own * grid.count // 4
    steps_back = min((longest - 2) // tokens + 1, teams - 1)
    bf16, f32 = jnp.bfloat16, jnp.float32
    order = Order(jnp.zeros((8, 128), jnp.int32))

    def dynamic(array, index, axis=0):
        return lax.dynamic_index_in_dim(array, index, axis, keepdims=False)

    def by_member(weight):
        return jnp.transpose(weight.reshape(rows, TEAM, -1), (1, 0, 2))

    def units_by_member(weight):
        blocks = jnp.transpose(weight.reshape(rows, teams, TEAM, unit_rows), (2, 0, 1, 3))
        return blocks.reshape(TEAM, rows, units)

    gains = jnp.pad(jnp.stack([norm_first, norm_second], axis=1), ((0, 0), (0, LANES - 2)))
    columns = jnp.concatenate(
        [
            by_member(query_weight),
            by_member(key_weight),
            by_member(value_weight),
            jnp.broadcast_to(gains[None], (TEAM, rows, LANES)),
            units_by_member(gate_weight),
            units_by_member(up_weight),
        ],
        axis=-1,
    )
    attn_wide = LINED + LANES
    columns = columns.reshape(TEAM // 2, 2, rows, attn_wide + 2 * units)
    position_chips = jnp.stack(grid.chips(positions))
    all_positions = jnp.concatenate([position_chips, grid.turn(position_chips, 1)]).reshape(tokens)
    inputs_t = inputs.T
    columns, inputs_t = order.step(columns, inputs_t)
    pairs = [
        dynamic(columns, chip)
        if other == 0
        else grid.turn(dynamic(columns, chip ^ other), 2 * other)
        for other in range(4)
    ]
    inputs_two = [grid.turn(inputs_t, 2), grid.turn(inputs_t, 4)]
    cosine, sine_table = rope_tables(all_positions)
    block_index = steps_back * TEAM + (
        jnp.array([relative(p) for p in range(TEAM)], jnp.int32) ^ member
    )
    token_index = (block_index[:, None] * own + jnp.arange(own, dtype=jnp.int32)).reshape(tokens)
    starts = token_index - all_positions
    low = jnp.concatenate([starts[::own] // BLOCK, member[None]]).astype(jnp.int32)
    starts = starts[None]
    third = width // 3
    down_thirds = jnp.concatenate(
        [down_weight[:, part * third : (part + 1) * third] for part in range(3)], axis=0
    ).reshape(TEAM, rows, third)
    cosine, sine_table, starts, low, down_thirds, pairs, inputs_two, inputs_t = order.step(
        cosine, sine_table, starts, low, down_thirds, pairs, inputs_two, inputs_t
    )
    inputs_three = grid.turn(inputs_t, 6)
    pairs = jnp.stack(pairs)
    pairs_keep, pairs_give = dynamic(pairs, core, 1), dynamic(pairs, 1 - core, 1)
    team_rows = jnp.concatenate([pairs_keep, grid.turn(pairs_give, 1)], axis=0)
    attn_rows, team_rows, out_weight = order.step(
        team_rows[..., :attn_wide], team_rows, out_weight
    )
    attn_z = grid.spread(attn_rows)
    inputs_others = [grid.turn(block, 1) for block in [inputs_t] + inputs_two]
    attn_z, inputs_three = order.step(attn_z, inputs_three)
    inputs_others = inputs_others + [grid.turn(inputs_three, 1)]
    inputs_team = [inputs_t] + inputs_two + [inputs_three] + inputs_others
    out_own = grid.to_members(out_weight)
    attn_w = place_rows(grid, attn_z, 0, attn_wide).reshape(width, attn_wide)
    attn_w, inputs_team, out_own = order.step(attn_w, inputs_team, out_own)

    out_own = order.step(out_own)
    out_z = grid.spread(out_own)
    normed_first, queries, own_piece = project(inputs_team, attn_w, cosine, sine_table)
    own_piece, out_z, attn_w, cotangent = order.step(own_piece, out_z, attn_w, cotangent)
    arrived = [grid.shift(own_piece, step, False) for step in range(1, steps_back + 1)]
    cotangent_chips = [cotangent, grid.turn(cotangent, 2), grid.turn(cotangent, 4)]
    out_rows = place_rows(grid, [block[None] for block in out_z], 0, width)
    out_rows = out_rows.reshape(Q_WIDTH, width)
    gain_first = attn_w[:, LINED : LINED + 1].astype(f32)
    gain_second = attn_w[:, LINED + 1 : LINED + 2].astype(f32)
    mixer_own = jnp.concatenate([team_rows[..., attn_wide:], down_thirds], axis=-1)
    arrived, gain_first, gain_second, mixer_own, out_rows, cotangent_chips = order.step(
        arrived, gain_first, gain_second, mixer_own, out_rows, cotangent_chips
    )
    cotangent_chips = cotangent_chips + [grid.turn(cotangent_chips[0], 6)]

    mixer_hops = [grid.both_ways(mixer_own, mixer_own)]

    def next_hop():
        if len(mixer_hops) < teams - 1:
            mixer_hops.append(grid.both_ways(*mixer_hops[-1]))

    pieces = [own_piece] + arrived
    attended, normalizer = attend(low, starts, queries, pieces, 0, OWN_KV)
    keep, give = project_out(attended, out_rows)
    give, mixer_hops[0], cotangent_chips = order.step(give, mixer_hops[0], cotangent_chips)
    other = grid.turn(give, 1)
    next_hop()
    cotangent_stack = jnp.stack(cotangent_chips)
    other, cotangent_stack = order.step(other, cotangent_stack)
    cotangent_other = grid.turn(cotangent_stack, 1)
    total, blocks = combine(keep, other, 1)
    blocks, cotangent_other = order.step(blocks, cotangent_other)
    cotangent_team = [cotangent_stack, cotangent_other]
    near = [grid.turn(blocks[0], 2), grid.turn(blocks[1], 4)]
    near, far, mixer_hops[-1] = order.step(near, blocks[2], mixer_hops[-1])
    terms = near + [grid.turn(far, 6)]
    next_hop()
    terms = order.step(terms)
    middle, normed_second = finish_middle([total] + terms, inputs_t, gain_second)
    normed_second, mixer_hops[-1] = order.step(normed_second, mixer_hops[-1])
    while len(mixer_hops) < teams - 1:
        next_hop()
        mixer_hops[-1] = order.step(mixer_hops[-1])
    second_chips = [normed_second, grid.turn(normed_second, 2), grid.turn(normed_second, 4)]
    second_other = [grid.turn(normed_second, 1)]
    mixer_w, down_w = place_mixer(grid, mixer_own, mixer_hops, units, unit_rows)
    mixer_w = mixer_w.reshape(width, 2 * units)
    down_w = down_w.reshape(units, width)
    mixer_w, down_w, second_other[0] = order.step(mixer_w, down_w, second_other[0])

    def send_teams(product, first=1, last=teams):
        return [grid.shift(product[steps], steps) for steps in range(first, last)]

    def run_mixer(other_chip):
        hidden_part, grads_part, keep, give = mixer(
            other_chip,
            (second_chips[other_chip], second_other[other_chip]),
            cotangent_team,
            mixer_w,
            down_w,
        )
        return hidden_part, grads_part, keep, order.step(give)

    parts = [run_mixer(0)]
    passed = [grid.turn(parts[0][3], 1)]
    second_chips = order.step(second_chips)
    second_chips = second_chips + [grid.turn(second_chips[0], 6)]
    second_other += order.step([grid.turn(second_chips[1], 1), grid.turn(second_chips[2], 1)])
    parts.append(run_mixer(1))
    passed.append(grid.turn(parts[1][3], 1))
    second_chips[3], passed[0] = order.step(second_chips[3], passed[0])
    second_other.append(grid.turn(second_chips[3], 1))
    parts.append(run_mixer(2))
    passed[1], second_other[3] = order.step(passed[1], second_other[3])
    block = order.step(add_block(parts[1][2], passed[1]))
    terms = [parts[0][2], passed[0], grid.turn(block, 2)]
    passed.append(grid.turn(parts[2][3], 1))
    parts.append(run_mixer(3))
    passed[2] = order.step(passed[2])
    passed.append(grid.turn(parts[3][3], 1))
    block = order.step(add_block(parts[2][2], passed[2]))
    terms.append(grid.turn(block, 4))
    passed[3] = order.step(passed[3])
    hidden, grads = [part[0] for part in parts], [part[1] for part in parts]
    block, grads, hidden = order.step(add_block(parts[3][2], passed[3]), grads, hidden)
    terms.append(grid.turn(block, 6))
    second_team = second_chips + second_other
    early = max(1, teams // 2)
    mixer_part = token_product(grid, second_team, grads)
    mixer_part, hidden = order.step(mixer_part, hidden)
    mixer_parts = send_teams(mixer_part, 1, early + 1)
    down_part = down_product(grid, hidden, cotangent_team)
    terms, down_part = order.step(terms, down_part)
    grad_middle, grad_attn, second_part = finish_second(terms, middle, cotangent, gain_second)
    grad_attn, hidden = order.step(grad_attn, hidden)
    attn_chips = grid.chips(grad_attn)
    out_keep, out_give = mixer_output(hidden, down_w)
    attn_chips, out_give, mixer_parts = order.step(attn_chips, out_give, mixer_parts)
    late_parts = send_teams(mixer_part, early + 1, teams)
    attn_team = order.step(grid.gather_team(attn_chips))

    grad_attended, out_part = project_out_back(grid, attn_team, out_rows, attended)
    grad_attended, down_part, out_give = order.step(grad_attended, down_part, out_give)
    down_late = send_teams(down_part, early + 1, teams)
    out_other = grid.turn(out_give, 1)
    query_rot, own_grads, back_grads = attend_back(
        low, starts, queries, grad_attended, attended, normalizer, pieces, 0, OWN_KV
    )
    query_rot, own_grads, back_grads, late_parts, down_late, out_other = order.step(
        query_rot, own_grads, back_grads, late_parts, down_late, out_other
    )
    returned = [
        grid.shift(back_grads[step - 1], -step, False) for step in range(1, steps_back + 1)
    ]
    out_total, out_blocks = combine(out_keep, out_other, 0)
    out_blocks = order.step(out_blocks)
    out_terms = grid.send_chips(out_blocks)
    mixer_total = sum_teams(mixer_part, mixer_parts + late_parts, bf16)
    def members_rows(total):
        blocks = total.reshape(TEAM // 2, 2, rows, -1)
        return dynamic(blocks, core, 1), grid.turn(dynamic(blocks, 1 - core, 1), 1)

    def owner_columns(mine, others):
        both = jnp.stack([mine, others])
        first = jnp.where(core == 0, both[0], both[1])
        second = jnp.where(core == 0, both[1], both[0])
        both = jnp.stack([first, second], axis=1)
        found = [
            dynamic(both, chip) if other == 0 else grid.turn(dynamic(both, chip ^ other), 2 * other)
            for other in range(4)
        ]
        return found

    def in_order(found):
        stacked = jnp.stack(found)
        return jnp.stack([dynamic(stacked, chip ^ other) for other in range(4)]).reshape(
            (TEAM,) + found[0].shape[1:]
        )

    returned, mixer_total = order.step(returned, mixer_total)
    down_parts = send_teams(down_part, 1, early + 1)
    mixer_mine, mixer_others = members_rows(mixer_total)
    keep, give, attn_part = project_back(
        grid, normed_first, query_rot, own_grads, returned, cosine, sine_table, attn_w
    )
    attn_part, give, out_terms, down_parts, mixer_others = order.step(
        attn_part, give, out_terms, down_parts, mixer_others
    )
    other = grid.turn(give, 1)
    mixer_found = owner_columns(mixer_mine, mixer_others)
    other = order.step(other)
    total, blocks = combine(keep, other, 1)
    blocks, mixer_found, out_part = order.step(blocks, mixer_found, out_part)
    terms = grid.send_chips(blocks)
    attn_parts = send_teams(attn_part, 1, early + 1)
    outputs = finish_output([out_total] + out_terms, middle)
    down_grad = sum_teams(down_part, down_parts + down_late, f32)
    mixer_columns = in_order(mixer_found)
    attn_parts, outputs, down_grad = order.step(attn_parts, outputs, down_grad)
    attn_late = send_teams(attn_part, early + 1, teams)
    terms, attn_late = order.step(terms, attn_late)
    out_parts = send_teams(out_part, 1, teams)
    input_grad, first_part = finish_first([total] + terms, inputs_t, grad_middle, gain_first)
    gain_parts = jnp.concatenate([first_part, second_part], axis=1).T
    attn_total = sum_teams(attn_part, attn_parts + attn_late, bf16)
    attn_mine, attn_others = members_rows(attn_total)
    gain_parts, attn_total = order.step(gain_parts, attn_total)
    gain_other = grid.turn(gain_parts, 1)
    gain_other, attn_others, out_parts = order.step(gain_other, attn_others, out_parts)
    gain_parts = gain_parts + gain_other
    gain_parts = order.step(gain_parts)
    gain_chips = [grid.turn(gain_parts, 2 * other) for other in range(1, 4)]
    out_own = sum_teams(out_part, out_parts, bf16)
    gain_chips, out_own = order.step(gain_chips, out_own)
    for other in gain_chips:
        gain_parts = gain_parts + other
    attn_found = owner_columns(attn_mine, attn_others)
    out_grad = grid.to_owners(out_own)

    def whole_units(blocks):
        blocks = blocks.reshape(TEAM, rows, teams, unit_rows)
        return jnp.transpose(blocks, (1, 2, 0, 3)).reshape(rows, TEAM * units).astype(f32)

    def whole(blocks):
        return jnp.transpose(blocks, (1, 0, 2)).reshape(rows, -1).astype(f32)

    gate_grad = whole_units(mixer_columns[..., :units])
    up_grad = whole_units(mixer_columns[..., units:])
    attn_found, out_grad, gain_parts = order.step(attn_found, out_grad, gain_parts)
    gain_blocks = gain_parts.reshape(2, teams, TEAM, rows)
    gain_sums = dynamic(dynamic(gain_blocks, grid.team, 1), member, 1)
    for steps in range(1, teams):
        block = dynamic(dynamic(gain_blocks, (grid.team + steps) % teams, 1), member, 1)
        gain_sums = gain_sums + grid.shift(block, steps)
    out_grad = out_grad.astype(f32)
    attn_columns = in_order(attn_found)
    gain_sums = gain_sums + order.token[0, 0].astype(f32)
    return (
        outputs,
        input_grad,
        gain_sums[0],
        whole(attn_columns[..., :Q_WIDTH]),
        whole(attn_columns[..., Q_WIDTH : Q_WIDTH + KV_WIDTH]),
        whole(attn_columns[..., Q_WIDTH + KV_WIDTH :]),
        out_grad,
        gain_sums[1],
        gate_grad,
        up_grad,
        down_grad,
    )


def solution(mesh):
    matrix, vector = P("dev", None), P("dev")
    in_specs = (matrix, vector, vector) + (matrix,) * 4 + (vector,) + (matrix,) * 4
    out_specs = (matrix, matrix, vector) + (matrix,) * 4 + (vector,) + (matrix,) * 3
    return jax.shard_map(
        per_device, mesh=mesh, in_specs=in_specs, out_specs=out_specs, check_vma=False
    )
```
